32 devices in a mesh: dp: 8 (over y, x, core), tensor: 4 (over z).
Axes of the slice: x: 2, y: 2, z: 4, core: 2. Of those that a mesh axis runs over, the one named last changes fastest.
Arguments:
- tokens: bfloat16 [16384, 1024], P(('dp', 'tensor')), may hold values from -6 to 6
- w_qkv: bfloat16 [1024, 3, 1024], P('dp', None, 'tensor'), may hold values from -0.25 to 0.25
- w_out: bfloat16 [1024, 1024], P('tensor', 'dp'), may hold values from -0.5 to 0.5
- w_in: bfloat16 [1024, 2, 2624], P('dp', None, 'tensor'), may hold values from -0.1875 to 0.1875
- w_down: bfloat16 [2624, 1024], P('tensor', 'dp'), may hold values from -0.125 to 0.125
- gain_attn: bfloat16 [1024], P('dp'), may hold values from 0.5 to 1.5
- gain_mlp: bfloat16 [1024], P('dp'), may hold values from 0.5 to 1.5
- grad_output: bfloat16 [16384, 1024], P(('dp', 'tensor')), may hold values from -6 to 6
Outputs:
- output: bfloat16 [16384, 1024], P(('dp', 'tensor'))
- grad_tokens: bfloat16 [16384, 1024], P(('dp', 'tensor'))
- grad_qkv: float32 [1024, 3, 1024], P('dp', None, 'tensor')
- grad_out: float32 [1024, 1024], P('tensor', 'dp')
- grad_in: float32 [1024, 2, 2624], P('dp', None, 'tensor')
- grad_down: float32 [2624, 1024], P('tensor', 'dp')
- grad_gain_attn: float32 [1024], P('dp')
- grad_gain_mlp: float32 [1024], P('dp')
The draws below stay inside these ranges and needn't reach their ends.
All inputs are finite; a program needn't handle non-finite values.
Results may differ from the reference program's by a relative error of at most 0.017.
The reference program's roundings to bfloat16 on the way count: a program that leaves them out, or rounds other values in their place, can miss the bound.
Values may be sent and summed in bfloat16 or wider, within the bound.
A program may use at most 192 MiB of HBM per device.

```python
import jax
import jax.numpy as jnp
from jax import lax

D = 1024
H = 16
HD = 64
FF = 2624
LEN = 1024
SEQS = 2
TOKENS = 16384


def steps_of(rng, shape, cuts, smallest, largest):
    level, own = 1.0, jax.random.fold_in(rng, 6)
    for position, blocks in cuts:
        steps = jnp.exp(jax.random.uniform(jax.random.fold_in(own, position), (blocks,), jnp.float32, smallest / len(cuts), largest / len(cuts)))
        level = level * jnp.repeat(steps, shape[position] // blocks).reshape([-1 if axis == position else 1 for axis in range(len(shape))])
    return level


def scatter_about(key, extent, scale, most, pieces=(), kind=jnp.bfloat16):
    values = jax.random.normal(key, extent, jnp.float32) * scale
    if len(pieces) > 0:
        values = steps_of(key, extent, pieces, -0.22, 0.18) * values
    return jnp.clip(values, min=-most, max=most).astype(kind)


def setup_inputs(seed: int = 0) -> dict:
    keys = jax.random.split(jax.random.key(seed), 9)
    return {
        "tokens": scatter_about(keys[0], (TOKENS, D), 1.0, 6.0, ((0, 32),)),
        "w_qkv": scatter_about(keys[1], (D, 3, D), (D // 2) ** -0.5, 0.25, ((0, 8), (2, 4))),
        "w_out": scatter_about(keys[2], (D, D), (D // 8) ** -0.5, 0.5, ((0, 4), (1, 8))),
        "w_in": scatter_about(keys[3], (D, 2, FF), D ** -0.5, 0.1875, ((0, 8), (2, 4))),
        "w_down": scatter_about(keys[4], (FF, D), FF ** -0.5, 0.125, ((0, 4), (1, 8))),
        "gain_attn": jnp.clip(1.0 + 0.1 * jax.random.normal(keys[5], (D,), jnp.float32), 0.5, 1.5).astype(jnp.bfloat16),
        "gain_mlp": jnp.clip(1.0 + 0.1 * jax.random.normal(keys[6], (D,), jnp.float32), 0.5, 1.5).astype(jnp.bfloat16),
        "grad_output": scatter_about(keys[7], (TOKENS, D), 1.0, 6.0, ((0, 32),)),
    }


EPS = 1e-05
THETA = 160000.0
HIGH = lax.Precision.HIGHEST

@jax.custom_vjp
def low(v):
    return lax.optimization_barrier(v.astype(jnp.bfloat16)).astype(jnp.float32)

@jax.custom_vjp
def low_back(v):
    return v

def low_keep(v):
    return (low(v), None)

def low_pass(kept, grad):
    return (grad,)

def back_keep(v):
    return (v, None)

def back_low(kept, grad):
    return (low(grad),)
low.defvjp(low_keep, low_pass)
low_back.defvjp(back_keep, back_low)

def layer_norm(values, gain):
    centred = values - lax.optimization_barrier(jnp.mean(values, axis=-1, keepdims=True))
    spread = lax.optimization_barrier(jnp.mean(centred * centred, axis=-1, keepdims=True))
    return centred * lax.rsqrt(spread + EPS) * gain

def rotary(values, length):
    rows = values.shape[0]
    half = values.shape[-1] // 2
    freq = THETA ** (-(jnp.arange(half).astype(jnp.float32) * 2.0 / values.shape[-1]))
    place = (jnp.arange(rows) % length).astype(jnp.float32)
    angle = place[:, None] * freq[None, :]
    cosine = jnp.cos(angle)[:, None, :]
    sine = jnp.sin(angle)[:, None, :]
    first = values[..., :half]
    second = values[..., half:]
    return jnp.concatenate([first * cosine - second * sine, second * cosine + first * sine], axis=-1)

def geglu(pair):
    return jax.nn.gelu(pair[:, 0], approximate=False) * pair[:, 1]

def layer(group, qkv_weight, out_weight, in_weight, down_weight, gain_one, gain_two):
    rows = group.shape[0]
    seqs = rows // LEN
    normed = low(layer_norm(group, gain_one))
    proj = low_back(jnp.einsum('td,dcf->tcf', normed, qkv_weight, precision=HIGH))
    split = proj.reshape(rows, 3, H, HD)
    query = low(rotary(split[:, 0], LEN)).reshape(seqs, LEN, H, HD)
    key = low(rotary(split[:, 1], LEN)).reshape(seqs, LEN, H, HD)
    value = low(split[:, 2]).reshape(seqs, LEN, H, HD)
    scores = low_back(jnp.einsum('slhe,smhe->shlm', query, key, precision=HIGH) * HD ** (-0.5))
    probs = jax.nn.softmax(scores, axis=-1)
    attended = jnp.einsum('shlm,smhe->slhe', low(probs), value, precision=HIGH).reshape(rows, D)
    attended = low(low_back(attended))
    branch = low_back(jnp.dot(attended, out_weight, precision=HIGH))
    residual = group + branch
    normed_two = low(layer_norm(residual, gain_two))
    pair = low_back(jnp.einsum('td,dcf->tcf', normed_two, in_weight, precision=HIGH))
    hidden = low(geglu(pair))
    branch_two = low_back(jnp.dot(hidden, down_weight, precision=HIGH))
    return residual + branch_two

def reference(tokens, w_qkv, w_out, w_in, w_down, gain_attn, gain_mlp, grad_output):
    groups = tokens.shape[0] // (SEQS * LEN)

    def forward(inputs, qkv_weight, out_weight, in_weight, down_weight, gain_one, gain_two):

        def single(group):
            return layer(group, qkv_weight, out_weight, in_weight, down_weight, gain_one, gain_two)
        results = lax.map(jax.checkpoint(single), inputs.reshape(groups, SEQS * LEN, D))
        return results.reshape(groups * SEQS * LEN, D)
    floats = [a.astype(jnp.float32) for a in (tokens, w_qkv, w_out, w_in, w_down, gain_attn, gain_mlp)]
    result, pull = jax.vjp(forward, *floats)
    grads = pull(grad_output.astype(jnp.float32))
    return (result.astype(jnp.bfloat16), grads[0].astype(jnp.bfloat16), grads[1], grads[2], grads[3], grads[4], grads[5], grads[6])
```

```python
import functools

import jax
import jax.numpy as jnp
from jax import lax
from jax.experimental import pallas as pl
from jax.experimental.pallas import tpu as pltpu
from jax.sharding import PartitionSpec as P

HD = 64
LEN = 1024
EPS = 1e-05
THETA = 160000.0
MESH = pl.DeviceIdType.MESH
BF = jnp.bfloat16
F32 = jnp.float32
LOW = 8


def up(n, m):
    return -(-n // m) * m


def dg(a, b, ca, cb):
    return lax.dot_general(a, b, (((ca,), (cb,)), ((), ())), preferred_element_type=F32)


class Plan:
    def __init__(self, nz, width, tokens, units, hidden):
        self.nz, self.width, self.tokens = nz, width, tokens
        self.lane = width // LOW
        self.block = 2 * self.lane
        self.units = units // 2
        self.hid_real = hidden // 2
        self.hid = up(self.hid_real, 16)
        self.heads = self.units // HD
        self.pieces = {}
        total = 0
        for name, rows in (
            ("n", 16),
            ("o", self.units),
            ("q", 3 * self.units),
            ("a", self.hid),
            ("b", self.hid),
            ("d", self.hid),
        ):
            self.pieces[name] = (total, rows)
            total += rows
        self.rows = total
        self.order = list(self.pieces)


def kernel(
    plan,
    x_hbm,
    dy_hbm,
    packed,
    cos_ref,
    sin_ref,
    out_hbm,
    gtok_hbm,
    gw_ref,
    W,
    xown,
    dyf,
    n1,
    qkv,
    att,
    lse,
    res,
    n2,
    AB,
    hid,
    gat,
    exs,
    exr,
    Gn,
    Gb,
    Gd,
    R1,
    R2,
    R3,
    zr,
    zs,
    xyr,
    xys,
    r1r,
    r1s,
    r2r,
    r2s,
    r3r,
    r3s,
    swr,
    sws,
    cr,
    cs,
):
    p = plan
    nz, D, T, U, H = p.nz, p.width, p.tokens, p.units, p.hid
    S = 2 * T
    L, B = p.lane, p.block
    d = lax.axis_index("dp")
    z = lax.axis_index("tensor")
    c = lax.rem(d, 2)
    r = lax.rem(d // 2, 4)
    xb = lax.rem(r, 2)
    yb = r // 2
    zb = lax.rem(z, 2)
    sib = d + 1 - 2 * c
    xp = d + 2 - 4 * xb
    yp = d + 4 - 8 * yb
    zpair = z + 1 - 2 * zb
    rx = r + 1 - 2 * xb
    ry = r + 2 - 4 * yb
    rd = 3 - r
    stay = lax.rem(c + z, 2) == 0

    def rows_at(start, n):
        return pl.ds(pl.multiple_of(start, 16), n)

    def lanes(block):
        return pl.ds(pl.multiple_of(block * B, L), B)

    mine = rows_at(c * T, T)
    theirs_start = (1 - c) * T

    def remote(src, dst, ssem, rsem, dev):
        pltpu.make_async_remote_copy(src, dst, ssem, rsem, device_id=dev, device_id_type=MESH).start()

    def take(ref, sem):
        pltpu.make_async_copy(ref, ref, sem).wait()

    partners = [(sib, z), (xp, z), (yp, z)]
    for dz in range(1, nz):
        there = lax.rem(z + dz, nz)
        partners += [(d, there), (sib, there)]
    bar = pltpu.get_barrier_semaphore()
    for dev in partners:
        pl.semaphore_signal(bar, inc=1, device_id=dev, device_id_type=MESH)
    pl.semaphore_wait(bar, len(partners))

    index = {name: i for i, name in enumerate(p.order)}

    def base(name):
        return nz * p.pieces[name][0]

    def count(name):
        return p.pieces[name][1]

    def z_start(name):
        off, n = p.pieces[name]
        i = index[name]
        dst = W.at[rows_at(base(name) + z * n, n), pl.ds(pl.multiple_of(r * B + c * L, L), L)]
        for dz in range(nz):
            there = lax.rem(z + dz, nz)
            for kk in range(2):
                k = lax.rem(c + kk, 2)
                src = packed.at[k, pl.ds(off, n), :]
                if dz == 0 and kk == 0:
                    pltpu.make_async_copy(src, dst, zr.at[i]).start()
                else:
                    remote(src, dst, zs.at[i], zr.at[i], (d if kk == 0 else sib, there))

    def half(name, which):
        n = (nz // 2) * count(name)
        return pl.ds(base(name) + which * n, n)

    def xy1(name):
        i = index[name]
        take(W.at[pl.ds(base(name), nz * count(name)), lanes(r)], zr.at[i])
        a = W.at[half(name, 0), lanes(r)]
        b = W.at[half(name, 1), lanes(r)]
        remote(a, a, xys.at[i], xyr.at[i, 0], (xp, z))
        remote(b, b, xys.at[i], xyr.at[i, 1], (yp, z))
        remote(a, a, xys.at[i], xyr.at[i, 2], (yp, z))
        remote(b, b, xys.at[i], xyr.at[i, 3], (xp, z))

    def xy2(name):
        i = index[name]
        a = W.at[half(name, 0), lanes(rx)]
        b = W.at[half(name, 1), lanes(ry)]
        take(a, xyr.at[i, 0])
        remote(a, a, xys.at[i], xyr.at[i, 4], (yp, z))
        take(b, xyr.at[i, 1])
        remote(b, b, xys.at[i], xyr.at[i, 5], (xp, z))

    def ready(name):
        i = index[name]
        take(W.at[half(name, 0), lanes(ry)], xyr.at[i, 2])
        take(W.at[half(name, 1), lanes(rx)], xyr.at[i, 3])
        take(W.at[half(name, 0), lanes(rd)], xyr.at[i, 4])
        take(W.at[half(name, 1), lanes(rd)], xyr.at[i, 5])

    def sent(name):
        i = index[name]
        n = count(name)
        take(R3.at[pl.ds(0, 2 * nz - 1), pl.ds(0, n), :], zs.at[i])
        take(W.at[pl.ds(0, 6 * (nz // 2) * n * B // D), :], xys.at[i])

    place = {
        "n": (Gn, 0),
        "q": (W, base("a")),
        "o": (W, base("a") + nz * 3 * U),
        "a": (W, base("d")),
        "b": (Gb, 0),
        "d": (Gd, 0),
    }

    def ghalf(name, which):
        n = (nz // 2) * count(name)
        return pl.ds(place[name][1] + which * n, n)

    def rhalf(name):
        return pl.ds((nz // 2) * p.pieces[name][0], (nz // 2) * count(name))

    def step_of(n):
        for s in (128, 112, 96, 80, 64, 48, 32, 16):
            if n % s == 0:
                return s
        return n

    def rs1(name):
        i = index[name]
        G = place[name][0]
        to = rhalf(name)
        for which, near, dev in ((0, ry, yp), (1, rx, xp)):
            rows = ghalf(name, which)
            remote(G.at[rows, lanes(rd)], R1.at[which, 0, to, :], r1s.at[i], r1r.at[i, which, 0], (dev, z))
        for which, near, dev in ((0, ry, yp), (1, rx, xp)):
            rows = ghalf(name, which)
            remote(G.at[rows, lanes(near)], R1.at[which, 1, to, :], r1s.at[i], r1r.at[i, which, 1], (dev, z))

    def rs2(name):
        i = index[name]
        G, gb = place[name]
        n = (nz // 2) * count(name)
        to = rhalf(name)
        s = step_of(n)
        for which, block, dev in ((0, rx, xp), (1, ry, yp)):
            take(R1.at[which, 0, to, :], r1r.at[i, which, 0])

            def add(t, _):
                g = rows_at(gb + which * n + t * s, s)
                q = rows_at(to.start + t * s, s)
                G[g, lanes(block)] = (G[g, lanes(block)].astype(F32) + R1[which, 0, q, :].astype(F32)).astype(BF)
                return 0

            lax.fori_loop(0, n // s, add, 0)
            remote(
                G.at[ghalf(name, which), lanes(block)],
                R2.at[which, to, :],
                r2s.at[i],
                r2r.at[i, which],
                (dev, z),
            )

    def rs3(name):
        i = index[name]
        G, gb = place[name]
        off, m = p.pieces[name]
        n = (nz // 2) * m
        to = rhalf(name)
        s = step_of(n)
        for which in range(2):
            take(R1.at[which, 1, to, :], r1r.at[i, which, 1])
            take(R2.at[which, to, :], r2r.at[i, which])

            def add(t, _):
                g = rows_at(gb + which * n + t * s, s)
                q = rows_at(to.start + t * s, s)
                total = G[g, lanes(r)].astype(F32) + R1[which, 1, q, :].astype(F32) + R2[which, q, :].astype(F32)
                G[g, lanes(r)] = total.astype(BF)
                return 0

            lax.fori_loop(0, n // s, add, 0)
        dst = R3.at[z * 2 + c, pl.ds(off, m), :]
        for dz in range(nz):
            there = lax.rem(z + dz, nz)
            for kk in range(2):
                k = lax.rem(c + kk, 2)
                src = G.at[rows_at(gb + there * m, m), pl.ds(pl.multiple_of(r * B + k * L, L), L)]
                if dz == 0 and kk == 0:
                    pltpu.make_async_copy(src, dst, r3r.at[i]).start()
                else:
                    remote(src, dst, r3s.at[i], r3r.at[i], (d if kk == 0 else sib, there))

    def rs4(name):
        i = index[name]
        off, m = p.pieces[name]
        take(R3.at[:, pl.ds(off, m), :], r3r.at[i])
        for k in range(2):
            total = R3[k, off : off + m, :].astype(F32)
            for j in range(1, nz):
                total += R3[2 * j + k, off : off + m, :].astype(F32)
            gw_ref[k, off : off + m, :] = total

    def rs_sent(name):
        i = index[name]
        m = count(name)
        n = (nz // 2) * m
        take(W.at[pl.ds(0, 4 * n * B // D), :], r1s.at[i])
        take(W.at[pl.ds(0, 2 * n * B // D), :], r2s.at[i])
        take(R3.at[pl.ds(0, 2 * nz - 1), pl.ds(0, m), :], r3s.at[i])

    def swap(src, dst_here, dst_there, i):
        @pl.when(stay)
        def _():
            pltpu.make_async_copy(src, dst_here, swr.at[i]).start()

        @pl.when(jnp.logical_not(stay))
        def _():
            remote(src, dst_there, sws.at[i], swr.at[i], (sib, zpair))

    def swap_sent(src, i):
        @pl.when(jnp.logical_not(stay))
        def _():
            take(src, sws.at[i])

    def give(src, dst, i):
        remote(src, dst, cs.at[i], cr.at[i], (sib, z))

    def give_rows(buf, i):
        give(buf.at[mine, :], buf.at[mine, :], i)

    def got_rows(buf, i):
        take(buf.at[mine, :], cr.at[i])

    NB = 64

    z_start("n")
    z_start("o")
    swap(x_hbm, xown, xown, 0)
    z_start("q")
    xy1("n")
    xy1("o")
    z_start("a")
    xy2("n")
    ready("n")
    swap(dy_hbm, dyf.at[mine, :], dyf.at[rows_at(theirs_start, T), :], 1)
    take(xown, swr.at[0])

    gain_one = W[0:16, :][0:1, :].astype(F32)
    gain_two = W[0:16, :][1:2, :].astype(F32)

    def norm_parts(v):
        mean = jnp.mean(v, axis=1, keepdims=True)
        cen = v - mean
        inv = lax.rsqrt(jnp.mean(cen * cen, axis=1, keepdims=True) + EPS)
        return cen, inv

    def norm_first(t, _):
        own = rows_at(t * NB, NB)
        cen, inv = norm_parts(xown[own, :].astype(F32))
        n1[rows_at(c * T + t * NB, NB), :] = (cen * inv * gain_one).astype(BF)
        return 0

    lax.fori_loop(0, T // NB, norm_first, 0)
    give_rows(n1, 0)
    xy2("o")
    xy1("q")
    z_start("b")
    got_rows(n1, 0)
    xy1("a")
    xy2("q")
    take(dyf.at[mine, :], swr.at[1])
    give_rows(dyf, 1)
    z_start("d")
    ready("q")

    TB = 256

    def project(t, _):
        zi, ti = t // (S // TB), lax.rem(t, S // TB)
        cols = pl.ds(pl.multiple_of(ti * TB, TB), TB)
        acc = dg(W[rows_at(base("q") + zi * 3 * U, 3 * U), :], n1[cols, :], 1, 1)
        co, si = cos_ref[:, cols], sin_ref[:, cols]
        parts = []
        for part in range(2):
            for h in range(p.heads):
                at = part * U + h * HD
                v1, v2 = acc[at : at + HD // 2], acc[at + HD // 2 : at + HD]
                w1, w2 = v1 * co - v2 * si, v2 * co + v1 * si
                if part == 0:
                    w1, w2 = w1 * HD**-0.5, w2 * HD**-0.5
                parts += [w1, w2]
        parts.append(acc[2 * U :])
        qkv[zi, :, cols] = jnp.concatenate(parts, axis=0).astype(BF)
        return 0

    lax.fori_loop(0, nz * (S // TB), project, 0)
    xy2("a")
    xy1("b")

    QB = 256

    def attend(t, _):
        zi, h = t // p.heads, lax.rem(t, p.heads)
        key = qkv[zi, rows_at(U + h * HD, HD), :].T
        val = qkv[zi, rows_at(2 * U + h * HD, HD), :]

        def block(b, _):
            cols = pl.ds(pl.multiple_of(b * QB, QB), QB)
            s = dg(key, qkv[zi, rows_at(h * HD, HD), cols], 1, 0)
            m = jnp.max(s, axis=0, keepdims=True)
            e = jnp.exp(s - m)
            l = jnp.sum(e, axis=0, keepdims=True)
            o = dg(val, e.astype(BF), 1, 0)
            att[rows_at(zi * U + h * HD, HD), cols] = (o / l).astype(BF)
            lse[t, :, cols] = m + jnp.log(l)
            return 0

        lax.fori_loop(0, S // QB, block, 0)
        return 0

    def attend_some(lo, hi):
        lax.fori_loop(lo, hi, attend, 0)

    NH = nz * p.heads
    attend_some(0, NH // 2)
    xy2("b")
    xy1("d")
    attend_some(NH // 2, NH)
    ready("o")

    MB = 256

    def partial(lhs_rows, rhs, start):
        cols = pl.ds(pl.multiple_of(start, MB), MB)
        total = None
        for lhs, w in zip(lhs_rows, rhs):
            term = dg(lhs(cols), w[...], 0, 0)
            total = term if total is None else total + term
        return total

    def send_partial(lhs_rows, rhs, slot, there, i):
        def some(t, _):
            exs[slot, rows_at(t * MB, MB), :] = partial(lhs_rows, rhs, theirs_start + t * MB).astype(BF)
            return 0

        lax.fori_loop(0, T // MB, some, 0)
        give(exs.at[slot], exr.at[there], i)

    w_o = W.at[pl.ds(base("o"), nz * U), :]
    w_q = W.at[pl.ds(base("q"), nz * 3 * U), :]
    w_a = W.at[pl.ds(base("a"), nz * H), :]
    w_b = W.at[pl.ds(base("b"), nz * H), :]

    lhs_att = [lambda cols: att[:, cols]]
    send_partial(lhs_att, [w_o], 0, 0, 2)

    def residual(t, _):
        own = rows_at(t * MB, MB)
        res[own, :] = xown[own, :].astype(F32) + partial(lhs_att, [w_o], c * T + t * MB)
        return 0

    lax.fori_loop(0, T // MB, residual, 0)
    take(exr.at[0], cr.at[2])

    def norm_second(t, _):
        own = rows_at(t * NB, NB)
        v = res[own, :] + exr[0, own, :].astype(F32)
        res[own, :] = v
        cen, inv = norm_parts(v)
        n2[rows_at(c * T + t * NB, NB), :] = (cen * inv * gain_two).astype(BF)
        return 0

    lax.fori_loop(0, T // NB, norm_second, 0)
    give_rows(n2, 3)
    ready("a")
    ready("b")
    got_rows(n2, 3)

    def hidden(t, _):
        zi, ti = t // (S // TB), lax.rem(t, S // TB)
        cols = pl.ds(pl.multiple_of(ti * TB, TB), TB)
        rows = rows_at(zi * H, H)
        normed = n2[cols, :]
        act = dg(W[rows_at(base("a") + zi * H, H), :], normed, 1, 1)
        gate = dg(W[rows_at(base("b") + zi * H, H), :], normed, 1, 1)
        cdf = 0.5 + 0.5 * lax.erf(act * 0.7071067811865476)
        gelu = act * cdf
        slope = cdf + act * (jnp.exp(-0.5 * act * act) * 0.3989422804014327)
        hid[rows, cols] = (gelu * gate).astype(BF)
        AB[0, rows, cols] = (slope * gate).astype(BF)
        AB[1, rows, cols] = gelu.astype(BF)
        return 0

    n_tile = nz * (S // TB)
    lax.fori_loop(0, n_tile // 2, hidden, 0)
    xy2("d")
    lax.fori_loop(n_tile // 2, n_tile, hidden, 0)
    got_rows(dyf, 1)

    def grad_of(dest, at, lhs, rhs, n, lo, hi):
        def some(t, _):
            dest[rows_at(at + t * n, n), :] = dg(lhs(rows_at(t * n, n)), rhs[...], 1, 0).astype(BF)
            return 0

        lax.fori_loop(lo, hi, some, 0)

    grad_of(Gd, 0, lambda rows: hid[rows, :], dyf, H, 0, nz)
    rs1("d")
    ready("d")

    def back_hidden(t, _):
        zi, ti = t // (S // TB), lax.rem(t, S // TB)
        cols = pl.ds(pl.multiple_of(ti * TB, TB), TB)
        rows = rows_at(zi * H, H)
        g = dg(W[rows_at(base("d") + zi * H, H), :], dyf[cols, :], 1, 1)
        AB[0, rows, cols] = (g * AB[0, rows, cols].astype(F32)).astype(BF)
        AB[1, rows, cols] = (g * AB[1, rows, cols].astype(F32)).astype(BF)
        return 0

    lax.fori_loop(0, n_tile, back_hidden, 0)

    w_d = W.at[pl.ds(base("d"), nz * H), :]
    lhs_hid = [lambda cols: hid[:, cols]]
    lhs_gp = [lambda cols: AB[0, :, cols], lambda cols: AB[1, :, cols]]
    take(exs.at[0], cs.at[2])
    send_partial(lhs_hid, [w_d], 0, 0, 4)
    take(exr.at[0], cr.at[4])

    def output(t, _):
        own = rows_at(t * MB, MB)
        total = partial(lhs_hid, [w_d], c * T + t * MB)
        xs = res[own, :] + (total + exr[0, own, :].astype(F32))
        exs[1, own, :] = xs.astype(BF)
        return 0

    lax.fori_loop(0, T // MB, output, 0)
    swap(exs.at[1], out_hbm, out_hbm, 2)

    sent("d")
    grad_of(W, base("d"), lambda rows: AB[0, rows, :], n2, H, 0, nz)
    rs1("a")
    grad_of(Gb, 0, lambda rows: AB[1, rows, :], n2, H, 0, nz)
    rs1("b")
    rs2("d")
    take(exs.at[0], cs.at[4])
    send_partial(lhs_gp, [w_a, w_b], 0, 1, 5)

    rs2("a")
    take(exr.at[1], cr.at[5])

    def grad_residual(t, carry):
        own = rows_at(t * MB, MB)
        total = partial(lhs_gp, [w_a, w_b], c * T + t * MB) + exr[1, own, :].astype(F32)
        v = res[own, :]
        cen, inv = norm_parts(v)
        hat = cen * inv
        carry = carry + jnp.sum(total * hat, axis=0, keepdims=True)
        dh = total * gain_two
        back = inv * (
            dh - jnp.mean(dh, axis=1, keepdims=True) - hat * jnp.mean(dh * hat, axis=1, keepdims=True)
        )
        g = dyf[rows_at(c * T + t * MB, MB), :].astype(F32) + back
        res[own, :] = g
        dyf[rows_at(c * T + t * MB, MB), :] = g.astype(BF)
        return carry

    take(dyf.at[mine, :], cs.at[1])
    gain_two_grad = lax.fori_loop(0, T // MB, grad_residual, jnp.zeros((1, D), F32))
    give_rows(dyf, 6)
    rs3("d")
    rs2("b")
    got_rows(dyf, 6)

    sent("o")
    sent("a")
    sent("b")

    def grad_att(t, _):
        rows = rows_at(t * U, U)
        gat[rows, :] = dg(W[rows_at(base("o") + t * U, U), :], dyf[...], 1, 1).astype(BF)
        return 0

    lax.fori_loop(0, nz, grad_att, 0)
    grad_of(W, place["o"][1], lambda rows: att[rows, :], dyf, U, 0, nz)
    rs1("o")
    rs3("a")

    def attend_back(t, _):
        zi, h = t // p.heads, lax.rem(t, p.heads)
        qr, kr, vr = (rows_at(j * U + h * HD, HD) for j in range(3))
        keyT = qkv[zi, kr, :]
        key = keyT.T
        val = qkv[zi, vr, :].T
        ar = rows_at(zi * U + h * HD, HD)

        def block(b, carry):
            dk, dv = carry
            cols = pl.ds(pl.multiple_of(b * QB, QB), QB)
            q = qkv[zi, qr, cols]
            g = gat[ar, cols]
            inner = jnp.sum(g.astype(F32) * att[ar, cols].astype(F32), axis=0, keepdims=True)
            prob = jnp.exp(dg(key, q, 1, 0) - lse[t, :, cols])
            dprob = dg(val, g, 1, 0)
            ds = (prob * (dprob - inner)).astype(BF)
            dv = dv + dg(g, prob.astype(BF), 1, 1)
            dk = dk + dg(q, ds, 1, 1)
            dq = dg(keyT, ds, 1, 0) * HD**-0.5
            co, si = cos_ref[:, cols], sin_ref[:, cols]
            g1, g2 = dq[: HD // 2], dq[HD // 2 :]
            qkv[zi, qr, cols] = jnp.concatenate([g1 * co + g2 * si, g2 * co - g1 * si], axis=0).astype(BF)
            return dk, dv

        zero = jnp.zeros((HD, S), F32)
        dk, dv = lax.fori_loop(0, S // QB, block, (zero, zero))
        g1, g2 = dk[: HD // 2], dk[HD // 2 :]
        co, si = cos_ref[...], sin_ref[...]
        qkv[zi, kr, :] = jnp.concatenate([g1 * co + g2 * si, g2 * co - g1 * si], axis=0).astype(BF)
        qkv[zi, vr, :] = dv.astype(BF)
        return 0

    quarter = NH // 4
    lax.fori_loop(0, quarter, attend_back, 0)
    rs2("o")
    rs3("b")
    lax.fori_loop(quarter, 2 * quarter, attend_back, 0)
    rs3("o")
    rs4("d")
    lax.fori_loop(2 * quarter, 3 * quarter, attend_back, 0)
    rs4("a")
    lax.fori_loop(3 * quarter, NH, attend_back, 0)

    def grad_qkv(t, _):
        W[rows_at(place["q"][1] + t * 3 * U, 3 * U), :] = dg(qkv[t, :, :], n1[...], 1, 0).astype(BF)
        return 0

    lax.fori_loop(0, nz, grad_qkv, 0)
    rs1("q")

    lhs_proj = [lambda cols: qkv[:, :, cols].reshape(nz * 3 * U, MB)]
    swap_sent(exs.at[1], 2)
    take(out_hbm, swr.at[2])
    send_partial(lhs_proj, [w_q], 1, 0, 7)
    rs4("b")
    rs2("q")
    take(exr.at[0], cr.at[7])
    take(exs.at[0], cs.at[5])

    def grad_input(t, carry):
        own = rows_at(t * MB, MB)
        total = partial(lhs_proj, [w_q], c * T + t * MB) + exr[0, own, :].astype(F32)
        cen, inv = norm_parts(xown[own, :].astype(F32))
        hat = cen * inv
        carry = carry + jnp.sum(total * hat, axis=0, keepdims=True)
        dh = total * gain_one
        back = inv * (
            dh - jnp.mean(dh, axis=1, keepdims=True) - hat * jnp.mean(dh * hat, axis=1, keepdims=True)
        )
        exs[0, own, :] = (res[own, :] + back).astype(BF)
        return carry

    gain_one_grad = lax.fori_loop(0, T // MB, grad_input, jnp.zeros((1, D), F32))
    swap(exs.at[0], gtok_hbm, gtok_hbm, 3)
    line = lax.broadcasted_iota(jnp.int32, (16, D), 0)
    both = jnp.where(line == 0, gain_one_grad, jnp.where(line == 1, gain_two_grad, 0.0)).astype(BF)
    for j in range(nz):
        Gn[16 * j : 16 * j + 16, :] = both
    rs1("n")
    rs2("n")
    rs3("q")
    rs3("n")
    rs4("o")
    rs4("q")
    rs4("n")

    sent("n")
    sent("q")
    for name in p.order:
        rs_sent(name)
    swap_sent(x_hbm, 0)
    swap_sent(dy_hbm, 1)
    swap_sent(exs.at[0], 3)
    take(gtok_hbm, swr.at[3])
    take(n1.at[mine, :], cs.at[0])
    take(n2.at[mine, :], cs.at[3])
    take(dyf.at[mine, :], cs.at[6])
    take(exs.at[1], cs.at[7])


def layer(plan, x, dy, packed, cosine, sine):
    p = plan
    nz, D, T, U, H = p.nz, p.width, p.tokens, p.units, p.hid
    S = 2 * T
    n = len(p.order)
    hbm = pl.BlockSpec(memory_space=pl.ANY)
    vmem = pl.BlockSpec(memory_space=pltpu.VMEM)
    dma = pltpu.SemaphoreType.DMA
    scratch = [
        pltpu.VMEM((nz * p.rows, D), BF),
        pltpu.VMEM((T, D), BF),
        pltpu.VMEM((S, D), BF),
        pltpu.VMEM((S, D), BF),
        pltpu.VMEM((nz, 3 * U, S), BF),
        pltpu.VMEM((nz * U, S), BF),
        pltpu.VMEM((nz * p.heads, 1, S), F32),
        pltpu.VMEM((T, D), F32),
        pltpu.VMEM((S, D), BF),
        pltpu.VMEM((2, nz * H, S), BF),
        pltpu.VMEM((nz * H, S), BF),
        pltpu.VMEM((nz * U, S), BF),
        pltpu.VMEM((2, T, D), BF),
        pltpu.VMEM((2, T, D), BF),
        pltpu.VMEM((nz * 16, D), BF),
        pltpu.VMEM((nz * H, D), BF),
        pltpu.VMEM((nz * H, D), BF),
        pltpu.VMEM((2, 2, (nz // 2) * p.rows, p.block), BF),
        pltpu.VMEM((2, (nz // 2) * p.rows, p.block), BF),
        pltpu.VMEM((2 * nz, p.rows, p.lane), BF),
        dma((n,)),
        dma((n,)),
        dma((n, 6)),
        dma((n,)),
        dma((n, 2, 2)),
        dma((n,)),
        dma((n, 2)),
        dma((n,)),
        dma((n,)),
        dma((n,)),
        dma((4,)),
        dma((4,)),
        dma((8,)),
        dma((8,)),
    ]
    return pl.pallas_call(
        functools.partial(kernel, p),
        out_shape=(
            jax.ShapeDtypeStruct((T, D), BF),
            jax.ShapeDtypeStruct((T, D), BF),
            jax.ShapeDtypeStruct((2, p.rows, p.lane), F32),
        ),
        in_specs=[hbm, hbm, hbm, vmem, vmem],
        out_specs=(hbm, hbm, vmem),
        scratch_shapes=scratch,
        compiler_params=pltpu.CompilerParams(
            collective_id=0, has_side_effects=True, vmem_limit_bytes=64 * 1024 * 1024 - 65536
        ),
        name="layer",
    )(x, dy, packed, cosine, sine)


def local(outer, nz, tokens, w_qkv, w_out, w_in, w_down, gain_attn, gain_mlp, grad_output):
    T, D = tokens.shape
    groups = [[hi * LOW + lo for hi in range(outer)] for lo in range(LOW)]
    piece = D // (outer * LOW)

    def widen(a, axis):
        if outer == 1:
            return a
        return lax.all_gather(a, "dp", axis=axis, tiled=True, axis_index_groups=groups)

    def narrow(a, axis):
        if outer == 1:
            return a
        return lax.psum_scatter(a, "dp", scatter_dimension=axis, tiled=True, axis_index_groups=groups)

    def turn(a, first, second):
        if outer == 1:
            return a
        return a.reshape(T, first, second, piece).swapaxes(1, 2).reshape(T, D)

    w_qkv, w_in = widen(w_qkv, 0), widen(w_in, 0)
    w_out, w_down = widen(w_out, 1), widen(w_down, 1)
    gains = [widen(g, 0) for g in (gain_attn, gain_mlp)]
    x = turn(tokens, outer, LOW)
    dy = turn(grad_output, outer, LOW)
    plan = Plan(nz, D, T, w_qkv.shape[2], w_in.shape[2])
    p = plan
    U, L, real, pad = p.units, p.lane, p.hid_real, p.hid - p.hid_real
    gain_rows = jnp.pad(jnp.stack(gains), ((0, 14), (0, 0)))
    gain_rows = jnp.broadcast_to(gain_rows[None], (2, 16, L))
    out_rows = w_out.reshape(2, U, L)
    qkv_rows = w_qkv.reshape(L, 3, 2, U).transpose(2, 1, 3, 0).reshape(2, 3 * U, L)
    in_rows = w_in.reshape(L, 2, 2, real).transpose(2, 1, 3, 0)
    in_rows = jnp.pad(in_rows, ((0, 0), (0, 0), (0, pad), (0, 0))).reshape(2, 2 * p.hid, L)
    down_rows = jnp.pad(w_down.reshape(2, real, L), ((0, 0), (0, pad), (0, 0)))
    packed = jnp.concatenate([gain_rows, out_rows, qkv_rows, in_rows, down_rows], axis=1)

    freq = THETA ** (-(jnp.arange(HD // 2).astype(F32) * 2.0 / HD))
    angle = freq[:, None] * jnp.arange(LEN).astype(F32)[None, :]
    out, gtok, gw = layer(plan, x, dy, packed, jnp.cos(angle), jnp.sin(angle))

    out, gtok = turn(out, LOW, outer), turn(gtok, LOW, outer)

    def rows(name):
        off, n = p.pieces[name]
        return gw[:, off : off + n, :]

    g_out = rows("o").reshape(2 * U, L)
    g_qkv = rows("q").reshape(2, 3, U, L).transpose(3, 1, 0, 2).reshape(L, 3, 2 * U)
    g_in = jnp.stack([rows("a")[:, :real], rows("b")[:, :real]]).transpose(3, 0, 1, 2).reshape(L, 2, 2 * real)
    g_down = rows("d")[:, :real].reshape(2 * real, L)
    g_gain = rows("n")[0] + rows("n")[1]
    return (
        out,
        gtok,
        narrow(g_qkv, 0),
        narrow(g_out, 1),
        narrow(g_in, 0),
        narrow(g_down, 1),
        narrow(g_gain[0], 0),
        narrow(g_gain[1], 0),
    )


def solution(mesh):
    rows = P(("dp", "tensor"), None)
    deep = P("dp", None, "tensor")
    wide = P("tensor", "dp")
    flat = P("dp")
    return jax.shard_map(
        functools.partial(local, mesh.shape["dp"] // LOW, mesh.shape["tensor"]),
        mesh=mesh,
        in_specs=(rows, deep, wide, deep, wide, flat, flat, rows),
        out_specs=(rows, rows, deep, wide, deep, wide, flat, flat),
        check_vma=False,
    )
```

```python
import functools

import jax
import jax.numpy as jnp
import numpy as np
from jax import lax
from jax.experimental import pallas as pl
from jax.experimental.pallas import tpu as pltpu
from jax.sharding import PartitionSpec as P

HD = 64
LEN = 1024
EPS = 1e-05
THETA = 160000.0
MESH = pl.DeviceIdType.MESH
BF = jnp.bfloat16
F32 = jnp.float32
LOW = 8


def up(n, m):
    return -(-n // m) * m


def dg(a, b, ca, cb):
    return lax.dot_general(a, b, (((ca,), (cb,)), ((), ())), preferred_element_type=F32)


class Plan:
    def __init__(self, nz, width, tokens, units, hidden):
        self.nz, self.width, self.tokens = nz, width, tokens
        self.lane = width // LOW
        self.block = 2 * self.lane
        self.units = units // 2
        self.heads = self.units // HD
        self.real = hidden
        self.hid = up(-(-hidden // 2), 16)
        self.cuts = next(n for n in (3, 2, 1) if self.hid % (16 * n) == 0)
        self.sub = self.hid // self.cuts
        self.pieces = {}
        total = 0
        sizes = [("n", 16), ("o", self.units)]
        sizes += [(f"q{j}", 3 * HD) for j in range(self.heads)]
        sizes += [(f"{m}{i}", self.sub) for m in "abd" for i in range(self.cuts)]
        for name, rows in sizes:
            self.pieces[name] = (total, rows)
            total += rows
        self.rows = total
        self.order = ["n", "o"] + [f"q{j}" for j in range(self.heads)]
        self.order += [f"{m}{i}" for i in range(self.cuts) for m in "ab"]
        self.order += [f"d{i}" for i in range(self.cuts)]


def kernel(
    plan,
    x_hbm,
    dy_hbm,
    gains,
    w_o_hbm,
    w_q_hbm,
    w_ab_hbm,
    w_d_hbm,
    rope_hbm,
    out_hbm,
    gtok_hbm,
    g_n_hbm,
    g_o_hbm,
    g_q_hbm,
    g_ab_hbm,
    g_d_hbm,
    W,
    xown,
    dyf,
    n1,
    qkv,
    att,
    lse,
    res,
    n2,
    AB,
    hid,
    gat,
    exs,
    exr,
    Gn,
    Gb,
    Gd,
    R1,
    R2,
    R3,
    rope,
    stage,
    zr,
    zs,
    xyr,
    xys,
    r1r,
    r1s,
    r2r,
    r2s,
    r3r,
    r3s,
    swr,
    sws,
    cr,
    cs,
    gs,
):
    p = plan
    nz, D, T, U, H = p.nz, p.width, p.tokens, p.units, p.hid
    S = 2 * T
    L, B = p.lane, p.block
    d = lax.axis_index("dp")
    z = lax.axis_index("tensor")
    c = lax.rem(d, 2)
    r = lax.rem(d // 2, 4)
    xb = lax.rem(r, 2)
    yb = r // 2
    zb = lax.rem(z, 2)
    sib = d + 1 - 2 * c
    xp = d + 2 - 4 * xb
    yp = d + 4 - 8 * yb
    zpair = z + 1 - 2 * zb
    rx = r + 1 - 2 * xb
    ry = r + 2 - 4 * yb
    rd = 3 - r
    stay = lax.rem(c + z, 2) == 0

    def rows_at(start, n):
        return pl.ds(pl.multiple_of(start, 16), n)

    def lanes(block):
        return pl.ds(pl.multiple_of(block * B, L), B)

    mine = rows_at(c * T, T)
    theirs_start = (1 - c) * T

    def remote(src, dst, ssem, rsem, dev):
        pltpu.make_async_remote_copy(src, dst, ssem, rsem, device_id=dev, device_id_type=MESH).start()

    def take(ref, sem):
        pltpu.make_async_copy(ref, ref, sem).wait()

    partners = [(sib, z), (xp, z), (yp, z)]
    for dz in range(1, nz):
        there = lax.rem(z + dz, nz)
        partners += [(d, there), (sib, there)]
    bar = pltpu.get_barrier_semaphore()
    for dev in partners:
        pl.semaphore_signal(bar, inc=1, device_id=dev, device_id_type=MESH)
    pl.semaphore_wait(bar, len(partners))

    index = {name: i for i, name in enumerate(p.pieces)}
    M, cuts = p.sub, p.cuts

    def shard(name, k):
        kind, j = name[0], int(name[1:] or 0)
        if kind == "n":
            return gains
        if kind == "o":
            return w_o_hbm.at[rows_at(k * U, U), :]
        if kind == "q":
            return w_q_hbm.at[rows_at(k * 3 * U + j * 3 * HD, 3 * HD), :]
        if kind == "d":
            return w_d_hbm.at[rows_at(k * H + j * M, M), :]
        return w_ab_hbm.at[0 if kind == "a" else 1, rows_at(k * H + j * M, M), :]

    def base(name):
        return nz * p.pieces[name][0]

    def count(name):
        return p.pieces[name][1]

    def z_start(name):
        off, n = p.pieces[name]
        i = index[name]
        dst = W.at[rows_at(base(name) + z * n, n), pl.ds(pl.multiple_of(r * B + c * L, L), L)]
        for dz in range(nz):
            there = lax.rem(z + dz, nz)
            for kk in range(2):
                k = lax.rem(c + kk, 2)
                src = shard(name, k)
                if dz == 0 and kk == 0:
                    pltpu.make_async_copy(src, dst, zr.at[i]).start()
                else:
                    remote(src, dst, zs.at[i], zr.at[i], (d if kk == 0 else sib, there))

    def half(name, which):
        n = (nz // 2) * count(name)
        return pl.ds(base(name) + which * n, n)

    def xy1(name):
        i = index[name]
        take(W.at[pl.ds(base(name), nz * count(name)), lanes(r)], zr.at[i])
        a = W.at[half(name, 0), lanes(r)]
        b = W.at[half(name, 1), lanes(r)]
        remote(a, a, xys.at[i], xyr.at[i, 0], (xp, z))
        remote(b, b, xys.at[i], xyr.at[i, 1], (yp, z))
        remote(a, a, xys.at[i], xyr.at[i, 2], (yp, z))
        remote(b, b, xys.at[i], xyr.at[i, 3], (xp, z))

    def xy2(name):
        i = index[name]
        a = W.at[half(name, 0), lanes(rx)]
        b = W.at[half(name, 1), lanes(ry)]
        take(a, xyr.at[i, 0])
        remote(a, a, xys.at[i], xyr.at[i, 4], (yp, z))
        take(b, xyr.at[i, 1])
        remote(b, b, xys.at[i], xyr.at[i, 5], (xp, z))

    def ready(name):
        i = index[name]
        take(W.at[half(name, 0), lanes(ry)], xyr.at[i, 2])
        take(W.at[half(name, 1), lanes(rx)], xyr.at[i, 3])
        take(W.at[half(name, 0), lanes(rd)], xyr.at[i, 4])
        take(W.at[half(name, 1), lanes(rd)], xyr.at[i, 5])

    def sent(name):
        i = index[name]
        n = count(name)
        take(R3.at[pl.ds(0, 2 * nz - 1), pl.ds(0, n), :], zs.at[i])
        take(W.at[pl.ds(0, 6 * (nz // 2) * n * B // D), :], xys.at[i])

    place = {"n": (Gn, 0), "o": (W, base("a0") + nz * 3 * U)}
    for j in range(p.heads):
        place[f"q{j}"] = (W, base("a0") + j * nz * 3 * HD)
    for i in range(cuts):
        place[f"a{i}"] = (W, base("d0") + i * nz * M)
        place[f"b{i}"] = (Gb, i * nz * M)
        place[f"d{i}"] = (Gd, i * nz * M)

    def ghalf(name, which):
        n = (nz // 2) * count(name)
        return pl.ds(place[name][1] + which * n, n)

    def rhalf(name):
        return pl.ds((nz // 2) * p.pieces[name][0], (nz // 2) * count(name))

    def step_of(n):
        for s in (128, 112, 96, 80, 64, 48, 32, 16):
            if n % s == 0:
                return s
        return n

    def rs1(name):
        i = index[name]
        G = place[name][0]
        to = rhalf(name)
        for which, near, dev in ((0, ry, yp), (1, rx, xp)):
            rows = ghalf(name, which)
            remote(G.at[rows, lanes(rd)], R1.at[which, 0, to, :], r1s.at[i], r1r.at[i, which, 0], (dev, z))
        for which, near, dev in ((0, ry, yp), (1, rx, xp)):
            rows = ghalf(name, which)
            remote(G.at[rows, lanes(near)], R1.at[which, 1, to, :], r1s.at[i], r1r.at[i, which, 1], (dev, z))

    def rs2(name):
        i = index[name]
        G, gb = place[name]
        n = (nz // 2) * count(name)
        to = rhalf(name)
        s = step_of(n)
        for which, block, dev in ((0, rx, xp), (1, ry, yp)):
            take(R1.at[which, 0, to, :], r1r.at[i, which, 0])

            def add(t, _):
                g = rows_at(gb + which * n + t * s, s)
                q = rows_at(to.start + t * s, s)
                G[g, lanes(block)] = (G[g, lanes(block)].astype(F32) + R1[which, 0, q, :].astype(F32)).astype(BF)
                return 0

            lax.fori_loop(0, n // s, add, 0)
            remote(
                G.at[ghalf(name, which), lanes(block)],
                R2.at[which, to, :],
                r2s.at[i],
                r2r.at[i, which],
                (dev, z),
            )

    def rs3(name):
        i = index[name]
        G, gb = place[name]
        off, m = p.pieces[name]
        n = (nz // 2) * m
        to = rhalf(name)
        s = step_of(n)
        for which in range(2):
            take(R1.at[which, 1, to, :], r1r.at[i, which, 1])
            take(R2.at[which, to, :], r2r.at[i, which])

            def add(t, _):
                g = rows_at(gb + which * n + t * s, s)
                q = rows_at(to.start + t * s, s)
                total = G[g, lanes(r)].astype(F32) + R1[which, 1, q, :].astype(F32) + R2[which, q, :].astype(F32)
                G[g, lanes(r)] = total.astype(BF)
                return 0

            lax.fori_loop(0, n // s, add, 0)
        dst = R3.at[z * 2 + c, pl.ds(off, m), :]
        for dz in range(nz):
            there = lax.rem(z + dz, nz)
            for kk in range(2):
                k = lax.rem(c + kk, 2)
                src = G.at[rows_at(gb + there * m, m), pl.ds(pl.multiple_of(r * B + k * L, L), L)]
                if dz == 0 and kk == 0:
                    pltpu.make_async_copy(src, dst, r3r.at[i]).start()
                else:
                    remote(src, dst, r3s.at[i], r3r.at[i], (d if kk == 0 else sib, there))

    def rs4(name):
        i = index[name]
        off, m = p.pieces[name]
        take(R3.at[:, pl.ds(off, m), :], r3r.at[i])
        for k in range(2):
            total = R3[k, off : off + m, :].astype(F32)
            for j in range(1, nz):
                total += R3[2 * j + k, off : off + m, :].astype(F32)
            stage[k, off : off + m, :] = total
        if name == "n":
            stage[0, off : off + m, :] += stage[1, off : off + m, :]
        for j, (src, dst) in enumerate(stores(name)):
            pltpu.make_async_copy(src, dst, gs.at[i, j]).start()

    def stores(name):
        off, m = p.pieces[name]
        kind, j = name[0], int(name[1:] or 0)
        if kind == "n":
            return [(stage.at[0, pl.ds(off, m), :], g_n_hbm)]
        pairs = []
        for k in range(2):
            n = m
            if kind == "o":
                dst, at = g_o_hbm, k * U
            elif kind == "q":
                dst, at = g_q_hbm, k * 3 * U + j * 3 * HD
            else:
                at = k * H + j * M
                n = min(m, p.real - at)
                dst = g_d_hbm if kind == "d" else g_ab_hbm.at[0 if kind == "a" else 1]
            if n > 0:
                pairs.append((stage.at[k, pl.ds(off, n), :], dst.at[pl.ds(at, n), :]))
        return pairs

    def stored(name):
        for j, (src, dst) in enumerate(stores(name)):
            take(dst, gs.at[index[name], j])

    def rs_sent(name):
        i = index[name]
        m = count(name)
        n = (nz // 2) * m
        take(W.at[pl.ds(0, 4 * n * B // D), :], r1s.at[i])
        take(W.at[pl.ds(0, 2 * n * B // D), :], r2s.at[i])
        take(R3.at[pl.ds(0, 2 * nz - 1), pl.ds(0, m), :], r3s.at[i])

    def swap(src, dst_here, dst_there, i):
        @pl.when(stay)
        def _():
            pltpu.make_async_copy(src, dst_here, swr.at[i]).start()

        @pl.when(jnp.logical_not(stay))
        def _():
            remote(src, dst_there, sws.at[i], swr.at[i], (sib, zpair))

    def swap_sent(src, i):
        @pl.when(jnp.logical_not(stay))
        def _():
            take(src, sws.at[i])

    def give(src, dst, i):
        remote(src, dst, cs.at[i], cr.at[i], (sib, z))

    def give_rows(buf, i):
        give(buf.at[mine, :], buf.at[mine, :], i)

    def got_rows(buf, i):
        take(buf.at[mine, :], cr.at[i])

    NB = 64

    order = p.order
    steps = iter(range(len(order) + 1))

    def pump():
        k = next(steps)
        if k < len(order):
            xy1(order[k])
        if k + 2 < len(order):
            z_start(order[k + 2])
        if 0 < k:
            xy2(order[k - 1])

    z_start(order[0])
    z_start(order[1])
    swap(x_hbm, xown, xown, 0)
    pltpu.make_async_copy(rope_hbm, rope, gs.at[len(order), 0]).start()
    cos_ref, sin_ref = rope.at[0], rope.at[1]
    pump()
    pump()
    ready("n")
    take(xown, swr.at[0])

    gain_one = W[0:16, :][0:1, :].astype(F32)
    gain_two = W[0:16, :][1:2, :].astype(F32)

    def norm_parts(v):
        mean = jnp.mean(v, axis=1, keepdims=True)
        cen = v - mean
        inv = lax.rsqrt(jnp.mean(cen * cen, axis=1, keepdims=True) + EPS)
        return cen, inv

    def norm_first(t, _):
        own = rows_at(t * NB, NB)
        cen, inv = norm_parts(xown[own, :].astype(F32))
        n1[rows_at(c * T + t * NB, NB), :] = (cen * inv * gain_one).astype(BF)
        return 0

    pump()
    lax.fori_loop(0, T // NB, norm_first, 0)
    give_rows(n1, 0)
    for j in range(p.heads):
        pump()
    swap(dy_hbm, dyf.at[mine, :], dyf.at[rows_at(theirs_start, T), :], 1)
    got_rows(n1, 0)
    take(rope, gs.at[len(order), 0])

    TB = 256
    QR = nz * 3 * HD

    def project(t, _):
        j, ti = t // (S // TB), lax.rem(t, S // TB)
        cols = pl.ds(pl.multiple_of(ti * TB, TB), TB)
        acc = dg(W[rows_at(base("q0") + j * QR, QR), :], n1[cols, :], 1, 1)
        co, si = cos_ref[:, cols], sin_ref[:, cols]
        for zi in range(nz):
            parts = []
            for part in range(2):
                at = (zi * 3 + part) * HD
                v1, v2 = acc[at : at + HD // 2], acc[at + HD // 2 : at + HD]
                w1, w2 = v1 * co - v2 * si, v2 * co + v1 * si
                if part == 0:
                    w1, w2 = w1 * HD**-0.5, w2 * HD**-0.5
                parts += [w1, w2]
            parts.append(acc[(zi * 3 + 2) * HD : (zi * 3 + 3) * HD])
            qkv[rows_at(j * QR + zi * 3 * HD, 3 * HD), cols] = jnp.concatenate(parts, axis=0).astype(BF)
        return 0

    QB = 256

    def head_rows(t):
        q, k, v = (rows_at((t * 3 + part) * HD, HD) for part in range(3))
        return q, k, v, rows_at(lax.rem(t, nz) * U + t // nz * HD, HD)

    def attend(t, _):
        q_rows, k_rows, v_rows, o_rows = head_rows(t)
        key = qkv[k_rows, :].T
        val = qkv[v_rows, :]

        def block(b, _):
            cols = pl.ds(pl.multiple_of(b * QB, QB), QB)
            s = dg(key, qkv[q_rows, cols], 1, 0)
            m = jnp.max(s, axis=0, keepdims=True)
            e = jnp.exp(s - m)
            l = jnp.sum(e, axis=0, keepdims=True)
            o = dg(val, e.astype(BF), 1, 0)
            att[o_rows, cols] = (o / l).astype(BF)
            lse[t, :, cols] = m + jnp.log(l)
            return 0

        lax.fori_loop(0, S // QB, block, 0)
        return 0

    for j in range(p.heads):
        ready(f"q{j}")
        lax.fori_loop(j * (S // TB), (j + 1) * (S // TB), project, 0)
    pump()
    NH = nz * p.heads
    for t in range(0, NH, 2):
        lax.fori_loop(t, t + 2, attend, 0)
        pump()
    ready("o")

    MB = 256

    def partial(lhs_rows, rhs, start):
        cols = pl.ds(pl.multiple_of(start, MB), MB)
        total = None
        for lhs, w in zip(lhs_rows, rhs):
            term = dg(lhs(cols), w[...], 0, 0)
            total = term if total is None else total + term
        return total

    def send_partial(lhs_rows, rhs, slot, there, i):
        def some(t, _):
            exs[slot, rows_at(t * MB, MB), :] = partial(lhs_rows, rhs, theirs_start + t * MB).astype(BF)
            return 0

        lax.fori_loop(0, T // MB, some, 0)
        give(exs.at[slot], exr.at[there], i)

    w_o = W.at[pl.ds(base("o"), nz * U), :]
    w_q = W.at[pl.ds(base("q0"), nz * 3 * U), :]
    w_a = W.at[pl.ds(base("a0"), nz * H), :]
    w_b = W.at[pl.ds(base("b0"), nz * H), :]
    w_d = W.at[pl.ds(base("d0"), nz * H), :]

    lhs_att = [lambda cols: att[:, cols]]
    send_partial(lhs_att, [w_o], 0, 0, 2)

    def residual(t, _):
        own = rows_at(t * MB, MB)
        res[own, :] = xown[own, :].astype(F32) + partial(lhs_att, [w_o], c * T + t * MB)
        return 0

    lax.fori_loop(0, T // MB, residual, 0)
    take(exr.at[0], cr.at[2])

    def norm_second(t, _):
        own = rows_at(t * NB, NB)
        v = res[own, :] + exr[0, own, :].astype(F32)
        res[own, :] = v
        cen, inv = norm_parts(v)
        n2[rows_at(c * T + t * NB, NB), :] = (cen * inv * gain_two).astype(BF)
        return 0

    lax.fori_loop(0, T // NB, norm_second, 0)
    give_rows(n2, 3)
    take(dyf.at[mine, :], swr.at[1])
    give_rows(dyf, 1)
    pump()
    got_rows(n2, 3)

    HB = nz * M

    def hidden(t, _):
        i, ti = t // (S // TB), lax.rem(t, S // TB)
        cols = pl.ds(pl.multiple_of(ti * TB, TB), TB)
        rows = rows_at(i * HB, HB)
        normed = n2[cols, :]
        act = dg(W[rows_at(base("a0") + i * HB, HB), :], normed, 1, 1)
        gate = dg(W[rows_at(base("b0") + i * HB, HB), :], normed, 1, 1)
        cdf = 0.5 + 0.5 * lax.erf(act * 0.7071067811865476)
        gelu = act * cdf
        slope = cdf + act * (jnp.exp(-0.5 * act * act) * 0.3989422804014327)
        hid[rows, cols] = (gelu * gate).astype(BF)
        AB[0, rows, cols] = (slope * gate).astype(BF)
        AB[1, rows, cols] = gelu.astype(BF)
        return 0

    def grad_of(name, lhs, rhs):
        dest, at = place[name]
        dest[pl.ds(at, nz * p.pieces[name][1]), :] = dg(lhs, rhs[...], 1, 0).astype(BF)

    for i in range(cuts):
        ready(f"a{i}")
        ready(f"b{i}")
        lax.fori_loop(i * (S // TB), (i + 1) * (S // TB), hidden, 0)
        if i == 0:
            got_rows(dyf, 1)
        grad_of(f"d{i}", hid[i * HB : (i + 1) * HB, :], dyf)
        rs1(f"d{i}")
        pump()
    for _ in steps:
        raise ValueError("steps left")

    def back_hidden(t, _):
        i, ti = t // (S // TB), lax.rem(t, S // TB)
        cols = pl.ds(pl.multiple_of(ti * TB, TB), TB)
        rows = rows_at(i * HB, HB)
        g = dg(W[rows_at(base("d0") + i * HB, HB), :], dyf[cols, :], 1, 1)
        AB[0, rows, cols] = (g * AB[0, rows, cols].astype(F32)).astype(BF)
        AB[1, rows, cols] = (g * AB[1, rows, cols].astype(F32)).astype(BF)
        return 0

    for i in range(cuts):
        ready(f"d{i}")
        lax.fori_loop(i * (S // TB), (i + 1) * (S // TB), back_hidden, 0)
        grad_of(f"b{i}", AB[1, i * HB : (i + 1) * HB, :], n2)
        rs1(f"b{i}")

    lhs_hid = [lambda cols: hid[:, cols]]
    lhs_gp = [lambda cols: AB[0, :, cols], lambda cols: AB[1, :, cols]]
    take(exs.at[0], cs.at[2])
    send_partial(lhs_hid, [w_d], 0, 0, 4)
    send_partial(lhs_gp, [w_a, w_b], 1, 1, 5)
    take(exr.at[0], cr.at[4])
    take(exs.at[0], cs.at[4])

    def output(t, _):
        own = rows_at(t * MB, MB)
        total = partial(lhs_hid, [w_d], c * T + t * MB)
        xs = res[own, :] + (total + exr[0, own, :].astype(F32))
        exs[0, own, :] = xs.astype(BF)
        return 0

    lax.fori_loop(0, T // MB, output, 0)
    swap(exs.at[0], out_hbm, out_hbm, 2)

    for i in range(cuts):
        sent(f"d{i}")
    for i in range(cuts):
        grad_of(f"a{i}", AB[0, i * HB : (i + 1) * HB, :], n2)
        rs1(f"a{i}")
    rs2("d0")
    take(exr.at[1], cr.at[5])

    def grad_residual(t, carry):
        own = rows_at(t * MB, MB)
        total = partial(lhs_gp, [w_a, w_b], c * T + t * MB) + exr[1, own, :].astype(F32)
        v = res[own, :]
        cen, inv = norm_parts(v)
        hat = cen * inv
        carry = carry + jnp.sum(total * hat, axis=0, keepdims=True)
        dh = total * gain_two
        back = inv * (
            dh - jnp.mean(dh, axis=1, keepdims=True) - hat * jnp.mean(dh * hat, axis=1, keepdims=True)
        )
        g = dyf[rows_at(c * T + t * MB, MB), :].astype(F32) + back
        res[own, :] = g
        dyf[rows_at(c * T + t * MB, MB), :] = g.astype(BF)
        return carry

    take(dyf.at[mine, :], cs.at[1])
    gain_two_grad = lax.fori_loop(0, T // MB, grad_residual, jnp.zeros((1, D), F32))
    give_rows(dyf, 6)
    for i in range(1, cuts):
        rs2(f"d{i}")
    got_rows(dyf, 6)

    sent("o")
    for i in range(cuts):
        sent(f"a{i}")
        sent(f"b{i}")

    def grad_att(t, _):
        rows = rows_at(t * U, U)
        gat[rows, :] = dg(W[rows_at(base("o") + t * U, U), :], dyf[...], 1, 1).astype(BF)
        return 0

    lax.fori_loop(0, nz, grad_att, 0)
    grad_of("o", att[...], dyf)
    rs1("o")

    def attend_back(t, _):
        q_rows, k_rows, v_rows, o_rows = head_rows(t)
        keyT = qkv[k_rows, :]
        key = keyT.T
        val = qkv[v_rows, :].T

        def block(b, carry):
            dk, dv = carry
            cols = pl.ds(pl.multiple_of(b * QB, QB), QB)
            q = qkv[q_rows, cols]
            g = gat[o_rows, cols]
            inner = jnp.sum(g.astype(F32) * att[o_rows, cols].astype(F32), axis=0, keepdims=True)
            prob = jnp.exp(dg(key, q, 1, 0) - lse[t, :, cols])
            dprob = dg(val, g, 1, 0)
            ds = (prob * (dprob - inner)).astype(BF)
            dv = dv + dg(g, prob.astype(BF), 1, 1)
            dk = dk + dg(q, ds, 1, 1)
            dq = dg(keyT, ds, 1, 0) * HD**-0.5
            co, si = cos_ref[:, cols], sin_ref[:, cols]
            g1, g2 = dq[: HD // 2], dq[HD // 2 :]
            qkv[q_rows, cols] = jnp.concatenate([g1 * co + g2 * si, g2 * co - g1 * si], axis=0).astype(BF)
            return dk, dv

        zero = jnp.zeros((HD, S), F32)
        dk, dv = lax.fori_loop(0, S // QB, block, (zero, zero))
        g1, g2 = dk[: HD // 2], dk[HD // 2 :]
        co, si = cos_ref[...], sin_ref[...]
        qkv[k_rows, :] = jnp.concatenate([g1 * co + g2 * si, g2 * co - g1 * si], axis=0).astype(BF)
        qkv[v_rows, :] = dv.astype(BF)
        return 0

    todo = [[] for _ in range(NH // 2)]
    ab = [f"{m}{i}" for i in range(cuts) for m in "ba"]
    ds = [f"d{i}" for i in range(cuts)]
    for t, name in enumerate(ab):
        todo[t * len(todo) // len(ab)].append((rs2, name))
    for t, name in enumerate(ds):
        todo[min(t + 1, len(todo) - 1)].append((rs3, name))
    for t in range(0, NH, 2):
        lax.fori_loop(t, t + 2, attend_back, 0)
        if (t + 2) % nz == 0:
            j = t // nz
            grad_of(f"q{j}", qkv[j * QR : (j + 1) * QR, :], n1)
            rs1(f"q{j}")
        for step, name in todo[t // 2]:
            step(name)
    rs2("o")
    for name in ab:
        rs3(name)

    lhs_proj = [lambda cols: qkv[:, cols]]
    take(exs.at[1], cs.at[5])
    send_partial(lhs_proj, [w_q], 1, 0, 7)
    for j in range(p.heads - 1):
        rs2(f"q{j}")
    swap_sent(exs.at[0], 2)
    take(out_hbm, swr.at[2])
    take(exr.at[0], cr.at[7])

    def grad_input(t, carry):
        own = rows_at(t * MB, MB)
        total = partial(lhs_proj, [w_q], c * T + t * MB) + exr[0, own, :].astype(F32)
        cen, inv = norm_parts(xown[own, :].astype(F32))
        hat = cen * inv
        carry = carry + jnp.sum(total * hat, axis=0, keepdims=True)
        dh = total * gain_one
        back = inv * (
            dh - jnp.mean(dh, axis=1, keepdims=True) - hat * jnp.mean(dh * hat, axis=1, keepdims=True)
        )
        exs[0, own, :] = (res[own, :] + back).astype(BF)
        return carry

    gain_one_grad = lax.fori_loop(0, T // MB, grad_input, jnp.zeros((1, D), F32))
    swap(exs.at[0], gtok_hbm, gtok_hbm, 3)
    line = lax.broadcasted_iota(jnp.int32, (16, D), 0)
    both = jnp.where(line == 0, gain_one_grad, jnp.where(line == 1, gain_two_grad, 0.0)).astype(BF)
    for j in range(nz):
        Gn[16 * j : 16 * j + 16, :] = both
    rs1("n")
    last = f"q{p.heads - 1}"
    rs2(last)
    rs2("n")
    rs3("o")
    for j in range(p.heads):
        rs3(f"q{j}")
    rs3("n")
    for name in ds + ab + ["o"] + [f"q{j}" for j in range(p.heads)] + ["n"]:
        rs4(name)

    sent("n")
    for j in range(p.heads):
        sent(f"q{j}")
    for name in p.order:
        rs_sent(name)
    swap_sent(x_hbm, 0)
    swap_sent(dy_hbm, 1)
    swap_sent(exs.at[0], 3)
    take(gtok_hbm, swr.at[3])
    take(n1.at[mine, :], cs.at[0])
    take(n2.at[mine, :], cs.at[3])
    take(dyf.at[mine, :], cs.at[6])
    take(exs.at[1], cs.at[7])
    for name in p.order:
        stored(name)


def layer(plan, x, dy, gains, w_o, w_q, w_ab, w_d, rope):
    p = plan
    nz, D, T, U, H = p.nz, p.width, p.tokens, p.units, p.hid
    S, L = 2 * T, p.lane
    n = len(p.order)
    hbm = pl.BlockSpec(memory_space=pl.ANY)
    dma = pltpu.SemaphoreType.DMA
    scratch = [
        pltpu.VMEM((nz * p.rows, D), BF),
        pltpu.VMEM((T, D), BF),
        pltpu.VMEM((S, D), BF),
        pltpu.VMEM((S, D), BF),
        pltpu.VMEM((nz * 3 * U, S), BF),
        pltpu.VMEM((nz * U, S), BF),
        pltpu.VMEM((nz * p.heads, 1, S), F32),
        pltpu.VMEM((T, D), F32),
        pltpu.VMEM((S, D), BF),
        pltpu.VMEM((2, nz * H, S), BF),
        pltpu.VMEM((nz * H, S), BF),
        pltpu.VMEM((nz * U, S), BF),
        pltpu.VMEM((2, T, D), BF),
        pltpu.VMEM((2, T, D), BF),
        pltpu.VMEM((nz * 16, D), BF),
        pltpu.VMEM((nz * H, D), BF),
        pltpu.VMEM((nz * H, D), BF),
        pltpu.VMEM((2, 2, (nz // 2) * p.rows, p.block), BF),
        pltpu.VMEM((2, (nz // 2) * p.rows, p.block), BF),
        pltpu.VMEM((2 * nz, p.rows, p.lane), BF),
        pltpu.VMEM((2, HD // 2, S), F32),
        pltpu.VMEM((2, p.rows, L), F32),
        dma((n,)),
        dma((n,)),
        dma((n, 6)),
        dma((n,)),
        dma((n, 2, 2)),
        dma((n,)),
        dma((n, 2)),
        dma((n,)),
        dma((n,)),
        dma((n,)),
        dma((4,)),
        dma((4,)),
        dma((8,)),
        dma((8,)),
        dma((n + 1, 2)),
    ]
    return pl.pallas_call(
        functools.partial(kernel, p),
        out_shape=(
            jax.ShapeDtypeStruct((T, D), BF),
            jax.ShapeDtypeStruct((T, D), BF),
            jax.ShapeDtypeStruct((16, L), F32),
            jax.ShapeDtypeStruct((2 * U, L), F32),
            jax.ShapeDtypeStruct((6 * U, L), F32),
            jax.ShapeDtypeStruct((2, p.real, L), F32),
            jax.ShapeDtypeStruct((p.real, L), F32),
        ),
        in_specs=[hbm] * 8,
        out_specs=(hbm,) * 7,
        scratch_shapes=scratch,
        compiler_params=pltpu.CompilerParams(
            collective_id=0, has_side_effects=True, vmem_limit_bytes=64 * 1024 * 1024 - 65536
        ),
        name="layer",
    )(x, dy, gains, w_o, w_q, w_ab, w_d, rope)


def rope_table():
    freq = THETA ** (-np.arange(HD // 2) * 2.0 / HD)
    angle = freq.astype(np.float32)[:, None] * np.arange(LEN, dtype=np.float32)[None, :]
    return np.stack([np.cos(angle), np.sin(angle)]).astype(np.float32)


def local(outer, nz, tokens, w_qkv, w_out, w_in, w_down, gain_attn, gain_mlp, grad_output):
    T, D = tokens.shape
    groups = [[hi * LOW + lo for hi in range(outer)] for lo in range(LOW)]
    piece = D // (outer * LOW)

    def widen(a, axis):
        if outer == 1:
            return a
        return lax.all_gather(a, "dp", axis=axis, tiled=True, axis_index_groups=groups)

    def narrow(a, axis):
        if outer == 1:
            return a
        return lax.psum_scatter(a, "dp", scatter_dimension=axis, tiled=True, axis_index_groups=groups)

    def turn(a, first, second):
        if outer == 1:
            return a
        return a.reshape(T, first, second, piece).swapaxes(1, 2).reshape(T, D)

    w_qkv, w_in = widen(w_qkv, 0), widen(w_in, 0)
    w_out, w_down = widen(w_out, 1), widen(w_down, 1)
    gains = [widen(g, 0) for g in (gain_attn, gain_mlp)]
    x = turn(tokens, outer, LOW)
    dy = turn(grad_output, outer, LOW)
    p = Plan(nz, D, T, w_qkv.shape[2], w_in.shape[2])
    U, L, H, heads, real = p.units, p.lane, p.hid, p.heads, p.real
    gain_rows = jnp.pad(jnp.stack(gains), ((0, 14), (0, 0)))
    qkv_rows = w_qkv.reshape(L, 3, 2, heads, HD).transpose(2, 3, 1, 4, 0).reshape(6 * U, L)
    in_rows = jnp.pad(w_in.transpose(1, 2, 0), ((0, 0), (0, 2 * H - real), (0, 0)))
    down_rows = jnp.pad(w_down, ((0, 2 * H - real), (0, 0)))
    rope = jnp.asarray(rope_table())
    out, gtok, g_n, g_out, g_q, g_ab, g_down = layer(p, x, dy, gain_rows, w_out, qkv_rows, in_rows, down_rows, rope)

    out, gtok = turn(out, LOW, outer), turn(gtok, LOW, outer)
    g_qkv = g_q.reshape(2, heads, 3, HD, L).transpose(4, 2, 0, 1, 3).reshape(L, 3, 2 * U)
    g_in = g_ab.transpose(2, 0, 1)
    return (
        out,
        gtok,
        narrow(g_qkv, 0),
        narrow(g_out, 1),
        narrow(g_in, 0),
        narrow(g_down, 1),
        narrow(g_n[0], 0),
        narrow(g_n[1], 0),
    )


def solution(mesh):
    rows = P(("dp", "tensor"), None)
    deep = P("dp", None, "tensor")
    wide = P("tensor", "dp")
    flat = P("dp")
    return jax.shard_map(
        functools.partial(local, mesh.shape["dp"] // LOW, mesh.shape["tensor"]),
        mesh=mesh,
        in_specs=(rows, deep, wide, deep, wide, flat, flat, rows),
        out_specs=(rows, rows, deep, wide, deep, wide, flat, flat),
        check_vma=False,
    )
```

```python
import functools

import jax
import jax.numpy as jnp
import numpy as np
from jax import lax
from jax.experimental import pallas as pl
from jax.experimental.pallas import tpu as pltpu
from jax.sharding import PartitionSpec as P

HD = 64
LEN = 1024
EPS = 1e-05
THETA = 160000.0
MESH = pl.DeviceIdType.MESH
BF = jnp.bfloat16
F32 = jnp.float32
VMEM = 64 * 1024 * 1024 - 65536
LOW = 8


def up(n, m):
    return -(-n // m) * m


def dg(a, b, ca, cb):
    return lax.dot_general(a, b, (((ca,), (cb,)), ((), ())), preferred_element_type=F32)


class Plan:
    def __init__(self, nz, width, tokens, units, hidden):
        self.nz, self.width, self.tokens = nz, width, tokens
        self.lane = width // LOW
        self.block = 2 * self.lane
        self.units = units // 2
        self.heads = self.units // HD
        self.real = hidden
        self.hid = up(-(-hidden // 2), 16)
        self.cuts = next(n for n in (3, 2, 1) if self.hid % (16 * n) == 0)
        self.sub = self.hid // self.cuts
        self.pieces = {}
        total = 0
        sizes = [("n", 16), ("o", self.units)]
        sizes += [(f"q{j}", 3 * HD) for j in range(self.heads)]
        sizes += [(f"{m}{i}", self.sub) for m in "abd" for i in range(self.cuts)]
        for name, rows in sizes:
            self.pieces[name] = (total, rows)
            total += rows
        self.rows = total
        self.order = ["n", "o"] + [f"q{j}" for j in range(self.heads)]
        self.order += [f"{m}{i}" for i in range(self.cuts) for m in "ab"]
        self.order += [f"d{i}" for i in range(self.cuts)]
        self.late = self.order[-1:] if self.cuts > 1 else []
        self.early = [f"d{i}" for i in range(len(self.late))]


def kernel(
    plan,
    x_hbm,
    dy_hbm,
    gain_a_hbm,
    gain_m_hbm,
    w_o_hbm,
    w_q_hbm,
    w_ab_hbm,
    w_d_hbm,
    rope_hbm,
    out_hbm,
    gtok_hbm,
    g_n_hbm,
    g_o_hbm,
    g_q_hbm,
    g_ab_hbm,
    g_d_hbm,
    W,
    xown,
    dyf,
    n1,
    qkv,
    att,
    lse,
    res,
    n2,
    AB,
    hid,
    gat,
    exs,
    exr,
    Gn,
    Gb,
    Gd,
    R1,
    R2,
    R3,
    RZ,
    rope,
    stage,
    gains,
    gain_rows,
    w_q_in,
    w_q,
    w_ab,
    w_d,
    g_q,
    zr,
    zs,
    xyr,
    xys,
    r1r,
    r1s,
    r2r,
    r2s,
    r3r,
    r3s,
    swr,
    sws,
    cr,
    cs,
    gs,
    lr,
    ls,
    er,
    es,
    ins,
):
    p = plan
    nz, D, T, U, H = p.nz, p.width, p.tokens, p.units, p.hid
    S = 2 * T
    L, B = p.lane, p.block
    d = lax.axis_index("dp")
    z = lax.axis_index("tensor")
    c = lax.rem(d, 2)
    r = lax.rem(d // 2, 4)
    xb = lax.rem(r, 2)
    yb = r // 2
    zb = lax.rem(z, 2)
    sib = d + 1 - 2 * c
    xp = d + 2 - 4 * xb
    yp = d + 4 - 8 * yb
    zpair = z + 1 - 2 * zb
    rx = r + 1 - 2 * xb
    ry = r + 2 - 4 * yb
    rd = 3 - r
    stay = lax.rem(c + z, 2) == 0

    def rows_at(start, n):
        return pl.ds(pl.multiple_of(start, 16), n)

    def lanes(block):
        return pl.ds(pl.multiple_of(block * B, L), B)

    mine = rows_at(c * T, T)
    theirs_start = (1 - c) * T

    def remote(src, dst, ssem, rsem, dev):
        pltpu.make_async_remote_copy(src, dst, ssem, rsem, device_id=dev, device_id_type=MESH).start()

    def take(ref, sem):
        pltpu.make_async_copy(ref, ref, sem).wait()

    partners = [(sib, z), (xp, z), (yp, z)]
    for dz in range(1, nz):
        there = lax.rem(z + dz, nz)
        partners += [(d, there), (sib, there)]
    bar = pltpu.get_barrier_semaphore()
    for dev in partners:
        pl.semaphore_signal(bar, inc=1, device_id=dev, device_id_type=MESH)

    def load(src, dst, i):
        return pltpu.make_async_copy(src, dst, ins.at[i])

    real = p.real
    loads = [
        load(gain_a_hbm, gains.at[0], 0),
        load(gain_m_hbm, gains.at[1], 1),
        load(w_q_hbm, w_q_in, 2),
        load(w_ab_hbm.at[0], w_ab.at[0, pl.ds(0, real), :], 3),
        load(w_ab_hbm.at[1], w_ab.at[1, pl.ds(0, real), :], 4),
        load(w_d_hbm, w_d.at[pl.ds(0, real), :], 5),
        load(rope_hbm, rope, 6),
    ]
    for copy in loads:
        copy.start()
    if 2 * H > real:
        zeros = jnp.zeros((2 * H - real, L), BF)
        w_ab[0, real:, :] = zeros
        w_ab[1, real:, :] = zeros
        w_d[real:, :] = zeros
    for copy in loads:
        copy.wait()
    line = lax.broadcasted_iota(jnp.int32, (16, L), 0)
    first, second = (gains[j, :, :].astype(F32) for j in range(2))
    gain_rows[...] = jnp.where(line == 0, first, jnp.where(line == 1, second, 0.0)).astype(BF)
    for part in range(3):
        turned = w_q_in[part, :, :].T
        for k in range(2):
            for j in range(p.heads):
                at = k * U + j * HD
                to = (k * p.heads + j) * 3 * HD + part * HD
                w_q[to : to + HD, :] = turned[at : at + HD, :]
    pl.semaphore_wait(bar, len(partners))

    index = {name: i for i, name in enumerate(p.pieces)}
    M, cuts = p.sub, p.cuts

    def shard(name, k):
        kind, j = name[0], int(name[1:] or 0)
        if kind == "n":
            return gain_rows
        if kind == "o":
            return w_o_hbm.at[rows_at(k * U, U), :]
        if kind == "q":
            return w_q.at[rows_at(k * 3 * U + j * 3 * HD, 3 * HD), :]
        if kind == "d":
            return w_d.at[rows_at(k * H + j * M, M), :]
        return w_ab.at[0 if kind == "a" else 1, rows_at(k * H + j * M, M), :]

    def base(name):
        return nz * p.pieces[name][0]

    def count(name):
        return p.pieces[name][1]

    def z_start(name):
        off, n = p.pieces[name]
        i = index[name]
        dst = W.at[rows_at(base(name) + z * n, n), pl.ds(pl.multiple_of(r * B + c * L, L), L)]
        for dz in range(nz):
            there = lax.rem(z + dz, nz)
            for kk in range(2):
                k = lax.rem(c + kk, 2)
                src = shard(name, k)
                if dz == 0 and kk == 0:
                    pltpu.make_async_copy(src, dst, zr.at[i]).start()
                else:
                    remote(src, dst, zs.at[i], zr.at[i], (d if kk == 0 else sib, there))

    def part(block, which):
        return pl.ds(pl.multiple_of(block * B + which * L, L), L)

    def own_rows(name):
        n = count(name)
        return rows_at(base(name) + z * n, n)

    def late0(name):
        i = index[name]
        dst = W.at[own_rows(name), part(r, c)]
        pltpu.make_async_copy(shard(name, c), dst, zr.at[i]).start()
        remote(shard(name, 1 - c), dst, zs.at[i], zr.at[i], (sib, z))

    def late1(name):
        i = index[name]
        own = own_rows(name)
        take(W.at[own, lanes(r)], zr.at[i])
        a = W.at[own, part(r, 0)]
        b = W.at[own, part(r, 1)]
        remote(a, a, xys.at[i], xyr.at[i, 0], (xp, z))
        remote(b, b, xys.at[i], xyr.at[i, 1], (yp, z))
        remote(a, a, xys.at[i], xyr.at[i, 2], (yp, z))
        remote(b, b, xys.at[i], xyr.at[i, 3], (xp, z))

    def late2(name):
        i = index[name]
        own = own_rows(name)
        a = W.at[own, part(rx, 0)]
        b = W.at[own, part(ry, 1)]
        take(a, xyr.at[i, 0])
        remote(a, a, xys.at[i], xyr.at[i, 4], (yp, z))
        take(b, xyr.at[i, 1])
        remote(b, b, xys.at[i], xyr.at[i, 5], (xp, z))

    def late3(name):
        i = index[name]
        own = own_rows(name)
        for slot, (block, which) in enumerate(((ry, 0), (rx, 1), (rd, 0), (rd, 1))):
            take(W.at[own, part(block, which)], xyr.at[i, 2 + slot])
        for dz in range(1, nz):
            remote(W.at[own, :], W.at[own, :], ls.at[i], lr.at[i], (d, lax.rem(z + dz, nz)))

    def half(name, which):
        n = (nz // 2) * count(name)
        return pl.ds(base(name) + which * n, n)

    def xy1(name):
        i = index[name]
        take(W.at[pl.ds(base(name), nz * count(name)), lanes(r)], zr.at[i])
        a = W.at[half(name, 0), lanes(r)]
        b = W.at[half(name, 1), lanes(r)]
        remote(a, a, xys.at[i], xyr.at[i, 0], (xp, z))
        remote(b, b, xys.at[i], xyr.at[i, 1], (yp, z))
        remote(a, a, xys.at[i], xyr.at[i, 2], (yp, z))
        remote(b, b, xys.at[i], xyr.at[i, 3], (xp, z))

    def xy2(name):
        i = index[name]
        a = W.at[half(name, 0), lanes(rx)]
        b = W.at[half(name, 1), lanes(ry)]
        take(a, xyr.at[i, 0])
        remote(a, a, xys.at[i], xyr.at[i, 4], (yp, z))
        take(b, xyr.at[i, 1])
        remote(b, b, xys.at[i], xyr.at[i, 5], (xp, z))

    def ready(name):
        i = index[name]
        if name in p.late:
            take(W.at[pl.ds(0, (nz - 1) * count(name)), :], lr.at[i])
            return
        take(W.at[half(name, 0), lanes(ry)], xyr.at[i, 2])
        take(W.at[half(name, 1), lanes(rx)], xyr.at[i, 3])
        take(W.at[half(name, 0), lanes(rd)], xyr.at[i, 4])
        take(W.at[half(name, 1), lanes(rd)], xyr.at[i, 5])

    def sent(name):
        i = index[name]
        n = count(name)
        if name in p.late:
            take(R3.at[0, pl.ds(0, n), :], zs.at[i])
            take(R3.at[pl.ds(0, 6), pl.ds(0, n), :], xys.at[i])
            take(W.at[pl.ds(0, (nz - 1) * n), :], ls.at[i])
            return
        take(R3.at[pl.ds(0, 2 * nz - 1), pl.ds(0, n), :], zs.at[i])
        take(W.at[pl.ds(0, 6 * (nz // 2) * n * B // D), :], xys.at[i])

    place = {"n": (Gn, 0), "o": (W, base("a0") + nz * 3 * U)}
    for j in range(p.heads):
        place[f"q{j}"] = (W, base("a0") + j * nz * 3 * HD)
    for i in range(cuts):
        place[f"a{i}"] = (W, base("d0") + i * nz * M)
        place[f"b{i}"] = (Gb, i * nz * M)
        place[f"d{i}"] = (Gd, i * nz * M)

    def ghalf(name, which):
        n = (nz // 2) * count(name)
        return pl.ds(place[name][1] + which * n, n)

    def rhalf(name):
        return pl.ds((nz // 2) * p.pieces[name][0], (nz // 2) * count(name))

    def step_of(n):
        for s in (128, 112, 96, 80, 64, 48, 32, 16):
            if n % s == 0:
                return s
        return n

    def rs1(name):
        i = index[name]
        G = place[name][0]
        to = rhalf(name)
        for which, near, dev in ((0, ry, yp), (1, rx, xp)):
            rows = ghalf(name, which)
            remote(G.at[rows, lanes(rd)], R1.at[which, 0, to, :], r1s.at[i], r1r.at[i, which, 0], (dev, z))
        for which, near, dev in ((0, ry, yp), (1, rx, xp)):
            rows = ghalf(name, which)
            remote(G.at[rows, lanes(near)], R1.at[which, 1, to, :], r1s.at[i], r1r.at[i, which, 1], (dev, z))

    def rs2(name):
        i = index[name]
        G, gb = place[name]
        n = (nz // 2) * count(name)
        to = rhalf(name)
        s = step_of(n)
        for which, block, dev in ((0, rx, xp), (1, ry, yp)):
            take(R1.at[which, 0, to, :], r1r.at[i, which, 0])

            def add(t, _):
                g = rows_at(gb + which * n + t * s, s)
                q = rows_at(to.start + t * s, s)
                G[g, lanes(block)] = (G[g, lanes(block)].astype(F32) + R1[which, 0, q, :].astype(F32)).astype(BF)
                return 0

            lax.fori_loop(0, n // s, add, 0)
            remote(
                G.at[ghalf(name, which), lanes(block)],
                R2.at[which, to, :],
                r2s.at[i],
                r2r.at[i, which],
                (dev, z),
            )

    def rs3(name):
        i = index[name]
        G, gb = place[name]
        off, m = p.pieces[name]
        n = (nz // 2) * m
        to = rhalf(name)
        s = step_of(n)
        for which in range(2):
            take(R1.at[which, 1, to, :], r1r.at[i, which, 1])
            take(R2.at[which, to, :], r2r.at[i, which])

            def add(t, _):
                g = rows_at(gb + which * n + t * s, s)
                q = rows_at(to.start + t * s, s)
                total = G[g, lanes(r)].astype(F32) + R1[which, 1, q, :].astype(F32) + R2[which, q, :].astype(F32)
                G[g, lanes(r)] = total.astype(BF)
                return 0

            lax.fori_loop(0, n // s, add, 0)
        dst = R3.at[z * 2 + c, pl.ds(off, m), :]
        for dz in range(nz):
            there = lax.rem(z + dz, nz)
            for kk in range(2):
                k = lax.rem(c + kk, 2)
                src = G.at[rows_at(gb + there * m, m), pl.ds(pl.multiple_of(r * B + k * L, L), L)]
                if dz == 0 and kk == 0:
                    pltpu.make_async_copy(src, dst, r3r.at[i]).start()
                else:
                    remote(src, dst, r3s.at[i], r3r.at[i], (d if kk == 0 else sib, there))

    def rs4(name):
        i = index[name]
        off, m = p.pieces[name]
        take(R3.at[:, pl.ds(off, m), :], r3r.at[i])
        for k in range(2):
            total = R3[k, off : off + m, :].astype(F32)
            for j in range(1, nz):
                total += R3[2 * j + k, off : off + m, :].astype(F32)
            stage[k, off : off + m, :] = total
        if name == "n":
            stage[0, off : off + m, :] += stage[1, off : off + m, :]
        if name[0] != "q":
            store(name)

    def store(name):
        for j, (src, dst) in enumerate(stores(name)):
            pltpu.make_async_copy(src, dst, gs.at[index[name], j]).start()

    def early1(name):
        i = index[name]
        G, gb = place[name]
        n = count(name)
        at = p.early.index(name) * n
        for dz in range(1, nz):
            there = lax.rem(z + dz, nz)
            src = G.at[rows_at(gb + there * n, n), :]
            remote(src, RZ.at[dz - 1, pl.ds(at, n), :], es.at[i], er.at[i], (d, there))

    def early2(name):
        i = index[name]
        G, gb = place[name]
        off, n = p.pieces[name]
        at = p.early.index(name) * n
        take(RZ.at[:, pl.ds(at, n), :], er.at[i])

        def add(t, _):
            g = rows_at(gb + z * n + t * 16, 16)
            q = rows_at(at + t * 16, 16)
            total = G[g, :].astype(F32)
            for j in range(nz - 1):
                total += RZ[j, q, :].astype(F32)
            G[g, :] = total.astype(BF)
            return 0

        lax.fori_loop(0, n // 16, add, 0)
        own = rows_at(gb + z * n, n)
        to = pl.ds(off, n)
        for slot, (block, which, dev) in enumerate(((rd, 0, yp), (ry, 0, yp), (rd, 1, xp), (rx, 1, xp))):
            remote(
                G.at[own, part(block, which)],
                R3.at[slot, to, :],
                r1s.at[i],
                r1r.at[i, which, slot % 2],
                (dev, z),
            )

    def early3(name):
        i = index[name]
        G, gb = place[name]
        off, n = p.pieces[name]
        own, to = rows_at(gb + z * n, n), pl.ds(off, n)
        for which, block, dev in ((0, rx, xp), (1, ry, yp)):
            take(R3.at[2 * which, to, :], r1r.at[i, which, 0])
            there = part(block, which)
            G[own, there] = (G[own, there].astype(F32) + R3[2 * which, to, :].astype(F32)).astype(BF)
            remote(G.at[own, there], R3.at[4 + which, to, :], r2s.at[i], r2r.at[i, which], (dev, z))

    def early4(name):
        i = index[name]
        G, gb = place[name]
        off, n = p.pieces[name]
        own, to = rows_at(gb + z * n, n), pl.ds(off, n)
        for which in range(2):
            take(R3.at[2 * which + 1, to, :], r1r.at[i, which, 1])
            take(R3.at[4 + which, to, :], r2r.at[i, which])
            total = G[own, part(r, which)].astype(F32) + R3[2 * which + 1, to, :].astype(F32)
            total += R3[4 + which, to, :].astype(F32)

            @pl.when(c == which)
            def _():
                stage[which, to, :] = total

            @pl.when(c != which)
            def _():
                R3[7, to, :] = total.astype(BF)

        remote(R3.at[7, to, :], R3.at[6, to, :], r3s.at[i], r3r.at[i], (sib, z))

    def early5(name):
        i = index[name]
        off, n = p.pieces[name]
        to = pl.ds(off, n)
        take(R3.at[6, to, :], r3r.at[i])
        for k in range(2):

            @pl.when(c != k)
            def _():
                stage[k, to, :] = R3[6, to, :].astype(F32)

        store(name)

    def stores(name):
        off, m = p.pieces[name]
        kind, j = name[0], int(name[1:] or 0)
        if kind == "n":
            return [(stage.at[0, pl.ds(off, m), :], g_n_hbm)]
        if kind == "q":
            return [(g_q, g_q_hbm)] if j == p.heads - 1 else []
        pairs = []
        for k in range(2):
            n = m
            if kind == "o":
                dst, at = g_o_hbm, k * U
            else:
                at = k * H + j * M
                n = min(m, p.real - at)
                dst = g_d_hbm if kind == "d" else g_ab_hbm.at[0 if kind == "a" else 1]
            if n > 0:
                pairs.append((stage.at[k, pl.ds(off, n), :], dst.at[pl.ds(at, n), :]))
        return pairs

    def stored(name):
        for j, (src, dst) in enumerate(stores(name)):
            take(dst, gs.at[index[name], j])

    def rs_sent(name):
        i = index[name]
        m = count(name)
        if name in p.early:
            take(W.at[pl.ds(0, (nz - 1) * m), :], es.at[i])
            take(R3.at[pl.ds(0, 4), pl.ds(0, m), :], r1s.at[i])
            take(R3.at[pl.ds(0, 2), pl.ds(0, m), :], r2s.at[i])
            take(R3.at[0, pl.ds(0, m), :], r3s.at[i])
            return
        n = (nz // 2) * m
        take(W.at[pl.ds(0, 4 * n * B // D), :], r1s.at[i])
        take(W.at[pl.ds(0, 2 * n * B // D), :], r2s.at[i])
        take(R3.at[pl.ds(0, 2 * nz - 1), pl.ds(0, m), :], r3s.at[i])

    def swap(src, dst_here, dst_there, i):
        @pl.when(stay)
        def _():
            pltpu.make_async_copy(src, dst_here, swr.at[i]).start()

        @pl.when(jnp.logical_not(stay))
        def _():
            remote(src, dst_there, sws.at[i], swr.at[i], (sib, zpair))

    def swap_sent(src, i):
        @pl.when(jnp.logical_not(stay))
        def _():
            take(src, sws.at[i])

    def give(src, dst, i):
        remote(src, dst, cs.at[i], cr.at[i], (sib, z))

    def give_rows(buf, i):
        give(buf.at[mine, :], buf.at[mine, :], i)

    def got_rows(buf, i):
        take(buf.at[mine, :], cr.at[i])

    NB = 64

    order = [name for name in p.order if name not in p.late]
    steps = iter(range(len(order) + 1))

    def pump():
        k = next(steps)
        if k < len(order):
            xy1(order[k])
        if k + 3 < len(order):
            z_start(order[k + 3])
        if 0 < k:
            xy2(order[k - 1])

    for name in p.late:
        late0(name)
    for name in order[:3]:
        z_start(name)
    for name in p.late:
        late1(name)
    swap(x_hbm, xown, xown, 0)
    cos_ref, sin_ref = rope.at[0], rope.at[1]
    pump()
    pump()
    for name in p.late:
        late2(name)
    ready("n")
    take(xown, swr.at[0])

    gain_one = W[0:16, :][0:1, :].astype(F32)
    gain_two = W[0:16, :][1:2, :].astype(F32)

    def norm_parts(v):
        mean = jnp.mean(v, axis=1, keepdims=True)
        cen = v - mean
        inv = lax.rsqrt(jnp.mean(cen * cen, axis=1, keepdims=True) + EPS)
        return cen, inv

    def norm_first(t, _):
        own = rows_at(t * NB, NB)
        cen, inv = norm_parts(xown[own, :].astype(F32))
        n1[rows_at(c * T + t * NB, NB), :] = (cen * inv * gain_one).astype(BF)
        return 0

    pump()
    lax.fori_loop(0, T // NB, norm_first, 0)
    give_rows(n1, 0)
    for j in range(p.heads):
        pump()
    swap(dy_hbm, dyf.at[mine, :], dyf.at[rows_at(theirs_start, T), :], 1)
    got_rows(n1, 0)

    TB = 256
    QR = nz * 3 * HD

    def project(t, _):
        j, ti = t // (S // TB), lax.rem(t, S // TB)
        cols = pl.ds(pl.multiple_of(ti * TB, TB), TB)
        acc = dg(W[rows_at(base("q0") + j * QR, QR), :], n1[cols, :], 1, 1)
        co, si = cos_ref[:, cols], sin_ref[:, cols]
        for zi in range(nz):
            parts = []
            for part in range(2):
                at = (zi * 3 + part) * HD
                v1, v2 = acc[at : at + HD // 2], acc[at + HD // 2 : at + HD]
                w1, w2 = v1 * co - v2 * si, v2 * co + v1 * si
                if part == 0:
                    w1, w2 = w1 * HD**-0.5, w2 * HD**-0.5
                parts += [w1, w2]
            parts.append(acc[(zi * 3 + 2) * HD : (zi * 3 + 3) * HD])
            qkv[rows_at(j * QR + zi * 3 * HD, 3 * HD), cols] = jnp.concatenate(parts, axis=0).astype(BF)
        return 0

    QB = 256

    def head_rows(t):
        q, k, v = (rows_at((t * 3 + part) * HD, HD) for part in range(3))
        return q, k, v, rows_at(lax.rem(t, nz) * U + t // nz * HD, HD)

    def attend(t, _):
        q_rows, k_rows, v_rows, o_rows = head_rows(t)
        key = qkv[k_rows, :].T
        val = qkv[v_rows, :]

        def block(b, _):
            cols = pl.ds(pl.multiple_of(b * QB, QB), QB)
            s = dg(key, qkv[q_rows, cols], 1, 0)
            m = jnp.max(s, axis=0, keepdims=True)
            e = jnp.exp(s - m)
            l = jnp.sum(e, axis=0, keepdims=True)
            o = dg(val, e.astype(BF), 1, 0)
            att[o_rows, cols] = (o / l).astype(BF)
            lse[t, :, cols] = m + jnp.log(l)
            return 0

        lax.fori_loop(0, S // QB, block, 0)
        return 0

    for j in range(p.heads):
        ready(f"q{j}")
        lax.fori_loop(j * (S // TB), (j + 1) * (S // TB), project, 0)
    pump()
    NH = nz * p.heads
    late = iter(p.late)
    for t in range(0, NH, 2):
        lax.fori_loop(t, t + 2, attend, 0)
        pump()
        for name in late:
            late3(name)
            break
    ready("o")

    MB = 256

    def partial(lhs_rows, rhs, start):
        cols = pl.ds(pl.multiple_of(start, MB), MB)
        total = None
        for lhs, w in zip(lhs_rows, rhs):
            term = dg(lhs(cols), w[...], 0, 0)
            total = term if total is None else total + term
        return total

    def send_partial(lhs_rows, rhs, slot, there, i):
        def some(t, _):
            exs[slot, rows_at(t * MB, MB), :] = partial(lhs_rows, rhs, theirs_start + t * MB).astype(BF)
            return 0

        lax.fori_loop(0, T // MB, some, 0)
        give(exs.at[slot], exr.at[there], i)

    full_o = W.at[pl.ds(base("o"), nz * U), :]
    full_q = W.at[pl.ds(base("q0"), nz * 3 * U), :]
    full_a = W.at[pl.ds(base("a0"), nz * H), :]
    full_b = W.at[pl.ds(base("b0"), nz * H), :]
    full_d = W.at[pl.ds(base("d0"), nz * H), :]

    lhs_att = [lambda cols: att[:, cols]]
    send_partial(lhs_att, [full_o], 0, 0, 2)

    def residual(t, _):
        own = rows_at(t * MB, MB)
        res[own, :] = xown[own, :].astype(F32) + partial(lhs_att, [full_o], c * T + t * MB)
        return 0

    lax.fori_loop(0, T // MB, residual, 0)
    take(exr.at[0], cr.at[2])

    def norm_second(t, _):
        own = rows_at(t * NB, NB)
        v = res[own, :] + exr[0, own, :].astype(F32)
        res[own, :] = v
        cen, inv = norm_parts(v)
        n2[rows_at(c * T + t * NB, NB), :] = (cen * inv * gain_two).astype(BF)
        return 0

    lax.fori_loop(0, T // NB, norm_second, 0)
    give_rows(n2, 3)
    take(dyf.at[mine, :], swr.at[1])
    give_rows(dyf, 1)
    pump()
    got_rows(n2, 3)

    HB = nz * M

    def hidden(t, _):
        i, ti = t // (S // TB), lax.rem(t, S // TB)
        cols = pl.ds(pl.multiple_of(ti * TB, TB), TB)
        rows = rows_at(i * HB, HB)
        normed = n2[cols, :]
        act = dg(W[rows_at(base("a0") + i * HB, HB), :], normed, 1, 1)
        gate = dg(W[rows_at(base("b0") + i * HB, HB), :], normed, 1, 1)
        cdf = 0.5 + 0.5 * lax.erf(act * 0.7071067811865476)
        gelu = act * cdf
        slope = cdf + act * (jnp.exp(-0.5 * act * act) * 0.3989422804014327)
        hid[rows, cols] = (gelu * gate).astype(BF)
        AB[0, rows, cols] = (slope * gate).astype(BF)
        AB[1, rows, cols] = gelu.astype(BF)
        return 0

    ds = [f"d{i}" for i in range(cuts) if f"d{i}" not in p.early]
    ab = [f"{m}{i}" for m in "ba" for i in range(cuts)]
    turn = ds + ab + ["o"] + [f"q{j}" for j in range(p.heads)] + ["n"]
    turns = iter(range(len(turn) + 2))

    def sum_next(count=1):
        for _ in range(count):
            k = next(turns)
            if k < len(turn):
                rs1(turn[k])
            if 0 < k <= len(turn):
                rs2(turn[k - 1])
            if 1 < k:
                rs3(turn[k - 2])

    def grad_of(name, lhs, rhs):
        dest, at = place[name]
        dest[pl.ds(at, nz * p.pieces[name][1]), :] = dg(lhs, rhs[...], 1, 0).astype(BF)

    for i in range(cuts):
        ready(f"a{i}")
        ready(f"b{i}")
        lax.fori_loop(i * (S // TB), (i + 1) * (S // TB), hidden, 0)
        if i == 0:
            got_rows(dyf, 1)
        grad_of(f"d{i}", hid[i * HB : (i + 1) * HB, :], dyf)
        if f"d{i}" in p.early:
            early1(f"d{i}")
        else:
            sum_next()
        if i < 2:
            pump()
    for _ in steps:
        raise ValueError("steps left")

    def back_hidden(t, _):
        i, ti = t // (S // TB), lax.rem(t, S // TB)
        cols = pl.ds(pl.multiple_of(ti * TB, TB), TB)
        rows = rows_at(i * HB, HB)
        g = dg(W[rows_at(base("d0") + i * HB, HB), :], dyf[cols, :], 1, 1)
        AB[0, rows, cols] = (g * AB[0, rows, cols].astype(F32)).astype(BF)
        AB[1, rows, cols] = (g * AB[1, rows, cols].astype(F32)).astype(BF)
        return 0

    for i in range(cuts):
        ready(f"d{i}")
        lax.fori_loop(i * (S // TB), (i + 1) * (S // TB), back_hidden, 0)
        grad_of(f"b{i}", AB[1, i * HB : (i + 1) * HB, :], n2)
        if i == 0:
            sum_next()

    lhs_hid = [lambda cols: hid[:, cols]]
    lhs_gp = [lambda cols: AB[0, :, cols], lambda cols: AB[1, :, cols]]
    take(exs.at[0], cs.at[2])
    send_partial(lhs_hid, [full_d], 0, 0, 4)
    send_partial(lhs_gp, [full_a, full_b], 1, 1, 5)
    sum_next()
    take(exr.at[0], cr.at[4])
    take(exs.at[0], cs.at[4])

    def output(t, _):
        own = rows_at(t * MB, MB)
        total = partial(lhs_hid, [full_d], c * T + t * MB)
        xs = res[own, :] + (total + exr[0, own, :].astype(F32))
        exs[0, own, :] = xs.astype(BF)
        return 0

    lax.fori_loop(0, T // MB, output, 0)
    swap(exs.at[0], out_hbm, out_hbm, 2)

    for i in range(cuts):
        sent(f"d{i}")
    for i in range(cuts):
        grad_of(f"a{i}", AB[0, i * HB : (i + 1) * HB, :], n2)
    sum_next()
    take(exr.at[1], cr.at[5])

    def grad_residual(t, carry):
        own = rows_at(t * MB, MB)
        total = partial(lhs_gp, [full_a, full_b], c * T + t * MB) + exr[1, own, :].astype(F32)
        v = res[own, :]
        cen, inv = norm_parts(v)
        hat = cen * inv
        carry = carry + jnp.sum(total * hat, axis=0, keepdims=True)
        dh = total * gain_two
        back = inv * (
            dh - jnp.mean(dh, axis=1, keepdims=True) - hat * jnp.mean(dh * hat, axis=1, keepdims=True)
        )
        g = dyf[rows_at(c * T + t * MB, MB), :].astype(F32) + back
        res[own, :] = g
        dyf[rows_at(c * T + t * MB, MB), :] = g.astype(BF)
        return carry

    take(dyf.at[mine, :], cs.at[1])
    gain_two_grad = lax.fori_loop(0, T // MB, grad_residual, jnp.zeros((1, D), F32))
    give_rows(dyf, 6)
    sum_next()
    for name in p.early:
        early2(name)
    got_rows(dyf, 6)

    sent("o")
    for i in range(cuts):
        sent(f"a{i}")
        sent(f"b{i}")

    def grad_att(t, _):
        rows = rows_at(t * U, U)
        gat[rows, :] = dg(W[rows_at(base("o") + t * U, U), :], dyf[...], 1, 1).astype(BF)
        return 0

    lax.fori_loop(0, nz, grad_att, 0)
    grad_of("o", att[...], dyf)
    sum_next()
    for name in p.early:
        early3(name)

    def attend_back(t, _):
        q_rows, k_rows, v_rows, o_rows = head_rows(t)
        keyT = qkv[k_rows, :]
        key = keyT.T
        val = qkv[v_rows, :].T

        def block(b, carry):
            dk, dv = carry
            cols = pl.ds(pl.multiple_of(b * QB, QB), QB)
            q = qkv[q_rows, cols]
            g = gat[o_rows, cols]
            inner = jnp.sum(g.astype(F32) * att[o_rows, cols].astype(F32), axis=0, keepdims=True)
            prob = jnp.exp(dg(key, q, 1, 0) - lse[t, :, cols])
            dprob = dg(val, g, 1, 0)
            ds = (prob * (dprob - inner)).astype(BF)
            dv = dv + dg(g, prob.astype(BF), 1, 1)
            dk = dk + dg(q, ds, 1, 1)
            dq = dg(keyT, ds, 1, 0) * HD**-0.5
            co, si = cos_ref[:, cols], sin_ref[:, cols]
            g1, g2 = dq[: HD // 2], dq[HD // 2 :]
            qkv[q_rows, cols] = jnp.concatenate([g1 * co + g2 * si, g2 * co - g1 * si], axis=0).astype(BF)
            return dk, dv

        zero = jnp.zeros((HD, S), F32)
        dk, dv = lax.fori_loop(0, S // QB, block, (zero, zero))
        g1, g2 = dk[: HD // 2], dk[HD // 2 :]
        co, si = cos_ref[...], sin_ref[...]
        qkv[k_rows, :] = jnp.concatenate([g1 * co + g2 * si, g2 * co - g1 * si], axis=0).astype(BF)
        qkv[v_rows, :] = dv.astype(BF)
        return 0

    for t in range(0, NH, 2):
        lax.fori_loop(t, t + 2, attend_back, 0)
        if (t + 2) % nz == 0:
            j = t // nz
            grad_of(f"q{j}", qkv[j * QR : (j + 1) * QR, :], n1)
        sum_next()
        if t == 0:
            for name in p.early:
                early4(name)

    lhs_proj = [lambda cols: qkv[:, cols]]
    take(exs.at[1], cs.at[5])
    send_partial(lhs_proj, [full_q], 1, 0, 7)
    swap_sent(exs.at[0], 2)
    take(out_hbm, swr.at[2])
    take(exr.at[0], cr.at[7])

    def grad_input(t, carry):
        own = rows_at(t * MB, MB)
        total = partial(lhs_proj, [full_q], c * T + t * MB) + exr[0, own, :].astype(F32)
        cen, inv = norm_parts(xown[own, :].astype(F32))
        hat = cen * inv
        carry = carry + jnp.sum(total * hat, axis=0, keepdims=True)
        dh = total * gain_one
        back = inv * (
            dh - jnp.mean(dh, axis=1, keepdims=True) - hat * jnp.mean(dh * hat, axis=1, keepdims=True)
        )
        exs[0, own, :] = (res[own, :] + back).astype(BF)
        return carry

    gain_one_grad = lax.fori_loop(0, T // MB, grad_input, jnp.zeros((1, D), F32))
    swap(exs.at[0], gtok_hbm, gtok_hbm, 3)
    line = lax.broadcasted_iota(jnp.int32, (16, D), 0)
    both = jnp.where(line == 0, gain_one_grad, jnp.where(line == 1, gain_two_grad, 0.0)).astype(BF)
    for j in range(nz):
        Gn[16 * j : 16 * j + 16, :] = both
    sum_next(3)
    for _ in turns:
        raise ValueError("turns left")
    for name in p.early:
        early5(name)
    for name in turn:
        rs4(name)
    for part in range(3):
        for k in range(2):
            firsts = [p.pieces[f"q{j}"][0] + part * HD for j in range(p.heads)]
            g_q[part, :, k * U : (k + 1) * U] = jnp.concatenate(
                [stage[k, at : at + HD, :] for at in firsts], axis=0
            ).T
    store(f"q{p.heads - 1}")

    sent("n")
    for j in range(p.heads):
        sent(f"q{j}")
    for name in p.order:
        rs_sent(name)
    swap_sent(x_hbm, 0)
    swap_sent(dy_hbm, 1)
    swap_sent(exs.at[0], 3)
    take(gtok_hbm, swr.at[3])
    take(n1.at[mine, :], cs.at[0])
    take(n2.at[mine, :], cs.at[3])
    take(dyf.at[mine, :], cs.at[6])
    take(exs.at[1], cs.at[7])
    for name in p.order:
        stored(name)


def layer(plan, x, dy, gain_a, gain_m, w_o, w_q, w_ab, w_d, rope):
    p = plan
    nz, D, T, U, H = p.nz, p.width, p.tokens, p.units, p.hid
    S, L = 2 * T, p.lane
    n = len(p.order)
    hbm = pl.BlockSpec(memory_space=pl.ANY)
    dma = pltpu.SemaphoreType.DMA
    scratch = [
        pltpu.VMEM((nz * p.rows, D), BF),
        pltpu.VMEM((T, D), BF),
        pltpu.VMEM((S, D), BF),
        pltpu.VMEM((S, D), BF),
        pltpu.VMEM((nz * 3 * U, S), BF),
        pltpu.VMEM((nz * U, S), BF),
        pltpu.VMEM((nz * p.heads, 1, S), F32),
        pltpu.VMEM((T, D), F32),
        pltpu.VMEM((S, D), BF),
        pltpu.VMEM((2, nz * H, S), BF),
        pltpu.VMEM((nz * H, S), BF),
        pltpu.VMEM((nz * U, S), BF),
        pltpu.VMEM((2, T, D), BF),
        pltpu.VMEM((2, T, D), BF),
        pltpu.VMEM((nz * 16, D), BF),
        pltpu.VMEM((nz * H, D), BF),
        pltpu.VMEM((nz * H, D), BF),
        pltpu.VMEM((2, 2, (nz // 2) * p.rows, p.block), BF),
        pltpu.VMEM((2, (nz // 2) * p.rows, p.block), BF),
        pltpu.VMEM((2 * nz, p.rows, p.lane), BF),
        pltpu.VMEM((nz - 1, max(len(p.early), 1) * p.sub, D), BF),
        pltpu.VMEM((2, HD // 2, S), F32),
        pltpu.VMEM((2, p.rows, L), F32),
        pltpu.VMEM((2, 1, L), BF),
        pltpu.VMEM((16, L), BF),
        pltpu.VMEM((3, L, 2 * U), BF),
        pltpu.VMEM((6 * U, L), BF),
        pltpu.VMEM((2, 2 * H, L), BF),
        pltpu.VMEM((2 * H, L), BF),
        pltpu.VMEM((3, L, 2 * U), F32),
        dma((n,)),
        dma((n,)),
        dma((n, 6)),
        dma((n,)),
        dma((n, 2, 2)),
        dma((n,)),
        dma((n, 2)),
        dma((n,)),
        dma((n,)),
        dma((n,)),
        dma((4,)),
        dma((4,)),
        dma((8,)),
        dma((8,)),
        dma((n, 2)),
        dma((n,)),
        dma((n,)),
        dma((n,)),
        dma((n,)),
        dma((7,)),
    ]
    return pl.pallas_call(
        functools.partial(kernel, p),
        out_shape=(
            jax.ShapeDtypeStruct((T, D), BF),
            jax.ShapeDtypeStruct((T, D), BF),
            jax.ShapeDtypeStruct((16, L), F32),
            jax.ShapeDtypeStruct((2 * U, L), F32),
            jax.ShapeDtypeStruct((3, L, 2 * U), F32),
            jax.ShapeDtypeStruct((2, p.real, L), F32),
            jax.ShapeDtypeStruct((p.real, L), F32),
        ),
        in_specs=[hbm] * 9,
        out_specs=(hbm,) * 7,
        scratch_shapes=scratch,
        compiler_params=pltpu.CompilerParams(
            collective_id=0, has_side_effects=True, vmem_limit_bytes=VMEM
        ),
        name="layer",
    )(x, dy, gain_a, gain_m, w_o, w_q, w_ab, w_d, rope)


def settle_kernel(count, *refs):
    ins, outs, held = refs[:count], refs[count : 2 * count + 1], refs[2 * count + 1 : 3 * count + 1]
    load_sem, store_sem = refs[3 * count + 1 :]
    loads = [pltpu.make_async_copy(a, b, load_sem.at[i]) for i, (a, b) in enumerate(zip(ins, held))]
    for copy in loads:
        copy.start()
    sources = [[h] for h in held]
    sources[2] = [held[2].at[pl.ds(0, 1), :], held[2].at[pl.ds(1, 1), :]]
    stores = []
    for copy, parts in zip(loads, sources):
        copy.wait()
        for part in parts:
            store = pltpu.make_async_copy(part, outs[len(stores)], store_sem.at[len(stores)])
            store.start()
            stores.append(store)
    for store in stores:
        store.wait()


def settle(out, gtok, g_n, *rest):
    arrays = (out, gtok, g_n) + rest
    row = jax.ShapeDtypeStruct((1, g_n.shape[1]), F32)
    like = [jax.ShapeDtypeStruct(a.shape, a.dtype) for a in arrays]
    shapes = (*like[:2], row, row, *like[3:])
    hbm = pl.BlockSpec(memory_space=pl.ANY)
    return pl.pallas_call(
        functools.partial(settle_kernel, len(arrays)),
        out_shape=shapes,
        in_specs=[hbm] * len(arrays),
        out_specs=(hbm,) * len(shapes),
        scratch_shapes=[pltpu.VMEM(a.shape, a.dtype) for a in arrays]
        + [pltpu.SemaphoreType.DMA((len(arrays),)), pltpu.SemaphoreType.DMA((len(shapes),))],
        compiler_params=pltpu.CompilerParams(vmem_limit_bytes=VMEM),
        name="settle",
    )(*arrays)


def rope_table():
    freq = THETA ** (-np.arange(HD // 2) * 2.0 / HD)
    angle = freq.astype(np.float32)[:, None] * np.arange(LEN, dtype=np.float32)[None, :]
    return np.stack([np.cos(angle), np.sin(angle)]).astype(np.float32)


def local(outer, nz, tokens, w_qkv, w_out, w_in, w_down, gain_attn, gain_mlp, grad_output):
    T, D = tokens.shape
    groups = [[hi * LOW + lo for hi in range(outer)] for lo in range(LOW)]
    piece = D // (outer * LOW)

    def widen(a, axis):
        if outer == 1:
            return a
        return lax.all_gather(a, "dp", axis=axis, tiled=True, axis_index_groups=groups)

    def narrow(a, axis):
        if outer == 1:
            return a
        return lax.psum_scatter(a, "dp", scatter_dimension=axis, tiled=True, axis_index_groups=groups)

    def turn(a, first, second):
        if outer == 1:
            return a
        return a.reshape(T, first, second, piece).swapaxes(1, 2).reshape(T, D)

    w_qkv, w_in = widen(w_qkv, 0), widen(w_in, 0)
    w_out, w_down = widen(w_out, 1), widen(w_down, 1)
    gains = [widen(g, 0) for g in (gain_attn, gain_mlp)]
    x = turn(tokens, outer, LOW)
    dy = turn(grad_output, outer, LOW)
    p = Plan(nz, D, T, w_qkv.shape[2], w_in.shape[2])
    L = p.lane
    rope = jnp.asarray(rope_table())
    results = layer(
        p,
        x,
        dy,
        gains[0].reshape(1, L),
        gains[1].reshape(1, L),
        w_out,
        w_qkv.transpose(1, 0, 2),
        w_in.transpose(1, 2, 0),
        w_down,
        rope,
    )
    out, gtok, g_a, g_m, g_out, g_q, g_ab, g_down = settle(*results)

    out, gtok = turn(out, LOW, outer), turn(gtok, LOW, outer)
    g_qkv = g_q.transpose(1, 0, 2)
    g_in = g_ab.transpose(2, 0, 1)
    return (
        out,
        gtok,
        narrow(g_qkv, 0),
        narrow(g_out, 1),
        narrow(g_in, 0),
        narrow(g_down, 1),
        narrow(g_a.reshape(L), 0),
        narrow(g_m.reshape(L), 0),
    )


def solution(mesh):
    rows = P(("dp", "tensor"), None)
    deep = P("dp", None, "tensor")
    wide = P("tensor", "dp")
    flat = P("dp")
    return jax.shard_map(
        functools.partial(local, mesh.shape["dp"] // LOW, mesh.shape["tensor"]),
        mesh=mesh,
        in_specs=(rows, deep, wide, deep, wide, flat, flat, rows),
        out_specs=(rows, rows, deep, wide, deep, wide, flat, flat),
        check_vma=False,
    )
```

```python
import functools

import jax
import jax.numpy as jnp
import numpy as np
from jax import lax
from jax.experimental import pallas as pl
from jax.experimental.pallas import tpu as pltpu
from jax.sharding import PartitionSpec as P

HD = 64
LEN = 1024
EPS = 1e-05
THETA = 160000.0
MESH = pl.DeviceIdType.MESH
BF = jnp.bfloat16
F32 = jnp.float32
VMEM = 64 * 1024 * 1024 - 65536
LOW = 8


def up(n, m):
    return -(-n // m) * m


def dg(a, b, ca, cb):
    return lax.dot_general(a, b, (((ca,), (cb,)), ((), ())), preferred_element_type=F32)


class Plan:
    def __init__(self, nz, width, tokens, units, hidden):
        self.nz, self.width, self.tokens = nz, width, tokens
        self.lane = width // LOW
        self.block = 2 * self.lane
        self.units = units // 2
        self.heads = self.units // HD
        self.real = hidden
        self.hid = up(-(-hidden // 2), 16)
        self.cuts = next(n for n in (3, 2, 1) if self.hid % (16 * n) == 0)
        self.sub = self.hid // self.cuts
        self.pieces = {}
        total = 0
        sizes = [("n", 16), ("o", self.units)]
        sizes += [(f"q{j}", 3 * HD) for j in range(self.heads)]
        sizes += [(f"{m}{i}", self.sub) for m in "abd" for i in range(self.cuts)]
        for name, rows in sizes:
            self.pieces[name] = (total, rows)
            total += rows
        self.rows = total
        self.order = ["n"] + [f"q{j}" for j in range(self.heads)] + ["o"]
        self.order += [f"{m}{i}" for i in range(self.cuts) for m in "ab"]
        self.order += [f"d{i}" for i in range(self.cuts)]
        self.late = self.order[-1:] if self.cuts > 1 else []
        self.early = [f"d{i}" for i in range(len(self.late))]


def kernel(
    plan,
    x_hbm,
    dy_hbm,
    gain_a_hbm,
    gain_m_hbm,
    w_o_hbm,
    w_q_hbm,
    w_ab_hbm,
    w_d_hbm,
    rope_hbm,
    out_hbm,
    gtok_hbm,
    g_n_hbm,
    g_o_hbm,
    g_q_hbm,
    g_ab_hbm,
    g_d_hbm,
    W,
    xown,
    dyf,
    n1,
    qkv,
    att,
    lse,
    res,
    n2,
    AB,
    hid,
    exs,
    exr,
    Gn,
    Gb,
    Gd,
    R1,
    R2,
    R3,
    RZ,
    rope,
    stage,
    gains,
    gain_rows,
    w_q_in,
    w_q,
    w_ab,
    w_d,
    g_q,
    zr,
    zs,
    xyr,
    xys,
    r1r,
    r1s,
    r2r,
    r2s,
    r3r,
    r3s,
    swr,
    sws,
    cr,
    cs,
    gs,
    lr,
    ls,
    er,
    es,
    ins,
):
    p = plan
    nz, D, T, U, H = p.nz, p.width, p.tokens, p.units, p.hid
    S = 2 * T
    L, B = p.lane, p.block
    d = lax.axis_index("dp")
    z = lax.axis_index("tensor")
    c = lax.rem(d, 2)
    r = lax.rem(d // 2, 4)
    xb = lax.rem(r, 2)
    yb = r // 2
    zb = lax.rem(z, 2)
    sib = d + 1 - 2 * c
    xp = d + 2 - 4 * xb
    yp = d + 4 - 8 * yb
    zpair = z + 1 - 2 * zb
    rx = r + 1 - 2 * xb
    ry = r + 2 - 4 * yb
    rd = 3 - r
    stay = lax.rem(c + z, 2) == 0

    def rows_at(start, n):
        return pl.ds(pl.multiple_of(start, 16), n)

    def lanes(block):
        return pl.ds(pl.multiple_of(block * B, L), B)

    mine = rows_at(c * T, T)
    theirs_start = (1 - c) * T

    def remote(src, dst, ssem, rsem, dev):
        pltpu.make_async_remote_copy(src, dst, ssem, rsem, device_id=dev, device_id_type=MESH).start()

    def take(ref, sem):
        pltpu.make_async_copy(ref, ref, sem).wait()

    partners = [(sib, z), (xp, z), (yp, z)]
    for dz in range(1, nz):
        there = lax.rem(z + dz, nz)
        partners += [(d, there), (sib, there)]
    bar = pltpu.get_barrier_semaphore()
    for dev in partners:
        pl.semaphore_signal(bar, inc=1, device_id=dev, device_id_type=MESH)

    def load(src, dst, i):
        return pltpu.make_async_copy(src, dst, ins.at[i])

    real = p.real
    loads = [
        load(gain_a_hbm, gains.at[0], 0),
        load(gain_m_hbm, gains.at[1], 1),
        load(w_q_hbm, w_q_in, 2),
        load(w_ab_hbm.at[0], w_ab.at[0, pl.ds(0, real), :], 3),
        load(w_ab_hbm.at[1], w_ab.at[1, pl.ds(0, real), :], 4),
        load(w_d_hbm, w_d.at[pl.ds(0, real), :], 5),
        load(rope_hbm, rope, 6),
    ]
    for copy in loads:
        copy.start()
    if 2 * H > real:
        zeros = jnp.zeros((2 * H - real, L), BF)
        w_ab[0, real:, :] = zeros
        w_ab[1, real:, :] = zeros
        w_d[real:, :] = zeros
    for copy in loads:
        copy.wait()
    line = lax.broadcasted_iota(jnp.int32, (16, L), 0)
    first, second = (gains[j, :, :].astype(F32) for j in range(2))
    gain_rows[...] = jnp.where(line == 0, first, jnp.where(line == 1, second, 0.0)).astype(BF)
    for part in range(3):
        turned = w_q_in[part, :, :].T
        for k in range(2):
            for j in range(p.heads):
                at = k * U + j * HD
                to = (k * p.heads + j) * 3 * HD + part * HD
                w_q[to : to + HD, :] = turned[at : at + HD, :]
    pl.semaphore_wait(bar, len(partners))

    index = {name: i for i, name in enumerate(p.pieces)}
    M, cuts = p.sub, p.cuts

    def shard(name, k):
        kind, j = name[0], int(name[1:] or 0)
        if kind == "n":
            return gain_rows
        if kind == "o":
            return w_o_hbm.at[rows_at(k * U, U), :]
        if kind == "q":
            return w_q.at[rows_at(k * 3 * U + j * 3 * HD, 3 * HD), :]
        if kind == "d":
            return w_d.at[rows_at(k * H + j * M, M), :]
        return w_ab.at[0 if kind == "a" else 1, rows_at(k * H + j * M, M), :]

    def base(name):
        return nz * p.pieces[name][0]

    def count(name):
        return p.pieces[name][1]

    def z_start(name):
        off, n = p.pieces[name]
        i = index[name]
        dst = W.at[rows_at(base(name) + z * n, n), pl.ds(pl.multiple_of(r * B + c * L, L), L)]
        for dz in range(nz):
            there = lax.rem(z + dz, nz)
            for kk in range(2):
                k = lax.rem(c + kk, 2)
                src = shard(name, k)
                if dz == 0 and kk == 0:
                    pltpu.make_async_copy(src, dst, zr.at[i]).start()
                else:
                    remote(src, dst, zs.at[i], zr.at[i], (d if kk == 0 else sib, there))

    def part(block, which):
        return pl.ds(pl.multiple_of(block * B + which * L, L), L)

    def own_rows(name):
        n = count(name)
        return rows_at(base(name) + z * n, n)

    def late0(name):
        i = index[name]
        dst = W.at[own_rows(name), part(r, c)]
        pltpu.make_async_copy(shard(name, c), dst, zr.at[i]).start()
        remote(shard(name, 1 - c), dst, zs.at[i], zr.at[i], (sib, z))

    def late1(name):
        i = index[name]
        own = own_rows(name)
        take(W.at[own, lanes(r)], zr.at[i])
        a = W.at[own, part(r, 0)]
        b = W.at[own, part(r, 1)]
        remote(a, a, xys.at[i], xyr.at[i, 0], (xp, z))
        remote(b, b, xys.at[i], xyr.at[i, 1], (yp, z))
        remote(a, a, xys.at[i], xyr.at[i, 2], (yp, z))
        remote(b, b, xys.at[i], xyr.at[i, 3], (xp, z))

    def late2(name):
        i = index[name]
        own = own_rows(name)
        a = W.at[own, part(rx, 0)]
        b = W.at[own, part(ry, 1)]
        take(a, xyr.at[i, 0])
        remote(a, a, xys.at[i], xyr.at[i, 4], (yp, z))
        take(b, xyr.at[i, 1])
        remote(b, b, xys.at[i], xyr.at[i, 5], (xp, z))

    def late3(name):
        i = index[name]
        own = own_rows(name)
        for slot, (block, which) in enumerate(((ry, 0), (rx, 1), (rd, 0), (rd, 1))):
            take(W.at[own, part(block, which)], xyr.at[i, 2 + slot])
        for dz in range(1, nz):
            remote(W.at[own, :], W.at[own, :], ls.at[i], lr.at[i], (d, lax.rem(z + dz, nz)))

    def half(name, which):
        n = (nz // 2) * count(name)
        return pl.ds(base(name) + which * n, n)

    def xy1(name):
        i = index[name]
        take(W.at[pl.ds(base(name), nz * count(name)), lanes(r)], zr.at[i])
        a = W.at[half(name, 0), lanes(r)]
        b = W.at[half(name, 1), lanes(r)]
        remote(a, a, xys.at[i], xyr.at[i, 0], (xp, z))
        remote(b, b, xys.at[i], xyr.at[i, 1], (yp, z))
        remote(a, a, xys.at[i], xyr.at[i, 2], (yp, z))
        remote(b, b, xys.at[i], xyr.at[i, 3], (xp, z))

    def xy2(name):
        i = index[name]
        a = W.at[half(name, 0), lanes(rx)]
        b = W.at[half(name, 1), lanes(ry)]
        take(a, xyr.at[i, 0])
        remote(a, a, xys.at[i], xyr.at[i, 4], (yp, z))
        take(b, xyr.at[i, 1])
        remote(b, b, xys.at[i], xyr.at[i, 5], (xp, z))

    def ready(name):
        i = index[name]
        if name in p.late:
            take(W.at[pl.ds(0, (nz - 1) * count(name)), :], lr.at[i])
            return
        take(W.at[half(name, 0), lanes(ry)], xyr.at[i, 2])
        take(W.at[half(name, 1), lanes(rx)], xyr.at[i, 3])
        take(W.at[half(name, 0), lanes(rd)], xyr.at[i, 4])
        take(W.at[half(name, 1), lanes(rd)], xyr.at[i, 5])

    def sent(name):
        i = index[name]
        n = count(name)
        if name in p.late:
            take(R3.at[0, pl.ds(0, n), :], zs.at[i])
            take(R3.at[pl.ds(0, 6), pl.ds(0, n), :], xys.at[i])
            take(W.at[pl.ds(0, (nz - 1) * n), :], ls.at[i])
            return
        take(R3.at[pl.ds(0, 2 * nz - 1), pl.ds(0, n), :], zs.at[i])
        take(W.at[pl.ds(0, 6 * (nz // 2) * n * B // D), :], xys.at[i])

    place = {"n": (Gn, 0), "o": (W, base("a0") + nz * 3 * U)}
    for j in range(p.heads):
        place[f"q{j}"] = (W, base("a0") + j * nz * 3 * HD)
    for i in range(cuts):
        place[f"a{i}"] = (W, base("d0") + i * nz * M)
        place[f"b{i}"] = (Gb, i * nz * M)
        place[f"d{i}"] = (Gd, i * nz * M)

    def ghalf(name, which):
        n = (nz // 2) * count(name)
        return pl.ds(place[name][1] + which * n, n)

    def rhalf(name):
        return pl.ds((nz // 2) * p.pieces[name][0], (nz // 2) * count(name))

    def step_of(n):
        for s in (128, 112, 96, 80, 64, 48, 32, 16):
            if n % s == 0:
                return s
        return n

    def rs1(name):
        i = index[name]
        G = place[name][0]
        to = rhalf(name)
        for which, near, dev in ((0, ry, yp), (1, rx, xp)):
            rows = ghalf(name, which)
            remote(G.at[rows, lanes(rd)], R1.at[which, 0, to, :], r1s.at[i], r1r.at[i, which, 0], (dev, z))
        for which, near, dev in ((0, ry, yp), (1, rx, xp)):
            rows = ghalf(name, which)
            remote(G.at[rows, lanes(near)], R1.at[which, 1, to, :], r1s.at[i], r1r.at[i, which, 1], (dev, z))

    def rs2(name):
        i = index[name]
        G, gb = place[name]
        n = (nz // 2) * count(name)
        to = rhalf(name)
        s = step_of(n)
        for which, block, dev in ((0, rx, xp), (1, ry, yp)):
            take(R1.at[which, 0, to, :], r1r.at[i, which, 0])

            def add(t, _):
                g = rows_at(gb + which * n + t * s, s)
                q = rows_at(to.start + t * s, s)
                G[g, lanes(block)] = (G[g, lanes(block)].astype(F32) + R1[which, 0, q, :].astype(F32)).astype(BF)
                return 0

            lax.fori_loop(0, n // s, add, 0)
            remote(
                G.at[ghalf(name, which), lanes(block)],
                R2.at[which, to, :],
                r2s.at[i],
                r2r.at[i, which],
                (dev, z),
            )

    def rs3(name):
        i = index[name]
        G, gb = place[name]
        off, m = p.pieces[name]
        n = (nz // 2) * m
        to = rhalf(name)
        s = step_of(n)
        for which in range(2):
            take(R1.at[which, 1, to, :], r1r.at[i, which, 1])
            take(R2.at[which, to, :], r2r.at[i, which])

            def add(t, _):
                g = rows_at(gb + which * n + t * s, s)
                q = rows_at(to.start + t * s, s)
                total = G[g, lanes(r)].astype(F32) + R1[which, 1, q, :].astype(F32) + R2[which, q, :].astype(F32)
                G[g, lanes(r)] = total.astype(BF)
                return 0

            lax.fori_loop(0, n // s, add, 0)
        dst = R3.at[z * 2 + c, pl.ds(off, m), :]
        for dz in range(nz):
            there = lax.rem(z + dz, nz)
            for kk in range(2):
                k = lax.rem(c + kk, 2)
                src = G.at[rows_at(gb + there * m, m), pl.ds(pl.multiple_of(r * B + k * L, L), L)]
                if dz == 0 and kk == 0:
                    pltpu.make_async_copy(src, dst, r3r.at[i]).start()
                else:
                    remote(src, dst, r3s.at[i], r3r.at[i], (d if kk == 0 else sib, there))

    def rs4(name):
        i = index[name]
        off, m = p.pieces[name]
        take(R3.at[:, pl.ds(off, m), :], r3r.at[i])
        for k in range(2):
            total = R3[k, off : off + m, :].astype(F32)
            for j in range(1, nz):
                total += R3[2 * j + k, off : off + m, :].astype(F32)
            stage[k, off : off + m, :] = total
        if name == "n":
            stage[0, off : off + m, :] += stage[1, off : off + m, :]
        if name[0] != "q":
            store(name)

    def store(name):
        for j, (src, dst) in enumerate(stores(name)):
            pltpu.make_async_copy(src, dst, gs.at[index[name], j]).start()

    def early1(name):
        i = index[name]
        G, gb = place[name]
        n = count(name)
        at = p.early.index(name) * n
        for dz in range(1, nz):
            there = lax.rem(z + dz, nz)
            src = G.at[rows_at(gb + there * n, n), :]
            remote(src, RZ.at[dz - 1, pl.ds(at, n), :], es.at[i], er.at[i], (d, there))

    def early2(name):
        i = index[name]
        G, gb = place[name]
        off, n = p.pieces[name]
        at = p.early.index(name) * n
        take(RZ.at[:, pl.ds(at, n), :], er.at[i])

        def add(t, _):
            g = rows_at(gb + z * n + t * 16, 16)
            q = rows_at(at + t * 16, 16)
            total = G[g, :].astype(F32)
            for j in range(nz - 1):
                total += RZ[j, q, :].astype(F32)
            G[g, :] = total.astype(BF)
            return 0

        lax.fori_loop(0, n // 16, add, 0)
        own = rows_at(gb + z * n, n)
        to = pl.ds(off, n)
        for slot, (block, which, dev) in enumerate(((rd, 0, yp), (ry, 0, yp), (rd, 1, xp), (rx, 1, xp))):
            remote(
                G.at[own, part(block, which)],
                R3.at[slot, to, :],
                r1s.at[i],
                r1r.at[i, which, slot % 2],
                (dev, z),
            )

    def early3(name):
        i = index[name]
        G, gb = place[name]
        off, n = p.pieces[name]
        own, to = rows_at(gb + z * n, n), pl.ds(off, n)
        for which, block, dev in ((0, rx, xp), (1, ry, yp)):
            take(R3.at[2 * which, to, :], r1r.at[i, which, 0])
            there = part(block, which)
            G[own, there] = (G[own, there].astype(F32) + R3[2 * which, to, :].astype(F32)).astype(BF)
            remote(G.at[own, there], R3.at[4 + which, to, :], r2s.at[i], r2r.at[i, which], (dev, z))

    def early4(name):
        i = index[name]
        G, gb = place[name]
        off, n = p.pieces[name]
        own, to = rows_at(gb + z * n, n), pl.ds(off, n)
        for which in range(2):
            take(R3.at[2 * which + 1, to, :], r1r.at[i, which, 1])
            take(R3.at[4 + which, to, :], r2r.at[i, which])
            total = G[own, part(r, which)].astype(F32) + R3[2 * which + 1, to, :].astype(F32)
            total += R3[4 + which, to, :].astype(F32)

            @pl.when(c == which)
            def _():
                stage[which, to, :] = total

            @pl.when(c != which)
            def _():
                R3[7, to, :] = total.astype(BF)

        remote(R3.at[7, to, :], R3.at[6, to, :], r3s.at[i], r3r.at[i], (sib, z))

    def early5(name):
        i = index[name]
        off, n = p.pieces[name]
        to = pl.ds(off, n)
        take(R3.at[6, to, :], r3r.at[i])
        for k in range(2):

            @pl.when(c != k)
            def _():
                stage[k, to, :] = R3[6, to, :].astype(F32)

        store(name)

    def stores(name):
        off, m = p.pieces[name]
        kind, j = name[0], int(name[1:] or 0)
        if kind == "n":
            return [(stage.at[0, pl.ds(off, m), :], g_n_hbm)]
        if kind == "q":
            return [(g_q, g_q_hbm)] if j == p.heads - 1 else []
        pairs = []
        for k in range(2):
            n = m
            if kind == "o":
                dst, at = g_o_hbm, k * U
            else:
                at = k * H + j * M
                n = min(m, p.real - at)
                dst = g_d_hbm if kind == "d" else g_ab_hbm.at[0 if kind == "a" else 1]
            if n > 0:
                pairs.append((stage.at[k, pl.ds(off, n), :], dst.at[pl.ds(at, n), :]))
        return pairs

    def stored(name):
        for j, (src, dst) in enumerate(stores(name)):
            take(dst, gs.at[index[name], j])

    def rs_sent(name):
        i = index[name]
        m = count(name)
        if name in p.early:
            take(W.at[pl.ds(0, (nz - 1) * m), :], es.at[i])
            take(R3.at[pl.ds(0, 4), pl.ds(0, m), :], r1s.at[i])
            take(R3.at[pl.ds(0, 2), pl.ds(0, m), :], r2s.at[i])
            take(R3.at[0, pl.ds(0, m), :], r3s.at[i])
            return
        n = (nz // 2) * m
        take(W.at[pl.ds(0, 4 * n * B // D), :], r1s.at[i])
        take(W.at[pl.ds(0, 2 * n * B // D), :], r2s.at[i])
        take(R3.at[pl.ds(0, 2 * nz - 1), pl.ds(0, m), :], r3s.at[i])

    def swap(src, dst_here, dst_there, i):
        @pl.when(stay)
        def _():
            pltpu.make_async_copy(src, dst_here, swr.at[i]).start()

        @pl.when(jnp.logical_not(stay))
        def _():
            remote(src, dst_there, sws.at[i], swr.at[i], (sib, zpair))

    def swap_sent(src, i):
        @pl.when(jnp.logical_not(stay))
        def _():
            take(src, sws.at[i])

    def give(src, dst, i):
        remote(src, dst, cs.at[i], cr.at[i], (sib, z))

    def give_rows(buf, i):
        give(buf.at[mine, :], buf.at[mine, :], i)

    def got_rows(buf, i):
        take(buf.at[mine, :], cr.at[i])

    NB = 64

    order = [name for name in p.order if name not in p.late]
    steps = iter(range(len(order) + 1))
    waiting = iter(order)

    def z_some(count):
        for _, name in zip(range(count), waiting):
            z_start(name)

    def pump(ahead=1):
        k = next(steps)
        if 0 < k:
            xy2(order[k - 1])
        if k < len(order):
            xy1(order[k])
        z_some(ahead)

    for name in p.late:
        late0(name)
    z_some(2)
    for name in p.late:
        late1(name)
    swap(x_hbm, xown, xown, 0)
    cos_ref, sin_ref = rope.at[0], rope.at[1]
    pump(0)
    pump(1)
    for name in p.late:
        late2(name)
    ready("n")

    gain_one = W[0:16, :][0:1, :].astype(F32)
    gain_two = W[0:16, :][1:2, :].astype(F32)

    def norm_parts(v):
        mean = jnp.mean(v, axis=1, keepdims=True)
        cen = v - mean
        inv = lax.rsqrt(jnp.mean(cen * cen, axis=1, keepdims=True) + EPS)
        return cen, inv

    def norm_first(t, _):
        own = rows_at(t * NB, NB)
        cen, inv = norm_parts(xown[own, :].astype(F32))
        n1[rows_at(c * T + t * NB, NB), :] = (cen * inv * gain_one).astype(BF)
        return 0

    pump(2)
    take(xown, swr.at[0])
    lax.fori_loop(0, T // NB, norm_first, 0)
    give_rows(n1, 0)
    got_rows(n1, 0)

    TB = 512
    QR = nz * 3 * HD

    def project(t, _):
        j, ti = t // (S // TB), lax.rem(t, S // TB)
        cols = pl.ds(pl.multiple_of(ti * TB, TB), TB)
        acc = dg(W[rows_at(base("q0") + j * QR, QR), :], n1[cols, :], 1, 1)
        co, si = cos_ref[:, cols], sin_ref[:, cols]
        for zi in range(nz):
            parts = []
            for part in range(2):
                at = (zi * 3 + part) * HD
                v1, v2 = acc[at : at + HD // 2], acc[at + HD // 2 : at + HD]
                w1, w2 = v1 * co - v2 * si, v2 * co + v1 * si
                if part == 0:
                    w1, w2 = w1 * HD**-0.5, w2 * HD**-0.5
                parts += [w1, w2]
            parts.append(acc[(zi * 3 + 2) * HD : (zi * 3 + 3) * HD])
            qkv[rows_at(j * QR + zi * 3 * HD, 3 * HD), cols] = jnp.concatenate(parts, axis=0).astype(BF)
        return 0

    QB = 1024

    def head_rows(t):
        q, k, v = (rows_at((t * 3 + part) * HD, HD) for part in range(3))
        return q, k, v, rows_at(lax.rem(t, nz) * U + t // nz * HD, HD)

    def attend(t, _):
        q_rows, k_rows, v_rows, o_rows = head_rows(t)
        key = qkv[k_rows, :].T
        val = qkv[v_rows, :]

        def block(b, _):
            cols = pl.ds(pl.multiple_of(b * QB, QB), QB)
            s = dg(key, qkv[q_rows, cols], 1, 0)
            m = jnp.max(s, axis=0, keepdims=True)
            e = jnp.exp(s - m)
            l = jnp.sum(e, axis=0, keepdims=True)
            o = dg(val, e.astype(BF), 1, 0)
            att[o_rows, cols] = (o / l).astype(BF)
            lse[t, :, cols] = m + jnp.log(l)
            return 0

        lax.fori_loop(0, S // QB, block, 0)
        return 0

    NH = nz * p.heads
    late = iter(p.late)
    for t in range(0, NH, 2):
        if t % nz == 0:
            j = t // nz
            ready(f"q{j}")
            lax.fori_loop(j * (S // TB), (j + 1) * (S // TB), project, 0)
        pump(2 if t == 0 else 1)
        lax.fori_loop(t, t + 2, attend, 0)
        for name in late:
            swap(dy_hbm, dyf.at[mine, :], dyf.at[rows_at(theirs_start, T), :], 1)
            late3(name)
            break
    ready("o")

    MB = 256

    def partial(lhs_rows, rhs, start):
        cols = pl.ds(pl.multiple_of(start, MB), MB)
        total = None
        for lhs, w in zip(lhs_rows, rhs):
            term = dg(lhs(cols), w[...], 0, 0)
            total = term if total is None else total + term
        return total

    def send_partial(lhs_rows, rhs, slot, there, i):
        def some(t, _):
            exs[slot, rows_at(t * MB, MB), :] = partial(lhs_rows, rhs, theirs_start + t * MB).astype(BF)
            return 0

        lax.fori_loop(0, T // MB, some, 0)
        give(exs.at[slot], exr.at[there], i)

    full_o = W.at[pl.ds(base("o"), nz * U), :]
    full_q = W.at[pl.ds(base("q0"), nz * 3 * U), :]
    full_a = W.at[pl.ds(base("a0"), nz * H), :]
    full_b = W.at[pl.ds(base("b0"), nz * H), :]
    full_d = W.at[pl.ds(base("d0"), nz * H), :]

    lhs_att = [lambda cols: att[:, cols]]
    send_partial(lhs_att, [full_o], 0, 0, 2)

    def residual(t, _):
        own = rows_at(t * MB, MB)
        res[own, :] = xown[own, :].astype(F32) + partial(lhs_att, [full_o], c * T + t * MB)
        return 0

    lax.fori_loop(0, T // MB, residual, 0)
    pump()
    take(exr.at[0], cr.at[2])

    def norm_second(t, _):
        own = rows_at(t * NB, NB)
        v = res[own, :] + exr[0, own, :].astype(F32)
        res[own, :] = v
        cen, inv = norm_parts(v)
        n2[rows_at(c * T + t * NB, NB), :] = (cen * inv * gain_two).astype(BF)
        return 0

    lax.fori_loop(0, T // NB, norm_second, 0)
    give_rows(n2, 3)
    pump()
    got_rows(n2, 3)
    take(dyf.at[mine, :], swr.at[1])
    give_rows(dyf, 1)

    HB = nz * M

    def hidden(t, _):
        i, ti = t // (S // TB), lax.rem(t, S // TB)
        cols = pl.ds(pl.multiple_of(ti * TB, TB), TB)
        rows = rows_at(i * HB, HB)
        normed = n2[cols, :]
        act = dg(W[rows_at(base("a0") + i * HB, HB), :], normed, 1, 1)
        gate = dg(W[rows_at(base("b0") + i * HB, HB), :], normed, 1, 1)
        cdf = 0.5 + 0.5 * lax.erf(act * 0.7071067811865476)
        gelu = act * cdf
        slope = cdf + act * (jnp.exp(-0.5 * act * act) * 0.3989422804014327)
        hid[rows, cols] = (gelu * gate).astype(BF)
        AB[0, rows, cols] = (slope * gate).astype(BF)
        AB[1, rows, cols] = gelu.astype(BF)
        return 0

    ds = [f"d{i}" for i in range(cuts) if f"d{i}" not in p.early]
    ab = [f"{m}{i}" for m in "ba" for i in range(cuts)]
    turn = ds + ab + ["o"] + [f"q{j}" for j in range(p.heads)] + ["n"]
    at = [0, 0, 0, 0]

    def sum_next(start=1):
        one, two, ready_for_three, three = at
        for name in turn[one : one + start]:
            rs1(name)
        for name in turn[two:one]:
            rs2(name)
        for name in turn[three:ready_for_three]:
            rs3(name)
        at[:] = min(one + start, len(turn)), one, two, ready_for_three

    def grad_of(name, lhs, rhs):
        dest, at = place[name]
        dest[pl.ds(at, nz * p.pieces[name][1]), :] = dg(lhs, rhs[...], 1, 0).astype(BF)

    for i in range(cuts):
        ready(f"a{i}")
        ready(f"b{i}")
        if i == cuts - 1:
            pump()
        lax.fori_loop(i * (S // TB), (i + 1) * (S // TB), hidden, 0)
        if i == 0:
            got_rows(dyf, 1)
        grad_of(f"d{i}", hid[i * HB : (i + 1) * HB, :], dyf)
        if f"d{i}" in p.early:
            early1(f"d{i}")
        else:
            sum_next()
        pump()
    for _ in steps:
        raise ValueError("steps left")

    def back_hidden(t, _):
        i, ti = t // (S // TB), lax.rem(t, S // TB)
        cols = pl.ds(pl.multiple_of(ti * TB, TB), TB)
        rows = rows_at(i * HB, HB)
        g = dg(W[rows_at(base("d0") + i * HB, HB), :], dyf[cols, :], 1, 1)
        AB[0, rows, cols] = (g * AB[0, rows, cols].astype(F32)).astype(BF)
        AB[1, rows, cols] = (g * AB[1, rows, cols].astype(F32)).astype(BF)
        return 0

    for i in range(cuts):
        ready(f"d{i}")
        lax.fori_loop(i * (S // TB), (i + 1) * (S // TB), back_hidden, 0)
        grad_of(f"b{i}", AB[1, i * HB : (i + 1) * HB, :], n2)
        if i < 2:
            sum_next()

    lhs_hid = [lambda cols: hid[:, cols]]
    lhs_gp = [lambda cols: AB[0, :, cols], lambda cols: AB[1, :, cols]]
    take(exs.at[0], cs.at[2])
    send_partial(lhs_hid, [full_d], 0, 0, 4)
    send_partial(lhs_gp, [full_a, full_b], 1, 1, 5)
    sum_next()
    take(exr.at[0], cr.at[4])
    take(exs.at[0], cs.at[4])

    def output(t, _):
        own = rows_at(t * MB, MB)
        total = partial(lhs_hid, [full_d], c * T + t * MB)
        xs = res[own, :] + (total + exr[0, own, :].astype(F32))
        exs[0, own, :] = xs.astype(BF)
        return 0

    lax.fori_loop(0, T // MB, output, 0)
    swap(exs.at[0], out_hbm, out_hbm, 2)

    for i in range(cuts):
        sent(f"d{i}")
    for i in range(cuts):
        grad_of(f"a{i}", AB[0, i * HB : (i + 1) * HB, :], n2)
    sum_next()
    take(exr.at[1], cr.at[5])

    def grad_residual(t, carry):
        own = rows_at(t * MB, MB)
        total = partial(lhs_gp, [full_a, full_b], c * T + t * MB) + exr[1, own, :].astype(F32)
        v = res[own, :]
        cen, inv = norm_parts(v)
        hat = cen * inv
        carry = carry + jnp.sum(total * hat, axis=0, keepdims=True)
        dh = total * gain_two
        back = inv * (
            dh - jnp.mean(dh, axis=1, keepdims=True) - hat * jnp.mean(dh * hat, axis=1, keepdims=True)
        )
        g = dyf[rows_at(c * T + t * MB, MB), :].astype(F32) + back
        res[own, :] = g
        dyf[rows_at(c * T + t * MB, MB), :] = g.astype(BF)
        return carry

    take(dyf.at[mine, :], cs.at[1])
    gain_two_grad = lax.fori_loop(0, T // MB, grad_residual, jnp.zeros((1, D), F32))
    give_rows(dyf, 6)
    sum_next()
    for name in p.early:
        early2(name)
    got_rows(dyf, 6)

    sent("o")
    for i in range(cuts):
        sent(f"a{i}")
        sent(f"b{i}")

    gat = AB.at[0]

    def grad_att(t, _):
        rows = rows_at(t * U, U)
        gat[rows, :] = dg(W[rows_at(base("o") + t * U, U), :], dyf[...], 1, 1).astype(BF)
        return 0

    lax.fori_loop(0, nz, grad_att, 0)
    grad_of("o", att[...], dyf)
    sum_next()
    for name in p.early:
        early3(name)

    QC = 512

    def attend_back(t, _):
        q_rows, k_rows, v_rows, o_rows = head_rows(t)
        keyT = qkv[k_rows, :]
        key = keyT.T
        val = qkv[v_rows, :].T

        def block(b, carry):
            dk, dv = carry
            cols = pl.ds(pl.multiple_of(b * QC, QC), QC)
            q = qkv[q_rows, cols]
            g = gat[o_rows, cols]
            inner = jnp.sum(g.astype(F32) * att[o_rows, cols].astype(F32), axis=0, keepdims=True)
            prob = jnp.exp(dg(key, q, 1, 0) - lse[t, :, cols])
            dprob = dg(val, g, 1, 0)
            ds = (prob * (dprob - inner)).astype(BF)
            dv = dv + dg(g, prob.astype(BF), 1, 1)
            dk = dk + dg(q, ds, 1, 1)
            dq = dg(keyT, ds, 1, 0) * HD**-0.5
            co, si = cos_ref[:, cols], sin_ref[:, cols]
            g1, g2 = dq[: HD // 2], dq[HD // 2 :]
            qkv[q_rows, cols] = jnp.concatenate([g1 * co + g2 * si, g2 * co - g1 * si], axis=0).astype(BF)
            return dk, dv

        zero = jnp.zeros((HD, S), F32)
        dk, dv = lax.fori_loop(0, S // QC, block, (zero, zero))
        g1, g2 = dk[: HD // 2], dk[HD // 2 :]
        co, si = cos_ref[...], sin_ref[...]
        qkv[k_rows, :] = jnp.concatenate([g1 * co + g2 * si, g2 * co - g1 * si], axis=0).astype(BF)
        qkv[v_rows, :] = dv.astype(BF)
        return 0

    for t in range(0, NH, 2):
        lax.fori_loop(t, t + 2, attend_back, 0)
        if (t + 2) % nz == 0:
            j = t // nz
            grad_of(f"q{j}", qkv[j * QR : (j + 1) * QR, :], n1)
        sum_next(min(1, turn.index(f"q{(t + 2) // nz}") - at[0]) if t + 2 < NH else 1)
        if t == 0:
            for name in p.early:
                early4(name)

    lhs_proj = [lambda cols: qkv[:, cols]]
    take(exs.at[1], cs.at[5])
    send_partial(lhs_proj, [full_q], 1, 0, 7)
    swap_sent(exs.at[0], 2)
    take(out_hbm, swr.at[2])
    take(exr.at[0], cr.at[7])

    def grad_input(t, carry):
        own = rows_at(t * MB, MB)
        total = partial(lhs_proj, [full_q], c * T + t * MB) + exr[0, own, :].astype(F32)
        cen, inv = norm_parts(xown[own, :].astype(F32))
        hat = cen * inv
        carry = carry + jnp.sum(total * hat, axis=0, keepdims=True)
        dh = total * gain_one
        back = inv * (
            dh - jnp.mean(dh, axis=1, keepdims=True) - hat * jnp.mean(dh * hat, axis=1, keepdims=True)
        )
        exs[0, own, :] = (res[own, :] + back).astype(BF)
        return carry

    gain_one_grad = lax.fori_loop(0, T // MB, grad_input, jnp.zeros((1, D), F32))
    swap(exs.at[0], gtok_hbm, gtok_hbm, 3)
    line = lax.broadcasted_iota(jnp.int32, (16, D), 0)
    both = jnp.where(line == 0, gain_one_grad, jnp.where(line == 1, gain_two_grad, 0.0)).astype(BF)
    for j in range(nz):
        Gn[16 * j : 16 * j + 16, :] = both
    for _ in range(4):
        sum_next()
    if at != [len(turn)] * 4:
        raise ValueError("turns left")
    for name in p.early:
        early5(name)
    for name in turn:
        rs4(name)
    for part in range(3):
        for k in range(2):
            firsts = [p.pieces[f"q{j}"][0] + part * HD for j in range(p.heads)]
            g_q[part, :, k * U : (k + 1) * U] = jnp.concatenate(
                [stage[k, at : at + HD, :] for at in firsts], axis=0
            ).T
    store(f"q{p.heads - 1}")

    sent("n")
    for j in range(p.heads):
        sent(f"q{j}")
    for name in p.order:
        rs_sent(name)
    swap_sent(x_hbm, 0)
    swap_sent(dy_hbm, 1)
    swap_sent(exs.at[0], 3)
    take(gtok_hbm, swr.at[3])
    take(n1.at[mine, :], cs.at[0])
    take(n2.at[mine, :], cs.at[3])
    take(dyf.at[mine, :], cs.at[6])
    take(exs.at[1], cs.at[7])
    for name in p.order:
        stored(name)


def layer(plan, x, dy, gain_a, gain_m, w_o, w_q, w_ab, w_d, rope):
    p = plan
    nz, D, T, U, H = p.nz, p.width, p.tokens, p.units, p.hid
    S, L = 2 * T, p.lane
    n = len(p.order)
    hbm = pl.BlockSpec(memory_space=pl.ANY)
    dma = pltpu.SemaphoreType.DMA
    scratch = [
        pltpu.VMEM((nz * p.rows, D), BF),
        pltpu.VMEM((T, D), BF),
        pltpu.VMEM((S, D), BF),
        pltpu.VMEM((S, D), BF),
        pltpu.VMEM((nz * 3 * U, S), BF),
        pltpu.VMEM((nz * U, S), BF),
        pltpu.VMEM((nz * p.heads, 1, S), F32),
        pltpu.VMEM((T, D), F32),
        pltpu.VMEM((S, D), BF),
        pltpu.VMEM((2, nz * H, S), BF),
        pltpu.VMEM((nz * H, S), BF),
        pltpu.VMEM((2, T, D), BF),
        pltpu.VMEM((2, T, D), BF),
        pltpu.VMEM((nz * 16, D), BF),
        pltpu.VMEM((nz * H, D), BF),
        pltpu.VMEM((nz * H, D), BF),
        pltpu.VMEM((2, 2, (nz // 2) * p.rows, p.block), BF),
        pltpu.VMEM((2, (nz // 2) * p.rows, p.block), BF),
        pltpu.VMEM((2 * nz, p.rows, p.lane), BF),
        pltpu.VMEM((nz - 1, max(len(p.early), 1) * p.sub, D), BF),
        pltpu.VMEM((2, HD // 2, S), F32),
        pltpu.VMEM((2, p.rows, L), F32),
        pltpu.VMEM((2, 1, L), BF),
        pltpu.VMEM((16, L), BF),
        pltpu.VMEM((3, L, 2 * U), BF),
        pltpu.VMEM((6 * U, L), BF),
        pltpu.VMEM((2, 2 * H, L), BF),
        pltpu.VMEM((2 * H, L), BF),
        pltpu.VMEM((3, L, 2 * U), F32),
        dma((n,)),
        dma((n,)),
        dma((n, 6)),
        dma((n,)),
        dma((n, 2, 2)),
        dma((n,)),
        dma((n, 2)),
        dma((n,)),
        dma((n,)),
        dma((n,)),
        dma((4,)),
        dma((4,)),
        dma((8,)),
        dma((8,)),
        dma((n, 2)),
        dma((n,)),
        dma((n,)),
        dma((n,)),
        dma((n,)),
        dma((7,)),
    ]
    return pl.pallas_call(
        functools.partial(kernel, p),
        out_shape=(
            jax.ShapeDtypeStruct((T, D), BF),
            jax.ShapeDtypeStruct((T, D), BF),
            jax.ShapeDtypeStruct((16, L), F32),
            jax.ShapeDtypeStruct((2 * U, L), F32),
            jax.ShapeDtypeStruct((3, L, 2 * U), F32),
            jax.ShapeDtypeStruct((2, p.real, L), F32),
            jax.ShapeDtypeStruct((p.real, L), F32),
        ),
        in_specs=[hbm] * 9,
        out_specs=(hbm,) * 7,
        scratch_shapes=scratch,
        compiler_params=pltpu.CompilerParams(
            collective_id=0, has_side_effects=True, vmem_limit_bytes=VMEM
        ),
        name="layer",
    )(x, dy, gain_a, gain_m, w_o, w_q, w_ab, w_d, rope)


def settle_kernel(count, *refs):
    ins, outs, held = refs[:count], refs[count : 2 * count + 1], refs[2 * count + 1 : 3 * count + 1]
    load_sem, store_sem = refs[3 * count + 1 :]
    loads = [pltpu.make_async_copy(a, b, load_sem.at[i]) for i, (a, b) in enumerate(zip(ins, held))]
    for copy in loads:
        copy.start()
    sources = [[h] for h in held]
    sources[2] = [held[2].at[pl.ds(0, 1), :], held[2].at[pl.ds(1, 1), :]]
    stores = []
    for copy, parts in zip(loads, sources):
        copy.wait()
        for part in parts:
            store = pltpu.make_async_copy(part, outs[len(stores)], store_sem.at[len(stores)])
            store.start()
            stores.append(store)
    for store in stores:
        store.wait()


def settle(out, gtok, g_n, *rest):
    arrays = (out, gtok, g_n) + rest
    row = jax.ShapeDtypeStruct((1, g_n.shape[1]), F32)
    like = [jax.ShapeDtypeStruct(a.shape, a.dtype) for a in arrays]
    shapes = (*like[:2], row, row, *like[3:])
    hbm = pl.BlockSpec(memory_space=pl.ANY)
    return pl.pallas_call(
        functools.partial(settle_kernel, len(arrays)),
        out_shape=shapes,
        in_specs=[hbm] * len(arrays),
        out_specs=(hbm,) * len(shapes),
        scratch_shapes=[pltpu.VMEM(a.shape, a.dtype) for a in arrays]
        + [pltpu.SemaphoreType.DMA((len(arrays),)), pltpu.SemaphoreType.DMA((len(shapes),))],
        compiler_params=pltpu.CompilerParams(vmem_limit_bytes=VMEM),
        name="settle",
    )(*arrays)


def rope_table():
    freq = THETA ** (-np.arange(HD // 2) * 2.0 / HD)
    angle = freq.astype(np.float32)[:, None] * np.arange(LEN, dtype=np.float32)[None, :]
    return np.stack([np.cos(angle), np.sin(angle)]).astype(np.float32)


def local(outer, nz, tokens, w_qkv, w_out, w_in, w_down, gain_attn, gain_mlp, grad_output):
    T, D = tokens.shape
    groups = [[hi * LOW + lo for hi in range(outer)] for lo in range(LOW)]
    piece = D // (outer * LOW)

    def widen(a, axis):
        if outer == 1:
            return a
        return lax.all_gather(a, "dp", axis=axis, tiled=True, axis_index_groups=groups)

    def narrow(a, axis):
        if outer == 1:
            return a
        return lax.psum_scatter(a, "dp", scatter_dimension=axis, tiled=True, axis_index_groups=groups)

    def turn(a, first, second):
        if outer == 1:
            return a
        return a.reshape(T, first, second, piece).swapaxes(1, 2).reshape(T, D)

    w_qkv, w_in = widen(w_qkv, 0), widen(w_in, 0)
    w_out, w_down = widen(w_out, 1), widen(w_down, 1)
    gains = [widen(g, 0) for g in (gain_attn, gain_mlp)]
    x = turn(tokens, outer, LOW)
    dy = turn(grad_output, outer, LOW)
    p = Plan(nz, D, T, w_qkv.shape[2], w_in.shape[2])
    L = p.lane
    rope = jnp.asarray(rope_table())
    results = layer(
        p,
        x,
        dy,
        gains[0].reshape(1, L),
        gains[1].reshape(1, L),
        w_out,
        w_qkv.transpose(1, 0, 2),
        w_in.transpose(1, 2, 0),
        w_down,
        rope,
    )
    out, gtok, g_a, g_m, g_out, g_q, g_ab, g_down = settle(*results)

    out, gtok = turn(out, LOW, outer), turn(gtok, LOW, outer)
    g_qkv = g_q.transpose(1, 0, 2)
    g_in = g_ab.transpose(2, 0, 1)
    return (
        out,
        gtok,
        narrow(g_qkv, 0),
        narrow(g_out, 1),
        narrow(g_in, 0),
        narrow(g_down, 1),
        narrow(g_a.reshape(L), 0),
        narrow(g_m.reshape(L), 0),
    )


def solution(mesh):
    rows = P(("dp", "tensor"), None)
    deep = P("dp", None, "tensor")
    wide = P("tensor", "dp")
    flat = P("dp")
    return jax.shard_map(
        functools.partial(local, mesh.shape["dp"] // LOW, mesh.shape["tensor"]),
        mesh=mesh,
        in_specs=(rows, deep, wide, deep, wide, flat, flat, rows),
        out_specs=(rows, rows, deep, wide, deep, wide, flat, flat),
        check_vma=False,
    )
```

```python
import functools

import jax
import jax.numpy as jnp
import numpy as np
from jax import lax
from jax.experimental import pallas as pl
from jax.experimental.pallas import tpu as pltpu
from jax.sharding import PartitionSpec as P

HD = 64
LEN = 1024
EPS = 1e-05
THETA = 160000.0
MESH = pl.DeviceIdType.MESH
BF = jnp.bfloat16
F32 = jnp.float32
VMEM = 64 * 1024 * 1024 - 65536
LOW = 8


def up(n, m):
    return -(-n // m) * m


def dg(a, b, ca, cb):
    return lax.dot_general(a, b, (((ca,), (cb,)), ((), ())), preferred_element_type=F32)


class Plan:
    def __init__(self, nz, width, tokens, units, hidden):
        self.nz, self.width, self.tokens = nz, width, tokens
        self.lane = width // LOW
        self.block = 2 * self.lane
        self.units = units // 2
        self.heads = self.units // HD
        self.real = hidden
        self.hid = up(-(-hidden // 2), 16)
        self.cuts = next(n for n in (3, 2, 1) if self.hid % (16 * n) == 0)
        self.sub = self.hid // self.cuts
        self.pieces = {}
        total = 0
        sizes = [("n", 16), ("o", self.units)]
        sizes += [(f"q{i}", HD) for i in range(3 * self.heads)]
        sizes += [(f"{m}{i}", self.sub) for m in "abd" for i in range(self.cuts)]
        for name, rows in sizes:
            self.pieces[name] = (total, rows)
            total += rows
        self.rows = total
        self.order = ["n"] + [f"q{i}" for i in range(3 * self.heads)] + ["o"]
        self.order += [f"{m}{i}" for i in range(self.cuts) for m in "ab"]
        self.order += [f"d{i}" for i in range(self.cuts)]
        self.late = self.order[-1:] if self.cuts > 1 else []
        self.early = [f"d{i}" for i in range(2 * len(self.late))]


def kernel(
    plan,
    x_hbm,
    dy_hbm,
    gain_a_hbm,
    gain_m_hbm,
    w_o_hbm,
    w_q_hbm,
    w_ab_hbm,
    w_d_hbm,
    rope_hbm,
    out_hbm,
    gtok_hbm,
    g_n_hbm,
    g_o_hbm,
    g_q_hbm,
    g_ab_hbm,
    g_d_hbm,
    W,
    xown,
    dyf,
    n1,
    qkv,
    att,
    lse,
    res,
    n2,
    AB,
    hid,
    exs,
    exr,
    Gn,
    Gb,
    Gd,
    R1,
    R2,
    R3,
    RZ,
    rope,
    stage,
    gains,
    gain_rows,
    w_q_in,
    w_q,
    w_ab,
    w_d,
    g_q,
    zr,
    zs,
    xyr,
    xys,
    r1r,
    r1s,
    r2r,
    r2s,
    r3r,
    r3s,
    swr,
    sws,
    cr,
    cs,
    gs,
    lr,
    ls,
    er,
    es,
    ins,
):
    p = plan
    nz, D, T, U, H = p.nz, p.width, p.tokens, p.units, p.hid
    S = 2 * T
    L, B = p.lane, p.block
    d = lax.axis_index("dp")
    z = lax.axis_index("tensor")
    c = lax.rem(d, 2)
    r = lax.rem(d // 2, 4)
    xb = lax.rem(r, 2)
    yb = r // 2
    zb = lax.rem(z, 2)
    sib = d + 1 - 2 * c
    xp = d + 2 - 4 * xb
    yp = d + 4 - 8 * yb
    zpair = z + 1 - 2 * zb
    rx = r + 1 - 2 * xb
    ry = r + 2 - 4 * yb
    rd = 3 - r
    stay = lax.rem(c + z, 2) == 0

    def rows_at(start, n):
        return pl.ds(pl.multiple_of(start, 16), n)

    def lanes(block):
        return pl.ds(pl.multiple_of(block * B, L), B)

    mine = rows_at(c * T, T)
    theirs_start = (1 - c) * T

    def remote(src, dst, ssem, rsem, dev):
        pltpu.make_async_remote_copy(src, dst, ssem, rsem, device_id=dev, device_id_type=MESH).start()

    def take(ref, sem):
        pltpu.make_async_copy(ref, ref, sem).wait()

    partners = [(sib, z), (xp, z), (yp, z)]
    for dz in range(1, nz):
        there = lax.rem(z + dz, nz)
        partners += [(d, there), (sib, there)]
    bar = pltpu.get_barrier_semaphore()
    for dev in partners:
        pl.semaphore_signal(bar, inc=1, device_id=dev, device_id_type=MESH)

    def load(src, dst, i):
        return pltpu.make_async_copy(src, dst, ins.at[i])

    real = p.real
    loads = [
        load(gain_a_hbm, gains.at[0], 0),
        load(gain_m_hbm, gains.at[1], 1),
        load(w_q_hbm, w_q_in, 2),
        load(w_ab_hbm.at[0], w_ab.at[0, pl.ds(0, real), :], 3),
        load(w_ab_hbm.at[1], w_ab.at[1, pl.ds(0, real), :], 4),
        load(w_d_hbm, w_d.at[pl.ds(0, real), :], 5),
        load(rope_hbm, rope, 6),
    ]
    for copy in loads:
        copy.start()
    if 2 * H > real:
        zeros = jnp.zeros((2 * H - real, L), BF)
        w_ab[0, real:, :] = zeros
        w_ab[1, real:, :] = zeros
        w_d[real:, :] = zeros
    for copy in loads:
        copy.wait()
    line = lax.broadcasted_iota(jnp.int32, (16, L), 0)
    first, second = (gains[j, :, :].astype(F32) for j in range(2))
    gain_rows[...] = jnp.where(line == 0, first, jnp.where(line == 1, second, 0.0)).astype(BF)
    for part in range(3):
        turned = w_q_in[part, :, :].T
        for k in range(2):
            for j in range(p.heads):
                at = k * U + j * HD
                to = (k * p.heads + j) * 3 * HD + part * HD
                w_q[to : to + HD, :] = turned[at : at + HD, :]
    pl.semaphore_wait(bar, len(partners))

    index = {name: i for i, name in enumerate(p.pieces)}
    M, cuts = p.sub, p.cuts

    def shard(name, k):
        kind, j = name[0], int(name[1:] or 0)
        if kind == "n":
            return gain_rows
        if kind == "o":
            return w_o_hbm.at[rows_at(k * U, U), :]
        if kind == "q":
            return w_q.at[rows_at(k * 3 * U + j * HD, HD), :]
        if kind == "d":
            return w_d.at[rows_at(k * H + j * M, M), :]
        return w_ab.at[0 if kind == "a" else 1, rows_at(k * H + j * M, M), :]

    def base(name):
        return nz * p.pieces[name][0]

    def count(name):
        return p.pieces[name][1]

    def z_start(name):
        off, n = p.pieces[name]
        i = index[name]
        dst = W.at[rows_at(base(name) + z * n, n), pl.ds(pl.multiple_of(r * B + c * L, L), L)]
        for dz in range(nz):
            there = lax.rem(z + dz, nz)
            for kk in range(2):
                k = lax.rem(c + kk, 2)
                src = shard(name, k)
                if dz == 0 and kk == 0:
                    pltpu.make_async_copy(src, dst, zr.at[i]).start()
                else:
                    remote(src, dst, zs.at[i], zr.at[i], (d if kk == 0 else sib, there))

    def part(block, which):
        return pl.ds(pl.multiple_of(block * B + which * L, L), L)

    def own_rows(name):
        n = count(name)
        return rows_at(base(name) + z * n, n)

    def late0(name):
        i = index[name]
        dst = W.at[own_rows(name), part(r, c)]
        pltpu.make_async_copy(shard(name, c), dst, zr.at[i]).start()
        remote(shard(name, 1 - c), dst, zs.at[i], zr.at[i], (sib, z))

    def late1(name):
        i = index[name]
        own = own_rows(name)
        take(W.at[own, lanes(r)], zr.at[i])
        a = W.at[own, part(r, 0)]
        b = W.at[own, part(r, 1)]
        remote(a, a, xys.at[i], xyr.at[i, 0], (xp, z))
        remote(b, b, xys.at[i], xyr.at[i, 1], (yp, z))
        remote(a, a, xys.at[i], xyr.at[i, 2], (yp, z))
        remote(b, b, xys.at[i], xyr.at[i, 3], (xp, z))

    def late2(name):
        i = index[name]
        own = own_rows(name)
        a = W.at[own, part(rx, 0)]
        b = W.at[own, part(ry, 1)]
        take(a, xyr.at[i, 0])
        remote(a, a, xys.at[i], xyr.at[i, 4], (yp, z))
        take(b, xyr.at[i, 1])
        remote(b, b, xys.at[i], xyr.at[i, 5], (xp, z))

    def late3(name):
        i = index[name]
        own = own_rows(name)
        for slot, (block, which) in enumerate(((ry, 0), (rx, 1), (rd, 0), (rd, 1))):
            take(W.at[own, part(block, which)], xyr.at[i, 2 + slot])
        for dz in range(1, nz):
            remote(W.at[own, :], W.at[own, :], ls.at[i], lr.at[i], (d, lax.rem(z + dz, nz)))

    def half(name, which):
        n = (nz // 2) * count(name)
        return pl.ds(base(name) + which * n, n)

    def xy1(name):
        i = index[name]
        take(W.at[pl.ds(base(name), nz * count(name)), lanes(r)], zr.at[i])
        a = W.at[half(name, 0), lanes(r)]
        b = W.at[half(name, 1), lanes(r)]
        remote(a, a, xys.at[i], xyr.at[i, 0], (xp, z))
        remote(b, b, xys.at[i], xyr.at[i, 1], (yp, z))
        remote(a, a, xys.at[i], xyr.at[i, 2], (yp, z))
        remote(b, b, xys.at[i], xyr.at[i, 3], (xp, z))

    def xy2(name):
        i = index[name]
        a = W.at[half(name, 0), lanes(rx)]
        b = W.at[half(name, 1), lanes(ry)]
        take(a, xyr.at[i, 0])
        remote(a, a, xys.at[i], xyr.at[i, 4], (yp, z))
        take(b, xyr.at[i, 1])
        remote(b, b, xys.at[i], xyr.at[i, 5], (xp, z))

    def ready(name):
        i = index[name]
        if name in p.late:
            take(W.at[pl.ds(0, (nz - 1) * count(name)), :], lr.at[i])
            return
        take(W.at[half(name, 0), lanes(ry)], xyr.at[i, 2])
        take(W.at[half(name, 1), lanes(rx)], xyr.at[i, 3])
        take(W.at[half(name, 0), lanes(rd)], xyr.at[i, 4])
        take(W.at[half(name, 1), lanes(rd)], xyr.at[i, 5])

    def sent(name):
        i = index[name]
        n = count(name)
        if name in p.late:
            take(R3.at[0, pl.ds(0, n), :], zs.at[i])
            take(R3.at[pl.ds(0, 6), pl.ds(0, n), :], xys.at[i])
            take(W.at[pl.ds(0, (nz - 1) * n), :], ls.at[i])
            return
        take(R3.at[pl.ds(0, 2 * nz - 1), pl.ds(0, n), :], zs.at[i])
        take(W.at[pl.ds(0, 6 * (nz // 2) * n * B // D), :], xys.at[i])

    place = {"n": (Gn, 0), "o": (W, base("a0") + nz * 3 * U)}
    for i in range(3 * p.heads):
        place[f"q{i}"] = (W, base("a0") + i * nz * HD)
    for i in range(cuts):
        place[f"a{i}"] = (W, base("d0") + i * nz * M)
        place[f"b{i}"] = (Gb, i * nz * M)
        place[f"d{i}"] = (Gd, i * nz * M)

    def ghalf(name, which):
        n = (nz // 2) * count(name)
        return pl.ds(place[name][1] + which * n, n)

    def rhalf(name):
        return pl.ds((nz // 2) * p.pieces[name][0], (nz // 2) * count(name))

    def step_of(n):
        for s in (128, 112, 96, 80, 64, 48, 32, 16):
            if n % s == 0:
                return s
        return n

    def rs1(name):
        i = index[name]
        G = place[name][0]
        to = rhalf(name)
        for which, near, dev in ((0, ry, yp), (1, rx, xp)):
            rows = ghalf(name, which)
            remote(G.at[rows, lanes(rd)], R1.at[which, 0, to, :], r1s.at[i], r1r.at[i, which, 0], (dev, z))
        for which, near, dev in ((0, ry, yp), (1, rx, xp)):
            rows = ghalf(name, which)
            remote(G.at[rows, lanes(near)], R1.at[which, 1, to, :], r1s.at[i], r1r.at[i, which, 1], (dev, z))

    def rs2(name):
        i = index[name]
        G, gb = place[name]
        n = (nz // 2) * count(name)
        to = rhalf(name)
        s = step_of(n)
        for which, block, dev in ((0, rx, xp), (1, ry, yp)):
            take(R1.at[which, 0, to, :], r1r.at[i, which, 0])

            def add(t, _):
                g = rows_at(gb + which * n + t * s, s)
                q = rows_at(to.start + t * s, s)
                G[g, lanes(block)] = (G[g, lanes(block)].astype(F32) + R1[which, 0, q, :].astype(F32)).astype(BF)
                return 0

            lax.fori_loop(0, n // s, add, 0)
            remote(
                G.at[ghalf(name, which), lanes(block)],
                R2.at[which, to, :],
                r2s.at[i],
                r2r.at[i, which],
                (dev, z),
            )

    def rs3(name):
        i = index[name]
        G, gb = place[name]
        off, m = p.pieces[name]
        n = (nz // 2) * m
        to = rhalf(name)
        s = step_of(n)
        for which in range(2):
            take(R1.at[which, 1, to, :], r1r.at[i, which, 1])
            take(R2.at[which, to, :], r2r.at[i, which])

            def add(t, _):
                g = rows_at(gb + which * n + t * s, s)
                q = rows_at(to.start + t * s, s)
                total = G[g, lanes(r)].astype(F32) + R1[which, 1, q, :].astype(F32) + R2[which, q, :].astype(F32)
                G[g, lanes(r)] = total.astype(BF)
                return 0

            lax.fori_loop(0, n // s, add, 0)
        dst = R3.at[z * 2 + c, pl.ds(off, m), :]
        for dz in range(nz):
            there = lax.rem(z + dz, nz)
            for kk in range(2):
                k = lax.rem(c + kk, 2)
                src = G.at[rows_at(gb + there * m, m), pl.ds(pl.multiple_of(r * B + k * L, L), L)]
                if dz == 0 and kk == 0:
                    pltpu.make_async_copy(src, dst, r3r.at[i]).start()
                else:
                    remote(src, dst, r3s.at[i], r3r.at[i], (d if kk == 0 else sib, there))

    def rs4(name):
        i = index[name]
        off, m = p.pieces[name]
        take(R3.at[:, pl.ds(off, m), :], r3r.at[i])
        for k in range(2):
            total = R3[k, off : off + m, :].astype(F32)
            for j in range(1, nz):
                total += R3[2 * j + k, off : off + m, :].astype(F32)
            stage[k, off : off + m, :] = total
        if name == "n":
            stage[0, off : off + m, :] += stage[1, off : off + m, :]
        if name[0] != "q":
            store(name)

    def store(name):
        for j, (src, dst) in enumerate(stores(name)):
            pltpu.make_async_copy(src, dst, gs.at[index[name], j]).start()

    def early1(name):
        i = index[name]
        G, gb = place[name]
        n = count(name)
        at = p.early.index(name) * n
        for dz in range(1, nz):
            there = lax.rem(z + dz, nz)
            src = G.at[rows_at(gb + there * n, n), :]
            remote(src, RZ.at[dz - 1, pl.ds(at, n), :], es.at[i], er.at[i], (d, there))

    def early2(name):
        i = index[name]
        G, gb = place[name]
        off, n = p.pieces[name]
        at = p.early.index(name) * n
        take(RZ.at[:, pl.ds(at, n), :], er.at[i])

        def add(t, _):
            g = rows_at(gb + z * n + t * 16, 16)
            q = rows_at(at + t * 16, 16)
            total = G[g, :].astype(F32)
            for j in range(nz - 1):
                total += RZ[j, q, :].astype(F32)
            G[g, :] = total.astype(BF)
            return 0

        lax.fori_loop(0, n // 16, add, 0)
        own = rows_at(gb + z * n, n)
        to = pl.ds(off, n)
        for slot, (block, which, dev) in enumerate(((rd, 0, yp), (ry, 0, yp), (rd, 1, xp), (rx, 1, xp))):
            remote(
                G.at[own, part(block, which)],
                R3.at[slot, to, :],
                r1s.at[i],
                r1r.at[i, which, slot % 2],
                (dev, z),
            )

    def early3(name):
        i = index[name]
        G, gb = place[name]
        off, n = p.pieces[name]
        own, to = rows_at(gb + z * n, n), pl.ds(off, n)
        for which, block, dev in ((0, rx, xp), (1, ry, yp)):
            take(R3.at[2 * which, to, :], r1r.at[i, which, 0])
            there = part(block, which)
            G[own, there] = (G[own, there].astype(F32) + R3[2 * which, to, :].astype(F32)).astype(BF)
            remote(G.at[own, there], R3.at[4 + which, to, :], r2s.at[i], r2r.at[i, which], (dev, z))

    def early4(name):
        i = index[name]
        G, gb = place[name]
        off, n = p.pieces[name]
        own, to = rows_at(gb + z * n, n), pl.ds(off, n)
        for which in range(2):
            take(R3.at[2 * which + 1, to, :], r1r.at[i, which, 1])
            take(R3.at[4 + which, to, :], r2r.at[i, which])
            total = G[own, part(r, which)].astype(F32) + R3[2 * which + 1, to, :].astype(F32)
            total += R3[4 + which, to, :].astype(F32)

            @pl.when(c == which)
            def _():
                stage[which, to, :] = total

            @pl.when(c != which)
            def _():
                R3[7, to, :] = total.astype(BF)

        remote(R3.at[7, to, :], R3.at[6, to, :], r3s.at[i], r3r.at[i], (sib, z))

    def early5(name):
        i = index[name]
        off, n = p.pieces[name]
        to = pl.ds(off, n)
        take(R3.at[6, to, :], r3r.at[i])
        for k in range(2):

            @pl.when(c != k)
            def _():
                stage[k, to, :] = R3[6, to, :].astype(F32)

        store(name)

    def stores(name):
        off, m = p.pieces[name]
        kind, j = name[0], int(name[1:] or 0)
        if kind == "n":
            return [(stage.at[0, pl.ds(off, m), :], g_n_hbm)]
        if kind == "q":
            return [(g_q, g_q_hbm)] if j == 3 * p.heads - 1 else []
        pairs = []
        for k in range(2):
            n = m
            if kind == "o":
                dst, at = g_o_hbm, k * U
            else:
                at = k * H + j * M
                n = min(m, p.real - at)
                dst = g_d_hbm if kind == "d" else g_ab_hbm.at[0 if kind == "a" else 1]
            if n > 0:
                pairs.append((stage.at[k, pl.ds(off, n), :], dst.at[pl.ds(at, n), :]))
        return pairs

    def stored(name):
        for j, (src, dst) in enumerate(stores(name)):
            take(dst, gs.at[index[name], j])

    def rs_sent(name):
        i = index[name]
        m = count(name)
        if name in p.early:
            take(W.at[pl.ds(0, (nz - 1) * m), :], es.at[i])
            take(R3.at[pl.ds(0, 4), pl.ds(0, m), :], r1s.at[i])
            take(R3.at[pl.ds(0, 2), pl.ds(0, m), :], r2s.at[i])
            take(R3.at[0, pl.ds(0, m), :], r3s.at[i])
            return
        n = (nz // 2) * m
        take(W.at[pl.ds(0, 4 * n * B // D), :], r1s.at[i])
        take(W.at[pl.ds(0, 2 * n * B // D), :], r2s.at[i])
        take(R3.at[pl.ds(0, 2 * nz - 1), pl.ds(0, m), :], r3s.at[i])

    def swap(src, dst_here, dst_there, i):
        @pl.when(stay)
        def _():
            pltpu.make_async_copy(src, dst_here, swr.at[i]).start()

        @pl.when(jnp.logical_not(stay))
        def _():
            remote(src, dst_there, sws.at[i], swr.at[i], (sib, zpair))

    def swap_sent(src, i):
        @pl.when(jnp.logical_not(stay))
        def _():
            take(src, sws.at[i])

    def give(src, dst, i):
        remote(src, dst, cs.at[i], cr.at[i], (sib, z))

    def give_rows(buf, i):
        give(buf.at[mine, :], buf.at[mine, :], i)

    def got_rows(buf, i):
        take(buf.at[mine, :], cr.at[i])

    NB = 64

    order = [[name] for name in p.order if name not in p.late and name[0] != "q"]
    order[1:1] = [["q0"], ["q1", "q2"]] + [[f"q{3 * j + i}" for i in range(3)] for j in range(1, p.heads)]
    steps = iter(range(len(order) + 1))
    waiting = iter(order)

    def z_some(count):
        for _, group in zip(range(count), waiting):
            for name in group:
                z_start(name)

    def pump(ahead=1):
        k = next(steps)
        z_some(ahead)
        if 0 < k:
            for name in order[k - 1]:
                xy2(name)
        if k < len(order):
            for name in order[k]:
                xy1(name)

    for name in p.late:
        late0(name)
    z_some(2)
    for name in p.late:
        late1(name)
    cos_ref, sin_ref = rope.at[0], rope.at[1]
    pump()
    pump()
    swap(x_hbm, xown, xown, 0)
    for name in p.late:
        late2(name)
    ready("n")

    gain_one = W[0:16, :][0:1, :].astype(F32)
    gain_two = W[0:16, :][1:2, :].astype(F32)

    def norm_parts(v):
        mean = jnp.mean(v, axis=1, keepdims=True)
        cen = v - mean
        inv = lax.rsqrt(jnp.mean(cen * cen, axis=1, keepdims=True) + EPS)
        return cen, inv

    def norm_first(t, _):
        own = rows_at(t * NB, NB)
        cen, inv = norm_parts(xown[own, :].astype(F32))
        n1[rows_at(c * T + t * NB, NB), :] = (cen * inv * gain_one).astype(BF)
        return 0

    pump()
    take(xown, swr.at[0])
    lax.fori_loop(0, T // NB, norm_first, 0)
    give_rows(n1, 0)
    pump(2)
    got_rows(n1, 0)

    TB = 512
    QR = nz * 3 * HD

    def project(t, _):
        j, ti = t // (S // TB), lax.rem(t, S // TB)
        cols = pl.ds(pl.multiple_of(ti * TB, TB), TB)
        acc = dg(W[rows_at(base("q0") + j * QR, QR), :], n1[cols, :], 1, 1)
        co, si = cos_ref[:, cols], sin_ref[:, cols]
        for part in range(3):
            parts = []
            for zi in range(nz):
                at = (part * nz + zi) * HD
                if part == 2:
                    parts.append(acc[at : at + HD])
                    continue
                v1, v2 = acc[at : at + HD // 2], acc[at + HD // 2 : at + HD]
                w1, w2 = v1 * co - v2 * si, v2 * co + v1 * si
                if part == 0:
                    w1, w2 = w1 * HD**-0.5, w2 * HD**-0.5
                parts += [w1, w2]
            qkv[rows_at(j * QR + part * nz * HD, nz * HD), cols] = jnp.concatenate(parts, axis=0).astype(BF)
        return 0

    QB = 1024

    def head_rows(t):
        q, k, v = (rows_at((t // nz * 3 * nz + part * nz + lax.rem(t, nz)) * HD, HD) for part in range(3))
        return q, k, v, rows_at(lax.rem(t, nz) * U + t // nz * HD, HD)

    def attend(t, _):
        q_rows, k_rows, v_rows, o_rows = head_rows(t)
        key = qkv[k_rows, :].T
        val = qkv[v_rows, :]

        def block(b, _):
            cols = pl.ds(pl.multiple_of(b * QB, QB), QB)
            s = dg(key, qkv[q_rows, cols], 1, 0)
            m = jnp.max(s, axis=0, keepdims=True)
            e = jnp.exp(s - m)
            l = jnp.sum(e, axis=0, keepdims=True)
            o = dg(val, e.astype(BF), 1, 0)
            att[o_rows, cols] = (o / l).astype(BF)
            lse[t, :, cols] = m + jnp.log(l)
            return 0

        lax.fori_loop(0, S // QB, block, 0)
        return 0

    NH = nz * p.heads
    late = iter(p.late)
    for t in range(0, NH, 2):
        if t % nz == 0:
            j = t // nz
            for i in range(3 * j, 3 * j + 3):
                ready(f"q{i}")
            lax.fori_loop(j * (S // TB), (j + 1) * (S // TB), project, 0)
        pump()
        lax.fori_loop(t, t + 2, attend, 0)
        if t == 2:
            swap(dy_hbm, dyf.at[mine, :], dyf.at[rows_at(theirs_start, T), :], 1)
        for name in late:
            late3(name)
            break
    ready("o")

    MB = 256

    def partial(lhs_rows, rhs, start):
        cols = pl.ds(pl.multiple_of(start, MB), MB)
        total = None
        for lhs, w in zip(lhs_rows, rhs):
            term = dg(lhs(cols), w[...], 0, 0)
            total = term if total is None else total + term
        return total

    def send_partial(lhs_rows, rhs, slot, there, i):
        def some(t, _):
            exs[slot, rows_at(t * MB, MB), :] = partial(lhs_rows, rhs, theirs_start + t * MB).astype(BF)
            return 0

        lax.fori_loop(0, T // MB, some, 0)
        give(exs.at[slot], exr.at[there], i)

    full_o = W.at[pl.ds(base("o"), nz * U), :]
    full_q = W.at[pl.ds(base("q0"), nz * 3 * U), :]
    full_a = W.at[pl.ds(base("a0"), nz * H), :]
    full_b = W.at[pl.ds(base("b0"), nz * H), :]
    full_d = W.at[pl.ds(base("d0"), nz * H), :]

    lhs_att = [lambda cols: att[:, cols]]
    send_partial(lhs_att, [full_o], 0, 0, 2)

    def residual(t, _):
        own = rows_at(t * MB, MB)
        res[own, :] = xown[own, :].astype(F32) + partial(lhs_att, [full_o], c * T + t * MB)
        return 0

    lax.fori_loop(0, T // MB, residual, 0)
    pump()
    take(exr.at[0], cr.at[2])

    def norm_second(t, _):
        own = rows_at(t * NB, NB)
        v = res[own, :] + exr[0, own, :].astype(F32)
        res[own, :] = v
        cen, inv = norm_parts(v)
        n2[rows_at(c * T + t * NB, NB), :] = (cen * inv * gain_two).astype(BF)
        return 0

    lax.fori_loop(0, T // NB, norm_second, 0)
    give_rows(n2, 3)
    pump()
    got_rows(n2, 3)
    take(dyf.at[mine, :], swr.at[1])
    give_rows(dyf, 1)

    HB = nz * M

    def hidden(t, _):
        i, ti = t // (S // TB), lax.rem(t, S // TB)
        cols = pl.ds(pl.multiple_of(ti * TB, TB), TB)
        rows = rows_at(i * HB, HB)
        normed = n2[cols, :]
        act = dg(W[rows_at(base("a0") + i * HB, HB), :], normed, 1, 1)
        gate = dg(W[rows_at(base("b0") + i * HB, HB), :], normed, 1, 1)
        cdf = 0.5 + 0.5 * lax.erf(act * 0.7071067811865476)
        gelu = act * cdf
        slope = cdf + act * (jnp.exp(-0.5 * act * act) * 0.3989422804014327)
        hid[rows, cols] = (gelu * gate).astype(BF)
        AB[0, rows, cols] = (slope * gate).astype(BF)
        AB[1, rows, cols] = gelu.astype(BF)
        return 0

    ds = [f"d{i}" for i in range(cuts) if f"d{i}" not in p.early]
    ab = [f"{m}{i}" for m in "ba" for i in range(cuts)]
    turn = ds + ab + ["o"] + [f"q{i}" for i in range(3 * p.heads)]
    at = [0, 0, 0, 0]

    def sum_next(start=1):
        one, two, ready_for_three, three = at
        for name in turn[one : one + start]:
            rs1(name)
        for name in turn[two:one]:
            rs2(name)
        for name in turn[three:ready_for_three]:
            rs3(name)
        at[:] = min(one + start, len(turn)), one, two, ready_for_three

    def grad_of(name, lhs, rhs):
        dest, at = place[name]
        dest[pl.ds(at, nz * p.pieces[name][1]), :] = dg(lhs, rhs[...], 1, 0).astype(BF)

    for i in range(cuts):
        ready(f"a{i}")
        ready(f"b{i}")
        if i == cuts - 1:
            pump()
        lax.fori_loop(i * (S // TB), (i + 1) * (S // TB), hidden, 0)
        if i == 0:
            got_rows(dyf, 1)
        grad_of(f"d{i}", hid[i * HB : (i + 1) * HB, :], dyf)
        if f"d{i}" in p.early:
            early1(f"d{i}")
        else:
            sum_next()
        pump()
    for _ in steps:
        raise ValueError("steps left")

    def back_hidden(t, _):
        i, ti = t // (S // TB), lax.rem(t, S // TB)
        cols = pl.ds(pl.multiple_of(ti * TB, TB), TB)
        rows = rows_at(i * HB, HB)
        g = dg(W[rows_at(base("d0") + i * HB, HB), :], dyf[cols, :], 1, 1)
        AB[0, rows, cols] = (g * AB[0, rows, cols].astype(F32)).astype(BF)
        AB[1, rows, cols] = (g * AB[1, rows, cols].astype(F32)).astype(BF)
        return 0

    for i in range(cuts):
        ready(f"d{i}")
        lax.fori_loop(i * (S // TB), (i + 1) * (S // TB), back_hidden, 0)
        grad_of(f"b{i}", AB[1, i * HB : (i + 1) * HB, :], n2)
        if i < 2:
            sum_next()

    lhs_hid = [lambda cols: hid[:, cols]]
    lhs_gp = [lambda cols: AB[0, :, cols], lambda cols: AB[1, :, cols]]
    take(exs.at[0], cs.at[2])
    send_partial(lhs_hid, [full_d], 0, 0, 4)
    send_partial(lhs_gp, [full_a, full_b], 1, 1, 5)
    sum_next()
    take(exr.at[0], cr.at[4])
    take(exs.at[0], cs.at[4])

    def output(t, _):
        own = rows_at(t * MB, MB)
        total = partial(lhs_hid, [full_d], c * T + t * MB)
        xs = res[own, :] + (total + exr[0, own, :].astype(F32))
        exs[0, own, :] = xs.astype(BF)
        return 0

    lax.fori_loop(0, T // MB, output, 0)
    swap(exs.at[0], out_hbm, out_hbm, 2)

    for i in range(cuts):
        sent(f"d{i}")
    for i in range(cuts):
        grad_of(f"a{i}", AB[0, i * HB : (i + 1) * HB, :], n2)
    sum_next()
    take(exr.at[1], cr.at[5])

    def grad_residual(t, carry):
        own = rows_at(t * MB, MB)
        total = partial(lhs_gp, [full_a, full_b], c * T + t * MB) + exr[1, own, :].astype(F32)
        v = res[own, :]
        cen, inv = norm_parts(v)
        hat = cen * inv
        carry = carry + jnp.sum(total * hat, axis=0, keepdims=True)
        dh = total * gain_two
        back = inv * (
            dh - jnp.mean(dh, axis=1, keepdims=True) - hat * jnp.mean(dh * hat, axis=1, keepdims=True)
        )
        g = dyf[rows_at(c * T + t * MB, MB), :].astype(F32) + back
        res[own, :] = g
        dyf[rows_at(c * T + t * MB, MB), :] = g.astype(BF)
        return carry

    take(dyf.at[mine, :], cs.at[1])
    gain_two_grad = lax.fori_loop(0, T // MB, grad_residual, jnp.zeros((1, D), F32))
    give_rows(dyf, 6)
    sum_next()
    for name in p.early[:1]:
        early2(name)
    got_rows(dyf, 6)

    sent("o")
    for i in range(cuts):
        sent(f"a{i}")
        sent(f"b{i}")

    gat = AB.at[0]

    def grad_att(t, _):
        rows = rows_at(t * U, U)
        gat[rows, :] = dg(W[rows_at(base("o") + t * U, U), :], dyf[...], 1, 1).astype(BF)
        return 0

    lax.fori_loop(0, nz, grad_att, 0)
    grad_of("o", att[...], dyf)
    sum_next()
    for name in p.early[:1]:
        early3(name)
    for name in p.early[1:]:
        early2(name)

    QC = 512

    def attend_back(t, _):
        q_rows, k_rows, v_rows, o_rows = head_rows(t)
        keyT = qkv[k_rows, :]
        key = keyT.T
        val = qkv[v_rows, :].T

        def block(b, carry):
            dk, dv = carry
            cols = pl.ds(pl.multiple_of(b * QC, QC), QC)
            q = qkv[q_rows, cols]
            g = gat[o_rows, cols]
            inner = jnp.sum(g.astype(F32) * att[o_rows, cols].astype(F32), axis=0, keepdims=True)
            prob = jnp.exp(dg(key, q, 1, 0) - lse[t, :, cols])
            dprob = dg(val, g, 1, 0)
            ds = (prob * (dprob - inner)).astype(BF)
            dv = dv + dg(g, prob.astype(BF), 1, 1)
            dk = dk + dg(q, ds, 1, 1)
            dq = dg(keyT, ds, 1, 0) * HD**-0.5
            co, si = cos_ref[:, cols], sin_ref[:, cols]
            g1, g2 = dq[: HD // 2], dq[HD // 2 :]
            qkv[q_rows, cols] = jnp.concatenate([g1 * co + g2 * si, g2 * co - g1 * si], axis=0).astype(BF)
            return dk, dv

        zero = jnp.zeros((HD, S), F32)
        dk, dv = lax.fori_loop(0, S // QC, block, (zero, zero))
        g1, g2 = dk[: HD // 2], dk[HD // 2 :]
        co, si = cos_ref[...], sin_ref[...]
        qkv[k_rows, :] = jnp.concatenate([g1 * co + g2 * si, g2 * co - g1 * si], axis=0).astype(BF)
        qkv[v_rows, :] = dv.astype(BF)
        return 0

    for t in range(0, NH, 2):
        lax.fori_loop(t, t + 2, attend_back, 0)
        if t == 0:
            sum_next()
        elif (t + 2) % nz == 0:
            first = (t // nz) * 3
            for i in range(first, first + 3):
                grad_of(f"q{i}", qkv[i * nz * HD : (i + 1) * nz * HD, :], n1)
            sum_next(3)
        else:
            sum_next(0)
        if t == 0:
            for name in p.early[:1]:
                early4(name)
            for name in p.early[1:]:
                early3(name)
        if t == 2:
            for name in p.early[1:]:
                early4(name)

    lhs_proj = [lambda cols: qkv[:, cols]]
    take(exs.at[1], cs.at[5])
    send_partial(lhs_proj, [full_q], 1, 0, 7)
    _, two, _, three = at
    for name in turn[three:two]:
        rs3(name)
    last = turn[two:]
    swap_sent(exs.at[0], 2)
    take(out_hbm, swr.at[2])
    take(exr.at[0], cr.at[7])
    rs2(last[0])

    def grad_input(t, carry):
        own = rows_at(t * MB, MB)
        total = partial(lhs_proj, [full_q], c * T + t * MB) + exr[0, own, :].astype(F32)
        cen, inv = norm_parts(xown[own, :].astype(F32))
        hat = cen * inv
        carry = carry + jnp.sum(total * hat, axis=0, keepdims=True)
        dh = total * gain_one
        back = inv * (
            dh - jnp.mean(dh, axis=1, keepdims=True) - hat * jnp.mean(dh * hat, axis=1, keepdims=True)
        )
        exs[0, own, :] = (res[own, :] + back).astype(BF)
        return carry

    gain_one_grad = lax.fori_loop(0, T // MB, grad_input, jnp.zeros((1, D), F32))
    swap(exs.at[0], gtok_hbm, gtok_hbm, 3)
    line = lax.broadcasted_iota(jnp.int32, (16, D), 0)
    both = jnp.where(line == 0, gain_one_grad, jnp.where(line == 1, gain_two_grad, 0.0)).astype(BF)
    for j in range(nz):
        Gn[16 * j : 16 * j + 16, :] = both
    rs1("n")
    for name in last[1:]:
        rs2(name)
    rs3(last[0])
    rs2("n")
    for name in last[1:] + ["n"]:
        rs3(name)
    for name in p.early:
        early5(name)
    for name in turn + ["n"]:
        rs4(name)
    for part in range(3):
        for k in range(2):
            firsts = [p.pieces[f"q{3 * j + part}"][0] for j in range(p.heads)]
            g_q[part, :, k * U : (k + 1) * U] = jnp.concatenate(
                [stage[k, at : at + HD, :] for at in firsts], axis=0
            ).T
    store(f"q{3 * p.heads - 1}")

    sent("n")
    for i in range(3 * p.heads):
        sent(f"q{i}")
    for name in p.order:
        rs_sent(name)
    swap_sent(x_hbm, 0)
    swap_sent(dy_hbm, 1)
    swap_sent(exs.at[0], 3)
    take(gtok_hbm, swr.at[3])
    take(n1.at[mine, :], cs.at[0])
    take(n2.at[mine, :], cs.at[3])
    take(dyf.at[mine, :], cs.at[6])
    take(exs.at[1], cs.at[7])
    for name in p.order:
        stored(name)


def layer(plan, x, dy, gain_a, gain_m, w_o, w_q, w_ab, w_d, rope):
    p = plan
    nz, D, T, U, H = p.nz, p.width, p.tokens, p.units, p.hid
    S, L = 2 * T, p.lane
    n = len(p.order)
    hbm = pl.BlockSpec(memory_space=pl.ANY)
    dma = pltpu.SemaphoreType.DMA
    scratch = [
        pltpu.VMEM((nz * p.rows, D), BF),
        pltpu.VMEM((T, D), BF),
        pltpu.VMEM((S, D), BF),
        pltpu.VMEM((S, D), BF),
        pltpu.VMEM((nz * 3 * U, S), BF),
        pltpu.VMEM((nz * U, S), BF),
        pltpu.VMEM((nz * p.heads, 1, S), F32),
        pltpu.VMEM((T, D), F32),
        pltpu.VMEM((S, D), BF),
        pltpu.VMEM((2, nz * H, S), BF),
        pltpu.VMEM((nz * H, S), BF),
        pltpu.VMEM((2, T, D), BF),
        pltpu.VMEM((2, T, D), BF),
        pltpu.VMEM((nz * 16, D), BF),
        pltpu.VMEM((nz * H, D), BF),
        pltpu.VMEM((nz * H, D), BF),
        pltpu.VMEM((2, 2, (nz // 2) * p.rows, p.block), BF),
        pltpu.VMEM((2, (nz // 2) * p.rows, p.block), BF),
        pltpu.VMEM((2 * nz, p.rows, p.lane), BF),
        pltpu.VMEM((nz - 1, max(len(p.early), 1) * p.sub, D), BF),
        pltpu.VMEM((2, HD // 2, S), F32),
        pltpu.VMEM((2, p.rows, L), F32),
        pltpu.VMEM((2, 1, L), BF),
        pltpu.VMEM((16, L), BF),
        pltpu.VMEM((3, L, 2 * U), BF),
        pltpu.VMEM((6 * U, L), BF),
        pltpu.VMEM((2, 2 * H, L), BF),
        pltpu.VMEM((2 * H, L), BF),
        pltpu.VMEM((3, L, 2 * U), F32),
        dma((n,)),
        dma((n,)),
        dma((n, 6)),
        dma((n,)),
        dma((n, 2, 2)),
        dma((n,)),
        dma((n, 2)),
        dma((n,)),
        dma((n,)),
        dma((n,)),
        dma((4,)),
        dma((4,)),
        dma((8,)),
        dma((8,)),
        dma((n, 2)),
        dma((n,)),
        dma((n,)),
        dma((n,)),
        dma((n,)),
        dma((7,)),
    ]
    return pl.pallas_call(
        functools.partial(kernel, p),
        out_shape=(
            jax.ShapeDtypeStruct((T, D), BF),
            jax.ShapeDtypeStruct((T, D), BF),
            jax.ShapeDtypeStruct((16, L), F32),
            jax.ShapeDtypeStruct((2 * U, L), F32),
            jax.ShapeDtypeStruct((3, L, 2 * U), F32),
            jax.ShapeDtypeStruct((2, p.real, L), F32),
            jax.ShapeDtypeStruct((p.real, L), F32),
        ),
        in_specs=[hbm] * 9,
        out_specs=(hbm,) * 7,
        scratch_shapes=scratch,
        compiler_params=pltpu.CompilerParams(
            collective_id=0, has_side_effects=True, vmem_limit_bytes=VMEM
        ),
        name="layer",
    )(x, dy, gain_a, gain_m, w_o, w_q, w_ab, w_d, rope)


def settle_kernel(count, *refs):
    ins, outs, held = refs[:count], refs[count : 2 * count + 1], refs[2 * count + 1 : 3 * count + 1]
    load_sem, store_sem = refs[3 * count + 1 :]
    loads = [pltpu.make_async_copy(a, b, load_sem.at[i]) for i, (a, b) in enumerate(zip(ins, held))]
    for copy in loads:
        copy.start()
    sources = [[h] for h in held]
    sources[2] = [held[2].at[pl.ds(0, 1), :], held[2].at[pl.ds(1, 1), :]]
    stores = []
    for copy, parts in zip(loads, sources):
        copy.wait()
        for part in parts:
            store = pltpu.make_async_copy(part, outs[len(stores)], store_sem.at[len(stores)])
            store.start()
            stores.append(store)
    for store in stores:
        store.wait()


def settle(out, gtok, g_n, *rest):
    arrays = (out, gtok, g_n) + rest
    row = jax.ShapeDtypeStruct((1, g_n.shape[1]), F32)
    like = [jax.ShapeDtypeStruct(a.shape, a.dtype) for a in arrays]
    shapes = (*like[:2], row, row, *like[3:])
    hbm = pl.BlockSpec(memory_space=pl.ANY)
    return pl.pallas_call(
        functools.partial(settle_kernel, len(arrays)),
        out_shape=shapes,
        in_specs=[hbm] * len(arrays),
        out_specs=(hbm,) * len(shapes),
        scratch_shapes=[pltpu.VMEM(a.shape, a.dtype) for a in arrays]
        + [pltpu.SemaphoreType.DMA((len(arrays),)), pltpu.SemaphoreType.DMA((len(shapes),))],
        compiler_params=pltpu.CompilerParams(vmem_limit_bytes=VMEM),
        name="settle",
    )(*arrays)


def rope_table():
    freq = THETA ** (-np.arange(HD // 2) * 2.0 / HD)
    angle = freq.astype(np.float32)[:, None] * np.arange(LEN, dtype=np.float32)[None, :]
    return np.stack([np.cos(angle), np.sin(angle)]).astype(np.float32)


def local(outer, nz, tokens, w_qkv, w_out, w_in, w_down, gain_attn, gain_mlp, grad_output):
    T, D = tokens.shape
    groups = [[hi * LOW + lo for hi in range(outer)] for lo in range(LOW)]
    piece = D // (outer * LOW)

    def widen(a, axis):
        if outer == 1:
            return a
        return lax.all_gather(a, "dp", axis=axis, tiled=True, axis_index_groups=groups)

    def narrow(a, axis):
        if outer == 1:
            return a
        return lax.psum_scatter(a, "dp", scatter_dimension=axis, tiled=True, axis_index_groups=groups)

    def turn(a, first, second):
        if outer == 1:
            return a
        return a.reshape(T, first, second, piece).swapaxes(1, 2).reshape(T, D)

    w_qkv, w_in = widen(w_qkv, 0), widen(w_in, 0)
    w_out, w_down = widen(w_out, 1), widen(w_down, 1)
    gains = [widen(g, 0) for g in (gain_attn, gain_mlp)]
    x = turn(tokens, outer, LOW)
    dy = turn(grad_output, outer, LOW)
    p = Plan(nz, D, T, w_qkv.shape[2], w_in.shape[2])
    L = p.lane
    rope = jnp.asarray(rope_table())
    results = layer(
        p,
        x,
        dy,
        gains[0].reshape(1, L),
        gains[1].reshape(1, L),
        w_out,
        w_qkv.transpose(1, 0, 2),
        w_in.transpose(1, 2, 0),
        w_down,
        rope,
    )
    out, gtok, g_a, g_m, g_out, g_q, g_ab, g_down = settle(*results)

    out, gtok = turn(out, LOW, outer), turn(gtok, LOW, outer)
    g_qkv = g_q.transpose(1, 0, 2)
    g_in = g_ab.transpose(2, 0, 1)
    return (
        out,
        gtok,
        narrow(g_qkv, 0),
        narrow(g_out, 1),
        narrow(g_in, 0),
        narrow(g_down, 1),
        narrow(g_a.reshape(L), 0),
        narrow(g_m.reshape(L), 0),
    )


def solution(mesh):
    rows = P(("dp", "tensor"), None)
    deep = P("dp", None, "tensor")
    wide = P("tensor", "dp")
    flat = P("dp")
    return jax.shard_map(
        functools.partial(local, mesh.shape["dp"] // LOW, mesh.shape["tensor"]),
        mesh=mesh,
        in_specs=(rows, deep, wide, deep, wide, flat, flat, rows),
        out_specs=(rows, rows, deep, wide, deep, wide, flat, flat),
        check_vma=False,
    )
```

```python
import functools

import jax
import jax.numpy as jnp
import numpy as np
from jax import lax
from jax.experimental import pallas as pl
from jax.experimental.pallas import tpu as pltpu
from jax.sharding import PartitionSpec as P

HD = 64
LEN = 1024
EPS = 1e-05
THETA = 160000.0
MESH = pl.DeviceIdType.MESH
BF = jnp.bfloat16
F32 = jnp.float32
VMEM = 64 * 1024 * 1024 - 65536
LOW = 8


def up(n, m):
    return -(-n // m) * m


def dg(a, b, ca, cb):
    return lax.dot_general(a, b, (((ca,), (cb,)), ((), ())), preferred_element_type=F32)


class Plan:
    def __init__(self, nz, width, tokens, units, hidden):
        self.nz, self.width, self.tokens = nz, width, tokens
        self.lane = width // LOW
        self.block = 2 * self.lane
        self.units = units // 2
        self.heads = self.units // HD
        self.real = hidden
        self.hid = up(-(-hidden // 2), 16)
        self.cuts = next(n for n in (3, 2, 1) if self.hid % (16 * n) == 0)
        self.sub = self.hid // self.cuts
        self.pieces = {}
        total = 0
        sizes = [("n", 16), ("o", self.units)]
        sizes += [(f"q{i}", HD) for i in range(3 * self.heads)]
        sizes += [(f"{m}{i}", self.sub) for m in "abd" for i in range(self.cuts)]
        for name, rows in sizes:
            self.pieces[name] = (total, rows)
            total += rows
        self.rows = total
        self.order = ["n"] + [f"q{i}" for i in range(3 * self.heads)] + ["o"]
        self.order += [f"{m}{i}" for i in range(self.cuts) for m in "ab"]
        self.order += [f"d{i}" for i in range(self.cuts)]
        self.late = self.order[-1:] if self.cuts > 1 else []
        self.early = [f"d{i}" for i in range(2 * len(self.late))]


def kernel(
    plan,
    x_hbm,
    dy_hbm,
    gain_a_hbm,
    gain_m_hbm,
    w_o_hbm,
    w_q_hbm,
    w_ab_hbm,
    w_d_hbm,
    rope_hbm,
    out_hbm,
    gtok_hbm,
    g_n_hbm,
    g_o_hbm,
    g_q_hbm,
    g_ab_hbm,
    g_d_hbm,
    W,
    xown,
    dyf,
    n1,
    qkv,
    att,
    lse,
    res,
    n2,
    AB,
    hid,
    exs,
    exr,
    Gn,
    Gb,
    Gd,
    R1,
    R2,
    R3,
    RZ,
    rope,
    stage,
    gains,
    gain_rows,
    w_q_in,
    w_q,
    w_ab,
    w_d,
    g_q,
    zr,
    zs,
    xyr,
    xys,
    r1r,
    r1s,
    r2r,
    r2s,
    r3r,
    r3s,
    swr,
    sws,
    cr,
    cs,
    gs,
    lr,
    ls,
    er,
    es,
    ins,
):
    p = plan
    nz, D, T, U, H = p.nz, p.width, p.tokens, p.units, p.hid
    S = 2 * T
    L, B = p.lane, p.block
    d = lax.axis_index("dp")
    z = lax.axis_index("tensor")
    c = lax.rem(d, 2)
    r = lax.rem(d // 2, 4)
    xb = lax.rem(r, 2)
    yb = r // 2
    zb = lax.rem(z, 2)
    sib = d + 1 - 2 * c
    xp = d + 2 - 4 * xb
    yp = d + 4 - 8 * yb
    zpair = z + 1 - 2 * zb
    rx = r + 1 - 2 * xb
    ry = r + 2 - 4 * yb
    rd = 3 - r
    stay = lax.rem(c + z, 2) == 0

    def rows_at(start, n):
        return pl.ds(pl.multiple_of(start, 16), n)

    def lanes(block):
        return pl.ds(pl.multiple_of(block * B, L), B)

    mine = rows_at(c * T, T)
    theirs_start = (1 - c) * T

    def remote(src, dst, ssem, rsem, dev):
        pltpu.make_async_remote_copy(src, dst, ssem, rsem, device_id=dev, device_id_type=MESH).start()

    def take(ref, sem):
        pltpu.make_async_copy(ref, ref, sem).wait()

    partners = [(sib, z), (xp, z), (yp, z)]
    for dz in range(1, nz):
        there = lax.rem(z + dz, nz)
        partners += [(d, there), (sib, there)]
    bar = pltpu.get_barrier_semaphore()
    for dev in partners:
        pl.semaphore_signal(bar, inc=1, device_id=dev, device_id_type=MESH)

    def load(src, dst, i):
        return pltpu.make_async_copy(src, dst, ins.at[i])

    real = p.real
    loads = [
        load(gain_a_hbm, gains.at[0], 0),
        load(gain_m_hbm, gains.at[1], 1),
        load(w_q_hbm, w_q_in, 2),
        load(w_ab_hbm.at[0], w_ab.at[0, pl.ds(0, real), :], 3),
        load(w_ab_hbm.at[1], w_ab.at[1, pl.ds(0, real), :], 4),
        load(w_d_hbm, w_d.at[pl.ds(0, real), :], 5),
        load(rope_hbm, rope, 6),
    ]
    for copy in loads:
        copy.start()
    if 2 * H > real:
        zeros = jnp.zeros((2 * H - real, L), BF)
        w_ab[0, real:, :] = zeros
        w_ab[1, real:, :] = zeros
        w_d[real:, :] = zeros
    for copy in loads:
        copy.wait()
    line = lax.broadcasted_iota(jnp.int32, (16, L), 0)
    first, second = (gains[j, :, :].astype(F32) for j in range(2))
    gain_rows[...] = jnp.where(line == 0, first, jnp.where(line == 1, second, 0.0)).astype(BF)
    for part in range(3):
        turned = w_q_in[part, :, :].T
        for k in range(2):
            for j in range(p.heads):
                at = k * U + j * HD
                to = (k * p.heads + j) * 3 * HD + part * HD
                w_q[to : to + HD, :] = turned[at : at + HD, :]
    pl.semaphore_wait(bar, len(partners))

    index = {name: i for i, name in enumerate(p.pieces)}
    M, cuts = p.sub, p.cuts

    def shard(name, k):
        kind, j = name[0], int(name[1:] or 0)
        if kind == "n":
            return gain_rows
        if kind == "o":
            return w_o_hbm.at[rows_at(k * U, U), :]
        if kind == "q":
            return w_q.at[rows_at(k * 3 * U + j * HD, HD), :]
        if kind == "d":
            return w_d.at[rows_at(k * H + j * M, M), :]
        return w_ab.at[0 if kind == "a" else 1, rows_at(k * H + j * M, M), :]

    def base(name):
        return nz * p.pieces[name][0]

    def count(name):
        return p.pieces[name][1]

    def z_start(name):
        off, n = p.pieces[name]
        i = index[name]
        dst = W.at[rows_at(base(name) + z * n, n), pl.ds(pl.multiple_of(r * B + c * L, L), L)]
        for dz in range(nz):
            there = lax.rem(z + dz, nz)
            for kk in range(2):
                k = lax.rem(c + kk, 2)
                src = shard(name, k)
                if dz == 0 and kk == 0:
                    pltpu.make_async_copy(src, dst, zr.at[i]).start()
                else:
                    remote(src, dst, zs.at[i], zr.at[i], (d if kk == 0 else sib, there))

    def part(block, which):
        return pl.ds(pl.multiple_of(block * B + which * L, L), L)

    def own_rows(name):
        n = count(name)
        return rows_at(base(name) + z * n, n)

    def late0(name):
        i = index[name]
        dst = W.at[own_rows(name), part(r, c)]
        pltpu.make_async_copy(shard(name, c), dst, zr.at[i]).start()
        remote(shard(name, 1 - c), dst, zs.at[i], zr.at[i], (sib, z))

    def late1(name):
        i = index[name]
        own = own_rows(name)
        take(W.at[own, lanes(r)], zr.at[i])
        a = W.at[own, part(r, 0)]
        b = W.at[own, part(r, 1)]
        remote(a, a, xys.at[i], xyr.at[i, 0], (xp, z))
        remote(b, b, xys.at[i], xyr.at[i, 1], (yp, z))
        remote(a, a, xys.at[i], xyr.at[i, 2], (yp, z))
        remote(b, b, xys.at[i], xyr.at[i, 3], (xp, z))

    def late2(name):
        i = index[name]
        own = own_rows(name)
        a = W.at[own, part(rx, 0)]
        b = W.at[own, part(ry, 1)]
        take(a, xyr.at[i, 0])
        remote(a, a, xys.at[i], xyr.at[i, 4], (yp, z))
        take(b, xyr.at[i, 1])
        remote(b, b, xys.at[i], xyr.at[i, 5], (xp, z))

    def late3(name):
        i = index[name]
        own = own_rows(name)
        for slot, (block, which) in enumerate(((ry, 0), (rx, 1), (rd, 0), (rd, 1))):
            take(W.at[own, part(block, which)], xyr.at[i, 2 + slot])
        for dz in range(1, nz):
            remote(W.at[own, :], W.at[own, :], ls.at[i], lr.at[i], (d, lax.rem(z + dz, nz)))

    def half(name, which):
        n = (nz // 2) * count(name)
        return pl.ds(base(name) + which * n, n)

    def xy1(name):
        i = index[name]
        take(W.at[pl.ds(base(name), nz * count(name)), lanes(r)], zr.at[i])
        a = W.at[half(name, 0), lanes(r)]
        b = W.at[half(name, 1), lanes(r)]
        remote(a, a, xys.at[i], xyr.at[i, 0], (xp, z))
        remote(b, b, xys.at[i], xyr.at[i, 1], (yp, z))
        remote(a, a, xys.at[i], xyr.at[i, 2], (yp, z))
        remote(b, b, xys.at[i], xyr.at[i, 3], (xp, z))

    def xy2(name):
        i = index[name]
        a = W.at[half(name, 0), lanes(rx)]
        b = W.at[half(name, 1), lanes(ry)]
        take(a, xyr.at[i, 0])
        remote(a, a, xys.at[i], xyr.at[i, 4], (yp, z))
        take(b, xyr.at[i, 1])
        remote(b, b, xys.at[i], xyr.at[i, 5], (xp, z))

    def ready(name):
        i = index[name]
        if name in p.late:
            take(W.at[pl.ds(0, (nz - 1) * count(name)), :], lr.at[i])
            return
        take(W.at[half(name, 0), lanes(ry)], xyr.at[i, 2])
        take(W.at[half(name, 1), lanes(rx)], xyr.at[i, 3])
        take(W.at[half(name, 0), lanes(rd)], xyr.at[i, 4])
        take(W.at[half(name, 1), lanes(rd)], xyr.at[i, 5])

    def sent(name):
        i = index[name]
        n = count(name)
        if name in p.late:
            take(R3.at[0, pl.ds(0, n), :], zs.at[i])
            take(R3.at[pl.ds(0, 6), pl.ds(0, n), :], xys.at[i])
            take(W.at[pl.ds(0, (nz - 1) * n), :], ls.at[i])
            return
        take(R3.at[pl.ds(0, 2 * nz - 1), pl.ds(0, n), :], zs.at[i])
        take(W.at[pl.ds(0, 6 * (nz // 2) * n * B // D), :], xys.at[i])

    place = {"n": (Gn, 0), "o": (W, base("a0") + nz * 3 * U)}
    for i in range(3 * p.heads):
        place[f"q{i}"] = (W, base("a0") + i * nz * HD)
    for i in range(cuts):
        place[f"a{i}"] = (W, base("d0") + i * nz * M)
        place[f"b{i}"] = (Gb, i * nz * M)
        place[f"d{i}"] = (Gd, i * nz * M)

    def ghalf(name, which):
        n = (nz // 2) * count(name)
        return pl.ds(place[name][1] + which * n, n)

    def rhalf(name):
        return pl.ds((nz // 2) * p.pieces[name][0], (nz // 2) * count(name))

    def step_of(n):
        for s in (128, 112, 96, 80, 64, 48, 32, 16):
            if n % s == 0:
                return s
        return n

    def rs1(name):
        i = index[name]
        G = place[name][0]
        to = rhalf(name)
        for which, near, dev in ((0, ry, yp), (1, rx, xp)):
            rows = ghalf(name, which)
            remote(G.at[rows, lanes(rd)], R1.at[which, 0, to, :], r1s.at[i], r1r.at[i, which, 0], (dev, z))
        for which, near, dev in ((0, ry, yp), (1, rx, xp)):
            rows = ghalf(name, which)
            remote(G.at[rows, lanes(near)], R1.at[which, 1, to, :], r1s.at[i], r1r.at[i, which, 1], (dev, z))

    def rs2(name):
        i = index[name]
        G, gb = place[name]
        n = (nz // 2) * count(name)
        to = rhalf(name)
        s = step_of(n)
        for which, block, dev in ((0, rx, xp), (1, ry, yp)):
            take(R1.at[which, 0, to, :], r1r.at[i, which, 0])

            def add(t, _):
                g = rows_at(gb + which * n + t * s, s)
                q = rows_at(to.start + t * s, s)
                G[g, lanes(block)] = (G[g, lanes(block)].astype(F32) + R1[which, 0, q, :].astype(F32)).astype(BF)
                return 0

            lax.fori_loop(0, n // s, add, 0)
            remote(
                G.at[ghalf(name, which), lanes(block)],
                R2.at[which, to, :],
                r2s.at[i],
                r2r.at[i, which],
                (dev, z),
            )

    def rs3(name):
        i = index[name]
        G, gb = place[name]
        off, m = p.pieces[name]
        n = (nz // 2) * m
        to = rhalf(name)
        s = step_of(n)
        for which in range(2):
            take(R1.at[which, 1, to, :], r1r.at[i, which, 1])
            take(R2.at[which, to, :], r2r.at[i, which])

            def add(t, _):
                g = rows_at(gb + which * n + t * s, s)
                q = rows_at(to.start + t * s, s)
                total = G[g, lanes(r)].astype(F32) + R1[which, 1, q, :].astype(F32) + R2[which, q, :].astype(F32)
                G[g, lanes(r)] = total.astype(BF)
                return 0

            lax.fori_loop(0, n // s, add, 0)
        dst = R3.at[z * 2 + c, pl.ds(off, m), :]
        for dz in range(nz):
            there = lax.rem(z + dz, nz)
            for kk in range(2):
                k = lax.rem(c + kk, 2)
                src = G.at[rows_at(gb + there * m, m), pl.ds(pl.multiple_of(r * B + k * L, L), L)]
                if dz == 0 and kk == 0:
                    pltpu.make_async_copy(src, dst, r3r.at[i]).start()
                else:
                    remote(src, dst, r3s.at[i], r3r.at[i], (d if kk == 0 else sib, there))

    def rs4(name):
        i = index[name]
        off, m = p.pieces[name]
        take(R3.at[:, pl.ds(off, m), :], r3r.at[i])
        for k in range(2):
            total = R3[k, off : off + m, :].astype(F32)
            for j in range(1, nz):
                total += R3[2 * j + k, off : off + m, :].astype(F32)
            stage[k, off : off + m, :] = total
        if name == "n":
            stage[0, off : off + m, :] += stage[1, off : off + m, :]
        if name[0] != "q":
            store(name)

    def store(name):
        for j, (src, dst) in enumerate(stores(name)):
            pltpu.make_async_copy(src, dst, gs.at[index[name], j]).start()

    def early1(name):
        i = index[name]
        G, gb = place[name]
        n = count(name)
        at = p.early.index(name) * n
        for dz in range(1, nz):
            there = lax.rem(z + dz, nz)
            src = G.at[rows_at(gb + there * n, n), :]
            remote(src, RZ.at[dz - 1, pl.ds(at, n), :], es.at[i], er.at[i], (d, there))

    def early2(name):
        i = index[name]
        G, gb = place[name]
        off, n = p.pieces[name]
        at = p.early.index(name) * n
        take(RZ.at[:, pl.ds(at, n), :], er.at[i])

        def add(t, _):
            g = rows_at(gb + z * n + t * 16, 16)
            q = rows_at(at + t * 16, 16)
            total = G[g, :].astype(F32)
            for j in range(nz - 1):
                total += RZ[j, q, :].astype(F32)
            G[g, :] = total.astype(BF)
            return 0

        lax.fori_loop(0, n // 16, add, 0)
        own = rows_at(gb + z * n, n)
        to = pl.ds(off, n)
        for slot, (block, which, dev) in enumerate(((rd, 0, yp), (ry, 0, yp), (rd, 1, xp), (rx, 1, xp))):
            remote(
                G.at[own, part(block, which)],
                R3.at[slot, to, :],
                r1s.at[i],
                r1r.at[i, which, slot % 2],
                (dev, z),
            )

    def early3(name):
        i = index[name]
        G, gb = place[name]
        off, n = p.pieces[name]
        own, to = rows_at(gb + z * n, n), pl.ds(off, n)
        for which, block, dev in ((0, rx, xp), (1, ry, yp)):
            take(R3.at[2 * which, to, :], r1r.at[i, which, 0])
            there = part(block, which)
            G[own, there] = (G[own, there].astype(F32) + R3[2 * which, to, :].astype(F32)).astype(BF)
            remote(G.at[own, there], R3.at[4 + which, to, :], r2s.at[i], r2r.at[i, which], (dev, z))

    def early4(name):
        i = index[name]
        G, gb = place[name]
        off, n = p.pieces[name]
        own, to = rows_at(gb + z * n, n), pl.ds(off, n)
        for which in range(2):
            take(R3.at[2 * which + 1, to, :], r1r.at[i, which, 1])
            take(R3.at[4 + which, to, :], r2r.at[i, which])
            total = G[own, part(r, which)].astype(F32) + R3[2 * which + 1, to, :].astype(F32)
            total += R3[4 + which, to, :].astype(F32)

            @pl.when(c == which)
            def _():
                stage[which, to, :] = total

            @pl.when(c != which)
            def _():
                R3[7, to, :] = total.astype(BF)

        remote(R3.at[7, to, :], R3.at[6, to, :], r3s.at[i], r3r.at[i], (sib, z))

    def early5(name):
        i = index[name]
        off, n = p.pieces[name]
        to = pl.ds(off, n)
        take(R3.at[6, to, :], r3r.at[i])
        for k in range(2):

            @pl.when(c != k)
            def _():
                stage[k, to, :] = R3[6, to, :].astype(F32)

        store(name)

    def stores(name):
        off, m = p.pieces[name]
        kind, j = name[0], int(name[1:] or 0)
        if kind == "n":
            return [(stage.at[0, pl.ds(off, m), :], g_n_hbm)]
        if kind == "q":
            return [(g_q, g_q_hbm)] if j == 3 * p.heads - 1 else []
        pairs = []
        for k in range(2):
            n = m
            if kind == "o":
                dst, at = g_o_hbm, k * U
            else:
                at = k * H + j * M
                n = min(m, p.real - at)
                dst = g_d_hbm if kind == "d" else g_ab_hbm.at[0 if kind == "a" else 1]
            if n > 0:
                pairs.append((stage.at[k, pl.ds(off, n), :], dst.at[pl.ds(at, n), :]))
        return pairs

    def stored(name):
        for j, (src, dst) in enumerate(stores(name)):
            take(dst, gs.at[index[name], j])

    def rs_sent(name):
        i = index[name]
        m = count(name)
        if name in p.early:
            take(W.at[pl.ds(0, (nz - 1) * m), :], es.at[i])
            take(R3.at[pl.ds(0, 4), pl.ds(0, m), :], r1s.at[i])
            take(R3.at[pl.ds(0, 2), pl.ds(0, m), :], r2s.at[i])
            take(R3.at[0, pl.ds(0, m), :], r3s.at[i])
            return
        n = (nz // 2) * m
        take(W.at[pl.ds(0, 4 * n * B // D), :], r1s.at[i])
        take(W.at[pl.ds(0, 2 * n * B // D), :], r2s.at[i])
        take(R3.at[pl.ds(0, 2 * nz - 1), pl.ds(0, m), :], r3s.at[i])

    def swap(src, dst_here, dst_there, i):
        @pl.when(stay)
        def _():
            pltpu.make_async_copy(src, dst_here, swr.at[i]).start()

        @pl.when(jnp.logical_not(stay))
        def _():
            remote(src, dst_there, sws.at[i], swr.at[i], (sib, zpair))

    def swap_sent(src, i):
        @pl.when(jnp.logical_not(stay))
        def _():
            take(src, sws.at[i])

    def give(src, dst, i):
        remote(src, dst, cs.at[i], cr.at[i], (sib, z))

    def give_rows(buf, i):
        give(buf.at[mine, :], buf.at[mine, :], i)

    def got_rows(buf, i):
        take(buf.at[mine, :], cr.at[i])

    NB = 64

    order = [[name] for name in p.order if name not in p.late and name[0] != "q"]
    order[1:1] = [["q0"], ["q1", "q2"]] + [[f"q{3 * j + i}" for i in range(3)] for j in range(1, p.heads)]
    steps = iter(range(len(order) + 1))
    waiting = iter(order)

    def z_some(count):
        for _, group in zip(range(count), waiting):
            for name in group:
                z_start(name)

    def pump(ahead=1):
        k = next(steps)
        z_some(ahead)
        if 0 < k:
            for name in order[k - 1]:
                xy2(name)
        if k < len(order):
            for name in order[k]:
                xy1(name)

    for name in p.late:
        late0(name)
    z_some(2)
    for name in p.late:
        late1(name)
    cos_ref, sin_ref = rope.at[0], rope.at[1]
    pump()
    pump()
    swap(x_hbm, xown, xown, 0)
    for name in p.late:
        late2(name)
    ready("n")

    gain_one = W[0:16, :][0:1, :].astype(F32)
    gain_two = W[0:16, :][1:2, :].astype(F32)

    def norm_parts(v):
        mean = jnp.mean(v, axis=1, keepdims=True)
        cen = v - mean
        inv = lax.rsqrt(jnp.mean(cen * cen, axis=1, keepdims=True) + EPS)
        return cen, inv

    def norm_first(t, _):
        own = rows_at(t * NB, NB)
        cen, inv = norm_parts(xown[own, :].astype(F32))
        n1[rows_at(c * T + t * NB, NB), :] = (cen * inv * gain_one).astype(BF)
        return 0

    pump()
    take(xown, swr.at[0])
    lax.fori_loop(0, T // NB, norm_first, 0)
    give_rows(n1, 0)
    pump(2)
    got_rows(n1, 0)

    TB = 256
    QR = nz * 3 * HD

    def project(t, _):
        j, ti = t // (S // TB), lax.rem(t, S // TB)
        cols = pl.ds(pl.multiple_of(ti * TB, TB), TB)
        acc = dg(W[rows_at(base("q0") + j * QR, QR), :], n1[cols, :], 1, 1)
        co, si = cos_ref[:, cols], sin_ref[:, cols]
        for part in range(3):
            parts = []
            for zi in range(nz):
                at = (part * nz + zi) * HD
                if part == 2:
                    parts.append(acc[at : at + HD])
                    continue
                v1, v2 = acc[at : at + HD // 2], acc[at + HD // 2 : at + HD]
                w1, w2 = v1 * co - v2 * si, v2 * co + v1 * si
                if part == 0:
                    w1, w2 = w1 * HD**-0.5, w2 * HD**-0.5
                parts += [w1, w2]
            qkv[rows_at(j * QR + part * nz * HD, nz * HD), cols] = jnp.concatenate(parts, axis=0).astype(BF)
        return 0

    QB = 512

    def head_rows(t):
        q, k, v = (rows_at((t // nz * 3 * nz + part * nz + lax.rem(t, nz)) * HD, HD) for part in range(3))
        return q, k, v, rows_at(lax.rem(t, nz) * U + t // nz * HD, HD)

    def attend(t, _):
        q_rows, k_rows, v_rows, o_rows = head_rows(t)
        key = qkv[k_rows, :].T
        val = qkv[v_rows, :]

        def block(b, _):
            cols = pl.ds(pl.multiple_of(b * QB, QB), QB)
            s = dg(key, qkv[q_rows, cols], 1, 0)
            m = jnp.max(s, axis=0, keepdims=True)
            e = jnp.exp(s - m)
            l = jnp.sum(e, axis=0, keepdims=True)
            o = dg(val, e.astype(BF), 1, 0)
            att[o_rows, cols] = (o / l).astype(BF)
            lse[t, :, cols] = m + jnp.log(l)
            return 0

        lax.fori_loop(0, S // QB, block, 0)
        return 0

    NH = nz * p.heads
    late = iter(p.late)
    for t in range(0, NH, 2):
        if t % nz == 0:
            j = t // nz
            for i in range(3 * j, 3 * j + 3):
                ready(f"q{i}")
            lax.fori_loop(j * (S // TB), (j + 1) * (S // TB), project, 0)
        pump()
        lax.fori_loop(t, t + 2, attend, 0)
        if t == 2:
            swap(dy_hbm, dyf.at[mine, :], dyf.at[rows_at(theirs_start, T), :], 1)
        for name in late:
            late3(name)
            break
    ready("o")

    MB = 256

    def partial(lhs_rows, rhs, start):
        cols = pl.ds(pl.multiple_of(start, MB), MB)
        total = None
        for lhs, w in zip(lhs_rows, rhs):
            term = dg(lhs(cols), w[...], 0, 0)
            total = term if total is None else total + term
        return total

    def send_partial(lhs_rows, rhs, slot, there, i):
        def some(t, _):
            exs[slot, rows_at(t * MB, MB), :] = partial(lhs_rows, rhs, theirs_start + t * MB).astype(BF)
            return 0

        lax.fori_loop(0, T // MB, some, 0)
        give(exs.at[slot], exr.at[there], i)

    full_o = W.at[pl.ds(base("o"), nz * U), :]
    full_q = W.at[pl.ds(base("q0"), nz * 3 * U), :]
    full_a = W.at[pl.ds(base("a0"), nz * H), :]
    full_b = W.at[pl.ds(base("b0"), nz * H), :]
    full_d = W.at[pl.ds(base("d0"), nz * H), :]

    lhs_att = [lambda cols: att[:, cols]]
    send_partial(lhs_att, [full_o], 0, 0, 2)

    def residual(t, _):
        own = rows_at(t * MB, MB)
        res[own, :] = xown[own, :].astype(F32) + partial(lhs_att, [full_o], c * T + t * MB)
        return 0

    lax.fori_loop(0, T // MB, residual, 0)
    pump()
    take(exr.at[0], cr.at[2])

    def norm_second(t, _):
        own = rows_at(t * NB, NB)
        v = res[own, :] + exr[0, own, :].astype(F32)
        res[own, :] = v
        cen, inv = norm_parts(v)
        n2[rows_at(c * T + t * NB, NB), :] = (cen * inv * gain_two).astype(BF)
        return 0

    lax.fori_loop(0, T // NB, norm_second, 0)
    give_rows(n2, 3)
    pump()
    got_rows(n2, 3)
    take(dyf.at[mine, :], swr.at[1])
    give_rows(dyf, 1)

    HB = nz * M

    def hidden(t, _):
        i, ti = t // (S // TB), lax.rem(t, S // TB)
        cols = pl.ds(pl.multiple_of(ti * TB, TB), TB)
        rows = rows_at(i * HB, HB)
        normed = n2[cols, :]
        act = dg(W[rows_at(base("a0") + i * HB, HB), :], normed, 1, 1)
        gate = dg(W[rows_at(base("b0") + i * HB, HB), :], normed, 1, 1)
        cdf = 0.5 + 0.5 * lax.erf(act * 0.7071067811865476)
        gelu = act * cdf
        slope = cdf + act * (jnp.exp(-0.5 * act * act) * 0.3989422804014327)
        hid[rows, cols] = (gelu * gate).astype(BF)
        AB[0, rows, cols] = (slope * gate).astype(BF)
        AB[1, rows, cols] = gelu.astype(BF)
        return 0

    ds = [f"d{i}" for i in range(cuts) if f"d{i}" not in p.early]
    ab = [f"{m}{i}" for m in "ba" for i in range(cuts)]
    turn = ds + ab + ["o"] + [f"q{i}" for i in range(3 * p.heads)]
    at = [0, 0, 0, 0]

    def sum_next(start=1):
        one, two, ready_for_three, three = at
        for name in turn[one : one + start]:
            rs1(name)
        for name in turn[two:one]:
            rs2(name)
        for name in turn[three:ready_for_three]:
            rs3(name)
        at[:] = min(one + start, len(turn)), one, two, ready_for_three

    def grad_of(name, lhs, rhs):
        dest, at = place[name]
        dest[pl.ds(at, nz * p.pieces[name][1]), :] = dg(lhs, rhs[...], 1, 0).astype(BF)

    for i in range(cuts):
        ready(f"a{i}")
        ready(f"b{i}")
        if i == cuts - 1:
            pump()
        lax.fori_loop(i * (S // TB), (i + 1) * (S // TB), hidden, 0)
        if i == 0:
            got_rows(dyf, 1)
        grad_of(f"d{i}", hid[i * HB : (i + 1) * HB, :], dyf)
        if f"d{i}" in p.early:
            early1(f"d{i}")
        else:
            sum_next()
        pump()
    for _ in steps:
        raise ValueError("steps left")

    def back_hidden(t, _):
        i, ti = t // (S // TB), lax.rem(t, S // TB)
        cols = pl.ds(pl.multiple_of(ti * TB, TB), TB)
        rows = rows_at(i * HB, HB)
        g = dg(W[rows_at(base("d0") + i * HB, HB), :], dyf[cols, :], 1, 1)
        AB[0, rows, cols] = (g * AB[0, rows, cols].astype(F32)).astype(BF)
        AB[1, rows, cols] = (g * AB[1, rows, cols].astype(F32)).astype(BF)
        return 0

    for i in range(cuts):
        ready(f"d{i}")
        lax.fori_loop(i * (S // TB), (i + 1) * (S // TB), back_hidden, 0)
        grad_of(f"b{i}", AB[1, i * HB : (i + 1) * HB, :], n2)
        if i < 2:
            sum_next()

    lhs_hid = [lambda cols: hid[:, cols]]
    lhs_gp = [lambda cols: AB[0, :, cols], lambda cols: AB[1, :, cols]]
    take(exs.at[0], cs.at[2])
    send_partial(lhs_hid, [full_d], 0, 0, 4)
    send_partial(lhs_gp, [full_a, full_b], 1, 1, 5)
    sum_next()
    take(exr.at[0], cr.at[4])
    take(exs.at[0], cs.at[4])

    def output(t, _):
        own = rows_at(t * MB, MB)
        total = partial(lhs_hid, [full_d], c * T + t * MB)
        xs = res[own, :] + (total + exr[0, own, :].astype(F32))
        exs[0, own, :] = xs.astype(BF)
        return 0

    lax.fori_loop(0, T // MB, output, 0)
    swap(exs.at[0], out_hbm, out_hbm, 2)

    for i in range(cuts):
        sent(f"d{i}")
    for i in range(cuts):
        grad_of(f"a{i}", AB[0, i * HB : (i + 1) * HB, :], n2)
    sum_next()
    take(exr.at[1], cr.at[5])

    def grad_residual(t, carry):
        own = rows_at(t * MB, MB)
        total = partial(lhs_gp, [full_a, full_b], c * T + t * MB) + exr[1, own, :].astype(F32)
        v = res[own, :]
        cen, inv = norm_parts(v)
        hat = cen * inv
        carry = carry + jnp.sum(total * hat, axis=0, keepdims=True)
        dh = total * gain_two
        back = inv * (
            dh - jnp.mean(dh, axis=1, keepdims=True) - hat * jnp.mean(dh * hat, axis=1, keepdims=True)
        )
        g = dyf[rows_at(c * T + t * MB, MB), :].astype(F32) + back
        res[own, :] = g
        dyf[rows_at(c * T + t * MB, MB), :] = g.astype(BF)
        return carry

    take(dyf.at[mine, :], cs.at[1])
    gain_two_grad = lax.fori_loop(0, T // MB, grad_residual, jnp.zeros((1, D), F32))
    give_rows(dyf, 6)
    sum_next()
    for name in p.early[:1]:
        early2(name)
    got_rows(dyf, 6)

    sent("o")
    for i in range(cuts):
        sent(f"a{i}")
        sent(f"b{i}")

    gat = AB.at[0]

    def grad_att(t, _):
        rows = rows_at(t * U, U)
        gat[rows, :] = dg(W[rows_at(base("o") + t * U, U), :], dyf[...], 1, 1).astype(BF)
        return 0

    lax.fori_loop(0, nz, grad_att, 0)
    grad_of("o", att[...], dyf)
    sum_next()
    for name in p.early[:1]:
        early3(name)
    for name in p.early[1:]:
        early2(name)

    QC = 512

    def attend_back(t, _):
        q_rows, k_rows, v_rows, o_rows = head_rows(t)
        keyT = qkv[k_rows, :]
        key = keyT.T
        val = qkv[v_rows, :].T

        def block(b, carry):
            dk, dv = carry
            cols = pl.ds(pl.multiple_of(b * QC, QC), QC)
            q = qkv[q_rows, cols]
            g = gat[o_rows, cols]
            inner = jnp.sum(g.astype(F32) * att[o_rows, cols].astype(F32), axis=0, keepdims=True)
            prob = jnp.exp(dg(key, q, 1, 0) - lse[t, :, cols])
            dprob = dg(val, g, 1, 0)
            ds = (prob * (dprob - inner)).astype(BF)
            dv = dv + dg(g, prob.astype(BF), 1, 1)
            dk = dk + dg(q, ds, 1, 1)
            dq = dg(keyT, ds, 1, 0) * HD**-0.5
            co, si = cos_ref[:, cols], sin_ref[:, cols]
            g1, g2 = dq[: HD // 2], dq[HD // 2 :]
            qkv[q_rows, cols] = jnp.concatenate([g1 * co + g2 * si, g2 * co - g1 * si], axis=0).astype(BF)
            return dk, dv

        zero = jnp.zeros((HD, S), F32)
        dk, dv = lax.fori_loop(0, S // QC, block, (zero, zero))
        g1, g2 = dk[: HD // 2], dk[HD // 2 :]
        co, si = cos_ref[...], sin_ref[...]
        qkv[k_rows, :] = jnp.concatenate([g1 * co + g2 * si, g2 * co - g1 * si], axis=0).astype(BF)
        qkv[v_rows, :] = dv.astype(BF)
        return 0

    for t in range(0, NH, 2):
        lax.fori_loop(t, t + 2, attend_back, 0)
        if t == 0:
            sum_next()
        elif (t + 2) % nz == 0:
            first = (t // nz) * 3
            for i in range(first, first + 3):
                grad_of(f"q{i}", qkv[i * nz * HD : (i + 1) * nz * HD, :], n1)
            sum_next(3)
        else:
            sum_next(0)
        if t == 0:
            for name in p.early[:1]:
                early4(name)
            for name in p.early[1:]:
                early3(name)
        if t == 2:
            for name in p.early[1:]:
                early4(name)

    lhs_proj = [lambda cols: qkv[:, cols]]
    take(exs.at[1], cs.at[5])
    send_partial(lhs_proj, [full_q], 1, 0, 7)
    _, two, _, three = at
    for name in turn[three:two]:
        rs3(name)
    last = turn[two:]
    swap_sent(exs.at[0], 2)
    take(out_hbm, swr.at[2])
    take(exr.at[0], cr.at[7])
    rs2(last[0])

    def grad_input(t, carry):
        own = rows_at(t * MB, MB)
        total = partial(lhs_proj, [full_q], c * T + t * MB) + exr[0, own, :].astype(F32)
        cen, inv = norm_parts(xown[own, :].astype(F32))
        hat = cen * inv
        carry = carry + jnp.sum(total * hat, axis=0, keepdims=True)
        dh = total * gain_one
        back = inv * (
            dh - jnp.mean(dh, axis=1, keepdims=True) - hat * jnp.mean(dh * hat, axis=1, keepdims=True)
        )
        exs[0, own, :] = (res[own, :] + back).astype(BF)
        return carry

    gain_one_grad = lax.fori_loop(0, T // MB, grad_input, jnp.zeros((1, D), F32))
    swap(exs.at[0], gtok_hbm, gtok_hbm, 3)
    line = lax.broadcasted_iota(jnp.int32, (16, D), 0)
    both = jnp.where(line == 0, gain_one_grad, jnp.where(line == 1, gain_two_grad, 0.0)).astype(BF)
    for j in range(nz):
        Gn[16 * j : 16 * j + 16, :] = both
    rs1("n")
    for name in last[1:]:
        rs2(name)
    rs3(last[0])
    rs2("n")
    for name in last[1:] + ["n"]:
        rs3(name)
    for name in p.early:
        early5(name)
    for name in turn + ["n"]:
        rs4(name)
    for part in range(3):
        for k in range(2):
            firsts = [p.pieces[f"q{3 * j + part}"][0] for j in range(p.heads)]
            g_q[part, :, k * U : (k + 1) * U] = jnp.concatenate(
                [stage[k, at : at + HD, :] for at in firsts], axis=0
            ).T
    store(f"q{3 * p.heads - 1}")

    sent("n")
    for i in range(3 * p.heads):
        sent(f"q{i}")
    for name in p.order:
        rs_sent(name)
    swap_sent(x_hbm, 0)
    swap_sent(dy_hbm, 1)
    swap_sent(exs.at[0], 3)
    take(gtok_hbm, swr.at[3])
    take(n1.at[mine, :], cs.at[0])
    take(n2.at[mine, :], cs.at[3])
    take(dyf.at[mine, :], cs.at[6])
    take(exs.at[1], cs.at[7])
    for name in p.order:
        stored(name)


def layer(plan, x, dy, gain_a, gain_m, w_o, w_q, w_ab, w_d, rope):
    p = plan
    nz, D, T, U, H = p.nz, p.width, p.tokens, p.units, p.hid
    S, L = 2 * T, p.lane
    n = len(p.order)
    hbm = pl.BlockSpec(memory_space=pl.ANY)
    dma = pltpu.SemaphoreType.DMA
    scratch = [
        pltpu.VMEM((nz * p.rows, D), BF),
        pltpu.VMEM((T, D), BF),
        pltpu.VMEM((S, D), BF),
        pltpu.VMEM((S, D), BF),
        pltpu.VMEM((nz * 3 * U, S), BF),
        pltpu.VMEM((nz * U, S), BF),
        pltpu.VMEM((nz * p.heads, 1, S), F32),
        pltpu.VMEM((T, D), F32),
        pltpu.VMEM((S, D), BF),
        pltpu.VMEM((2, nz * H, S), BF),
        pltpu.VMEM((nz * H, S), BF),
        pltpu.VMEM((2, T, D), BF),
        pltpu.VMEM((2, T, D), BF),
        pltpu.VMEM((nz * 16, D), BF),
        pltpu.VMEM((nz * H, D), BF),
        pltpu.VMEM((nz * H, D), BF),
        pltpu.VMEM((2, 2, (nz // 2) * p.rows, p.block), BF),
        pltpu.VMEM((2, (nz // 2) * p.rows, p.block), BF),
        pltpu.VMEM((2 * nz, p.rows, p.lane), BF),
        pltpu.VMEM((nz - 1, max(len(p.early), 1) * p.sub, D), BF),
        pltpu.VMEM((2, HD // 2, S), F32),
        pltpu.VMEM((2, p.rows, L), F32),
        pltpu.VMEM((2, 1, L), BF),
        pltpu.VMEM((16, L), BF),
        pltpu.VMEM((3, L, 2 * U), BF),
        pltpu.VMEM((6 * U, L), BF),
        pltpu.VMEM((2, 2 * H, L), BF),
        pltpu.VMEM((2 * H, L), BF),
        pltpu.VMEM((3, L, 2 * U), F32),
        dma((n,)),
        dma((n,)),
        dma((n, 6)),
        dma((n,)),
        dma((n, 2, 2)),
        dma((n,)),
        dma((n, 2)),
        dma((n,)),
        dma((n,)),
        dma((n,)),
        dma((4,)),
        dma((4,)),
        dma((8,)),
        dma((8,)),
        dma((n, 2)),
        dma((n,)),
        dma((n,)),
        dma((n,)),
        dma((n,)),
        dma((7,)),
    ]
    return pl.pallas_call(
        functools.partial(kernel, p),
        out_shape=(
            jax.ShapeDtypeStruct((T, D), BF),
            jax.ShapeDtypeStruct((T, D), BF),
            jax.ShapeDtypeStruct((16, L), F32),
            jax.ShapeDtypeStruct((2 * U, L), F32),
            jax.ShapeDtypeStruct((3, L, 2 * U), F32),
            jax.ShapeDtypeStruct((2, p.real, L), F32),
            jax.ShapeDtypeStruct((p.real, L), F32),
        ),
        in_specs=[hbm] * 9,
        out_specs=(hbm,) * 7,
        scratch_shapes=scratch,
        compiler_params=pltpu.CompilerParams(
            collective_id=0, has_side_effects=True, vmem_limit_bytes=VMEM
        ),
        name="layer",
    )(x, dy, gain_a, gain_m, w_o, w_q, w_ab, w_d, rope)


def settle_kernel(count, *refs):
    ins, outs, held = refs[:count], refs[count : 2 * count + 1], refs[2 * count + 1 : 3 * count + 1]
    load_sem, store_sem = refs[3 * count + 1 :]
    loads = [pltpu.make_async_copy(a, b, load_sem.at[i]) for i, (a, b) in enumerate(zip(ins, held))]
    for copy in loads:
        copy.start()
    sources = [[h] for h in held]
    sources[2] = [held[2].at[pl.ds(0, 1), :], held[2].at[pl.ds(1, 1), :]]
    stores = []
    for copy, parts in zip(loads, sources):
        copy.wait()
        for part in parts:
            store = pltpu.make_async_copy(part, outs[len(stores)], store_sem.at[len(stores)])
            store.start()
            stores.append(store)
    for store in stores:
        store.wait()


def settle(out, gtok, g_n, *rest):
    arrays = (out, gtok, g_n) + rest
    row = jax.ShapeDtypeStruct((1, g_n.shape[1]), F32)
    like = [jax.ShapeDtypeStruct(a.shape, a.dtype) for a in arrays]
    shapes = (*like[:2], row, row, *like[3:])
    hbm = pl.BlockSpec(memory_space=pl.ANY)
    return pl.pallas_call(
        functools.partial(settle_kernel, len(arrays)),
        out_shape=shapes,
        in_specs=[hbm] * len(arrays),
        out_specs=(hbm,) * len(shapes),
        scratch_shapes=[pltpu.VMEM(a.shape, a.dtype) for a in arrays]
        + [pltpu.SemaphoreType.DMA((len(arrays),)), pltpu.SemaphoreType.DMA((len(shapes),))],
        compiler_params=pltpu.CompilerParams(vmem_limit_bytes=VMEM),
        name="settle",
    )(*arrays)


def rope_table():
    freq = THETA ** (-np.arange(HD // 2) * 2.0 / HD)
    angle = freq.astype(np.float32)[:, None] * np.arange(LEN, dtype=np.float32)[None, :]
    return np.stack([np.cos(angle), np.sin(angle)]).astype(np.float32)


def local(outer, nz, tokens, w_qkv, w_out, w_in, w_down, gain_attn, gain_mlp, grad_output):
    T, D = tokens.shape
    groups = [[hi * LOW + lo for hi in range(outer)] for lo in range(LOW)]
    piece = D // (outer * LOW)

    def widen(a, axis):
        if outer == 1:
            return a
        return lax.all_gather(a, "dp", axis=axis, tiled=True, axis_index_groups=groups)

    def narrow(a, axis):
        if outer == 1:
            return a
        return lax.psum_scatter(a, "dp", scatter_dimension=axis, tiled=True, axis_index_groups=groups)

    def turn(a, first, second):
        if outer == 1:
            return a
        return a.reshape(T, first, second, piece).swapaxes(1, 2).reshape(T, D)

    w_qkv, w_in = widen(w_qkv, 0), widen(w_in, 0)
    w_out, w_down = widen(w_out, 1), widen(w_down, 1)
    gains = [widen(g, 0) for g in (gain_attn, gain_mlp)]
    x = turn(tokens, outer, LOW)
    dy = turn(grad_output, outer, LOW)
    p = Plan(nz, D, T, w_qkv.shape[2], w_in.shape[2])
    L = p.lane
    rope = jnp.asarray(rope_table())
    results = layer(
        p,
        x,
        dy,
        gains[0].reshape(1, L),
        gains[1].reshape(1, L),
        w_out,
        w_qkv.transpose(1, 0, 2),
        w_in.transpose(1, 2, 0),
        w_down,
        rope,
    )
    out, gtok, g_a, g_m, g_out, g_q, g_ab, g_down = settle(*results)

    out, gtok = turn(out, LOW, outer), turn(gtok, LOW, outer)
    g_qkv = g_q.transpose(1, 0, 2)
    g_in = g_ab.transpose(2, 0, 1)
    return (
        out,
        gtok,
        narrow(g_qkv, 0),
        narrow(g_out, 1),
        narrow(g_in, 0),
        narrow(g_down, 1),
        narrow(g_a.reshape(L), 0),
        narrow(g_m.reshape(L), 0),
    )


def solution(mesh):
    rows = P(("dp", "tensor"), None)
    deep = P("dp", None, "tensor")
    wide = P("tensor", "dp")
    flat = P("dp")
    return jax.shard_map(
        functools.partial(local, mesh.shape["dp"] // LOW, mesh.shape["tensor"]),
        mesh=mesh,
        in_specs=(rows, deep, wide, deep, wide, flat, flat, rows),
        out_specs=(rows, rows, deep, wide, deep, wide, flat, flat),
        check_vma=False,
    )
```
